128 devices in a mesh: gx: 4 (over x), gy: 4 (over y), gz: 8 (over z, core).
Axes of the slice: x: 4, y: 4, z: 4, core: 2. Of those that a mesh axis runs over, the one named last changes fastest.
Arguments:
- latent: bfloat16 [4, 4, 8, 1024, 128], P('gx', 'gy', 'gz'), may hold values from -6 to 6
- destination: int32 [4, 4, 8, 1024, 1], P('gx', 'gy', 'gz'), may hold values from 0 to 127, as said below
- neighbours: int32 [4, 4, 8, 3456, 24], P('gx', 'gy', 'gz'), may hold values from 0 to 5247
- valid: int32 [4, 4, 8, 3456, 24], P('gx', 'gy', 'gz'), may hold values 0 or 1
- ghost_index: int32 [4, 4, 8, 8, 32], P('gx', 'gy', 'gz'), may hold values from 0 to 3455
- edge_first: bfloat16 [2, 256, 128], replicated, may hold values from -0.375 to 0.375
- edge_second: bfloat16 [2, 128, 128], replicated, may hold values from -0.5 to 0.5
- edge_third: bfloat16 [2, 128, 128], replicated, may hold values from -0.25 to 0.25
- node_first: bfloat16 [2, 256, 128], replicated, may hold values from -0.375 to 0.375
- node_second: bfloat16 [2, 128, 128], replicated, may hold values from -0.5 to 0.5
- node_third: bfloat16 [2, 128, 128], replicated, may hold values from -0.5 to 0.5
Outputs:
- settled: bfloat16 [4, 4, 8, 3456, 128], P('gx', 'gy', 'gz')
The draws below stay inside these ranges and needn't reach their ends.
Inputs may be any that keep to these rules, and one draw needn't show every extreme that they name: Each particle's destination is its own bin or one of the bins beside it, diagonals included; at most 128 particles of one bin have one destination, and exactly 128 of every bin stay in it. `neighbours`: rows below 3456 are the bin's own slots, the others its ghosts.
All inputs are finite; a program needn't handle non-finite values. No bound on the sum of `valid` on one device may be relied on, other than what follows from the above.
Results may differ from the reference program's by a relative error of at most 0.011.
Values may be sent and summed in bfloat16 or wider, within the bound.
No kernel may reach another device: no remote copies, remote signals or barrier semaphores. Data moves between devices by JAX's collectives and lax.ppermute only.
A program may use at most 64 MiB of HBM per device.

```python
import jax
import jax.numpy as jnp
import numpy as np
from jax import lax

L = 128
P_SIZE = 1024
G = 32
K = 24
LAYERS = 2
BX = 4
BY = 4
BZ = 8
BINS = 128
CAP = 128
R = 3456
NODES = 5248


def draw_destination(key, part):
    key = jax.random.fold_in(key, 1)
    bins = BX * BY * BZ
    slots = 27 * CAP
    code = jnp.arange(slots, dtype=jnp.int32) // CAP
    bin_id = jnp.arange(bins, dtype=jnp.int32)
    first = bin_id // (BY * BZ)
    second = bin_id // BZ % BY
    third = bin_id % BZ
    target_first = first[:, None] + code[None, :] // 9 - 1
    target_second = second[:, None] + code[None, :] // 3 % 3 - 1
    target_third = third[:, None] + code[None, :] % 3 - 1
    inside = (target_first >= 0) & (target_first < BX) & (target_second >= 0) & (target_second < BY) & (target_third >= 0) & (target_third < BZ)
    score_key, shuffle_key = jax.random.split(key)
    score = jax.random.randint(score_key, (bins, slots), 0, 1 << 20, dtype=jnp.int32)
    score = jnp.where(code[None, :] == 13, -1, score)
    score = jnp.where(inside, score, 1 << 21)
    order = jnp.argsort(score, axis=1, stable=True)[:, :P_SIZE]
    chosen = code[order]
    shuffle = jnp.argsort(jax.random.randint(shuffle_key, (bins, P_SIZE), 0, 1 << 20, dtype=jnp.int32), axis=1, stable=True)
    chosen = jnp.take_along_axis(chosen, shuffle, axis=1)
    target = ((first[:, None] + chosen // 9 - 1) * BY + (second[:, None] + chosen // 3 % 3 - 1)) * BZ + third[:, None] + chosen % 3 - 1
    return target.reshape(BX, BY, BZ, P_SIZE, 1).astype(jnp.int32)


def place_ends(values, stream_key, least, largest):
    index_at = [jax.random.randint(jax.random.fold_in(stream_key, axis), (), 0, length) for axis, length in enumerate(values.shape)]
    main_axis = values.shape.index(max(values.shape))
    beside = index_at[:main_axis] + [(index_at[main_axis] + 1) % values.shape[main_axis]] + index_at[main_axis + 1:]
    return values.at[tuple(index_at)].set(least).at[tuple(beside)].set(largest)


def levels(rng, shape, shards, least, top_value):
    def one(dim, shards_of):
        heights = jax.random.uniform(jax.random.fold_in(jax.random.fold_in(rng, 6), dim), (shards_of,), jnp.float32, least / len(shards), top_value / len(shards))
        return jnp.repeat(jnp.exp(heights), shape[dim] // shards_of).reshape((-1,) + (1,) * (len(shape) - dim - 1))

    factor_of = one(*shards[0])
    for cut in shards[1:]:
        factor_of = factor_of * one(*cut)
    return factor_of


def normal_values(key, dims, scale, limit, cuts=(), kind=jnp.bfloat16):
    gain = levels(key, dims, cuts, -0.22, 0.18) if cuts else 1.0
    values = jax.random.normal(key, dims, jnp.float32) * scale * gain
    return jnp.minimum(jnp.maximum(values, -limit), limit).astype(kind)


def setup_inputs(seed: int = 0) -> dict:
    keys = jax.random.split(jax.random.key(seed), 12)
    return {
        "latent": normal_values(keys[0], (BX, BY, BZ, P_SIZE, L), 1.0, 6.0, ((0, 4), (1, 4), (2, 8))),
        "destination": draw_destination(jax.random.fold_in(keys[11], 71), 0),
        "neighbours": place_ends(jax.random.randint(keys[2], (BX, BY, BZ, R, K), 0, NODES), jax.random.fold_in(keys[2], 1), 0, NODES - 1).astype(jnp.int32),
        "valid": place_ends((jax.random.randint(keys[3], (BX, BY, BZ, R, K), 0, 8) < 7).astype(jnp.int32), jax.random.fold_in(keys[3], 1), 0, 1),
        "ghost_index": place_ends(jax.random.randint(keys[4], (BX, BY, BZ, 8, G), 0, R), jax.random.fold_in(keys[4], 1), 0, R - 1).astype(jnp.int32),
        "edge_first": normal_values(keys[5], (LAYERS, 2 * L, L), (2 * L) ** -0.5, 0.375),
        "edge_second": normal_values(keys[6], (LAYERS, L, L), L ** -0.5, 0.5),
        "edge_third": normal_values(keys[7], (LAYERS, L, L), (L * 4) ** -0.5, 0.25),
        "node_first": normal_values(keys[8], (LAYERS, 2 * L, L), (2 * L) ** -0.5, 0.375),
        "node_second": normal_values(keys[9], (LAYERS, L, L), L ** -0.5, 0.5),
        "node_third": normal_values(keys[10], (LAYERS, L, L), L ** -0.5, 0.5),
    }


outer_slabs = np.array([p for p in range(64) if p // 16 in (0, 3) or p // 4 % 4 in (0, 3) or p % 4 in (0, 3)], dtype=np.int32)
code_first = np.array([c // 9 for c in range(27)], dtype=np.int32)
code_second = np.array([c // 3 % 3 for c in range(27)], dtype=np.int32)
code_third = np.array([c % 3 for c in range(27)], dtype=np.int32)

def layer_norm(values):
    mean = lax.optimization_barrier(jnp.mean(values, axis=1, keepdims=True))
    centred = values - mean
    var = lax.optimization_barrier(jnp.mean(centred * centred, axis=1, keepdims=True))
    return centred / jnp.sqrt(var + 1e-05)

def message_pass(state, ghosts, nbr_rows, valid_rows, live_rows, weights):
    efirst, esecond, ethird, nfirst, nsecond, nthird = weights
    width = state.shape[1]
    rows = state.shape[0]
    degree = nbr_rows.shape[1]
    table = jnp.concatenate([state, ghosts], axis=0)
    send_part = jnp.dot(table, efirst[width:], preferred_element_type=jnp.float32)
    recv_part = jnp.dot(state, efirst[:width], preferred_element_type=jnp.float32)
    blocks = 27

    def edge_block(pieces):
        recv, nbr, mask = pieces
        hidden = jnp.maximum(recv[:, None, :] + jnp.take(send_part, nbr, axis=0), 0.0)
        hidden = hidden.astype(jnp.bfloat16).reshape(-1, width)
        hidden = jnp.maximum(jnp.dot(hidden, esecond, preferred_element_type=jnp.float32), 0.0).astype(jnp.bfloat16)
        message = jnp.dot(hidden, ethird, preferred_element_type=jnp.float32).reshape(-1, degree, width)
        return lax.optimization_barrier(jnp.sum(message * mask[:, :, None], axis=1))
    aggregate = lax.map(edge_block, (recv_part.reshape(blocks, -1, width), nbr_rows.reshape(blocks, -1, degree), valid_rows.astype(jnp.float32).reshape(blocks, -1, degree)))
    aggregate = aggregate.reshape(rows, width).astype(jnp.bfloat16)
    hidden = jnp.dot(state, nfirst[:width], preferred_element_type=jnp.float32) + jnp.dot(aggregate, nfirst[width:], preferred_element_type=jnp.float32)
    hidden = jnp.maximum(hidden, 0.0).astype(jnp.bfloat16)
    hidden = jnp.maximum(jnp.dot(hidden, nsecond, preferred_element_type=jnp.float32), 0.0).astype(jnp.bfloat16)
    update = jnp.dot(hidden, nthird, preferred_element_type=jnp.float32)
    return (live_rows[:, None] * (state.astype(jnp.float32) + layer_norm(update))).astype(jnp.bfloat16)

def reference(latent, destination, neighbours, valid, ghost_index, edge_first, edge_second, edge_third, node_first, node_second, node_third):
    flat_latent = latent.reshape(BINS, P_SIZE, L)
    flat_dest = destination.reshape(BINS, P_SIZE)
    bin_ids = jnp.arange(BINS, dtype=jnp.int32)

    def pack(pieces):
        rows, dest, bin_id = pieces
        first = bin_id // (BY * BZ)
        second = bin_id // BZ % BY
        third = bin_id % BZ
        code = (dest // (BY * BZ) - first + 1) * 9 + (dest // BZ % BY - second + 1) * 3 + (dest % BZ - third + 1)
        code = code.astype(jnp.int32)
        onehot = (code[:, None] == jnp.arange(27, dtype=jnp.int32)[None, :]).astype(jnp.int32)
        before = jnp.cumsum(onehot, axis=0) - onehot
        rank = lax.optimization_barrier(jnp.sum(before * onehot, axis=1)).astype(jnp.int32)
        counts = lax.optimization_barrier(jnp.sum(onehot, axis=0)).astype(jnp.int32)
        buffer = jnp.zeros((27, CAP, L), jnp.bfloat16).at[code, rank].set(rows)
        return (buffer, counts)
    buffers, counts = lax.map(pack, (flat_latent, flat_dest, bin_ids))
    grid_buffers = jnp.pad(buffers.reshape(BX, BY, BZ, 3, 3, 3, CAP, L), ((1, 1), (1, 1), (1, 1), (0, 0), (0, 0), (0, 0), (0, 0), (0, 0)))
    grid_counts = jnp.pad(counts.reshape(BX, BY, BZ, 3, 3, 3), ((1, 1), (1, 1), (1, 1), (0, 0), (0, 0), (0, 0)))

    def receive(bin_id):
        first = (bin_id // (BY * BZ)).astype(jnp.int32)
        second = (bin_id // BZ % BY).astype(jnp.int32)
        third = (bin_id % BZ).astype(jnp.int32)
        zero = (bin_id * 0).astype(jnp.int32)
        window = lax.dynamic_slice(grid_buffers, (first, second, third, zero, zero, zero, zero, zero), (3, 3, 3, 3, 3, 3, CAP, L))
        got = lax.dynamic_slice(grid_counts, (first, second, third, zero, zero, zero), (3, 3, 3, 3, 3, 3))
        rows = window[code_first, code_second, code_third, 2 - code_first, 2 - code_second, 2 - code_third]
        sent = got[code_first, code_second, code_third, 2 - code_first, 2 - code_second, 2 - code_third]
        live_rows = (jnp.arange(CAP, dtype=jnp.int32)[None, :] < sent[:, None]).astype(jnp.float32)
        return (rows.reshape(R, L), live_rows.reshape(R))
    state, live = lax.map(receive, bin_ids)
    nbr = neighbours.reshape(BINS, R, K)
    val = valid.reshape(BINS, R, K)
    gidx = ghost_index.reshape(BINS, 8 * G)
    for layer in range(LAYERS):
        weights = (edge_first[layer], edge_second[layer], edge_third[layer], node_first[layer], node_second[layer], node_third[layer])
        slabs = jax.vmap(lambda rows, index: jnp.take(rows, index, axis=0))(state, gidx)
        slabs = slabs.reshape(BX, BY, BZ, 2, 2, 2, G, L)
        whole = jnp.transpose(slabs, (0, 3, 1, 4, 2, 5, 6, 7)).reshape(2 * BX, 2 * BY, 2 * BZ, G, L)
        padded = jnp.pad(whole, ((1, 1), (1, 1), (1, 1), (0, 0), (0, 0)))

        def one_bin(device, padded=padded, weights=weights, state=state):
            first = (device // (BY * BZ)).astype(jnp.int32)
            second = (device // BZ % BY).astype(jnp.int32)
            third = (device % BZ).astype(jnp.int32)
            zero = (device * 0).astype(jnp.int32)
            window = lax.dynamic_slice(padded, (2 * first, 2 * second, 2 * third, zero, zero), (4, 4, 4, G, L))
            ghosts = window.reshape(64, G, L)[outer_slabs].reshape(56 * G, L)
            return message_pass(state[device], ghosts, nbr[device], val[device], live[device], weights)
        state = lax.map(one_bin, bin_ids)
    return state.reshape(BX, BY, BZ, R, L)
```

```python
import jax
import jax.numpy as jnp
import numpy as np
from jax import lax
from jax.experimental import pallas as pl
from jax.experimental.pallas import tpu as pltpu
from jax.sharding import PartitionSpec as P

F32 = jnp.float32
BF16 = jnp.bfloat16
I32 = jnp.int32
W = 128
CODES = 27
ROWS = CODES * W
DEG = 24
SLAB = 32
OUTER = [
    p for p in range(64) if p // 16 in (0, 3) or p // 4 % 4 in (0, 3) or p % 4 in (0, 3)
]
GHOSTS = len(OUTER) * SLAB
NODES = ROWS + GHOSTS
DUMMY = NODES
MARK = 2.0**100
CH = 4
HALO_AXES = ("gx", "gy", "gz")
VMEM_LIMIT = 56 * 2**20


def dot(a, b):
    return jnp.dot(a, b, preferred_element_type=F32)


def vmem():
    return pl.BlockSpec(memory_space=pltpu.VMEM)


def smem():
    return pl.BlockSpec(memory_space=pltpu.SMEM)


def iota(shape, dim):
    return lax.broadcasted_iota(I32, shape, dim)


def pack_kernel(dest_ref, rows_ref, out_ref, slot_ref):
    n_y, n_z = 4, 8
    ix, iy, iz = (lax.axis_index(a) for a in HALO_AXES)
    tri = (iota((W, W), 0) < iota((W, W), 1)).astype(BF16)
    ones = jnp.ones((W, W), BF16)
    off = jnp.zeros((32, W), F32)
    for j in range(8):
        d = dest_ref[:, j * W : (j + 1) * W]
        code = (
            (lax.shift_right_logical(d, 5) - ix + 1) * 9
            + ((lax.shift_right_logical(d, 3) & (n_y - 1)) - iy + 1) * 3
            + ((d & (n_z - 1)) - iz + 1)
        )
        hit = iota((32, W), 0) == code
        one = jnp.where(hit, 1.0, 0.0).astype(BF16)
        before = dot(one, tri) + off
        rank = jnp.sum(jnp.where(hit, before, 0.0), axis=0, keepdims=True)
        slot_ref[:, j * W : (j + 1) * W] = code * W + rank.astype(I32)
        off = off + dot(one, ones)
    slot = slot_ref[...]
    rows = rows_ref[...]
    for c in range(CODES):
        chosen = jnp.where(slot == iota((W, 1024), 0) + c * W, 1.0, 0.0).astype(BF16)
        got = dot(chosen, rows)
        alive = iota((W, W), 0).astype(F32) < off[c : c + 1, :]
        out_ref[c] = jnp.where(alive, got, MARK).astype(BF16)


def pack(dest, rows):
    return pl.pallas_call(
        pack_kernel,
        out_shape=jax.ShapeDtypeStruct((CODES, W, W), BF16),
        in_specs=[vmem(), vmem()],
        out_specs=vmem(),
        scratch_shapes=[pltpu.VMEM((1, 1024), I32)],
        compiler_params=pltpu.CompilerParams(vmem_limit_bytes=VMEM_LIMIT),
        name="pack",
    )(dest, rows)


def receive_kernel(gidx_ref, raw_ref, state_ref, cnt_ref, slab_ref, full, picked):
    sizes = (4, 4, 8)
    pos = [lax.axis_index(a) for a in HALO_AXES]
    cnt_ref[...] = jnp.zeros_like(cnt_ref)
    for c in range(CODES):
        offs = (c // 9 - 1, c // 3 % 3 - 1, c % 3 - 1)
        inside = jnp.int32(1)
        for p, o, s in zip(pos, offs, sizes):
            if o < 0:
                inside = inside * (p > 0).astype(I32)
            if o > 0:
                inside = inside * (p < s - 1).astype(I32)
        x = raw_ref[c].astype(F32)
        alive = x < MARK * 0.5
        count = jnp.sum(jnp.where(alive, 1.0, 0.0), axis=0, keepdims=True).astype(I32)
        cnt_ref[c : c + 1, :] = count * inside
        clean = jnp.where(alive, x, 0.0)
        full[c * W : (c + 1) * W, :] = clean
        state_ref[c * W : (c + 1) * W, :] = clean.astype(BF16)
    pick_slabs(gidx_ref, full, picked)
    slab_ref[...] = picked[...].astype(BF16)


def pick_slabs(gidx_ref, full, picked):
    def some(b, carry):
        for r in range(16):
            picked[pl.ds(b * 16 + r, 1), :] = full[pl.ds(gidx_ref[b * 16 + r], 1), :]
        return carry

    lax.fori_loop(0, 16, some, 0)


def receive(gidx, raw):
    return pl.pallas_call(
        receive_kernel,
        out_shape=[
            jax.ShapeDtypeStruct((ROWS, W), BF16),
            jax.ShapeDtypeStruct((32, W), I32),
            jax.ShapeDtypeStruct((8 * SLAB, W), BF16),
        ],
        in_specs=[smem(), vmem()],
        out_specs=[vmem()] * 3,
        scratch_shapes=[pltpu.VMEM((ROWS, W), F32), pltpu.VMEM((8 * SLAB, W), F32)],
        compiler_params=pltpu.CompilerParams(vmem_limit_bytes=VMEM_LIMIT),
        name="receive",
    )(gidx, raw)


def index_kernel(nbr_ref, valid_ref, idx_ref, steps_ref):
    steps_ref[...] = jnp.zeros_like(steps_ref) + DEG
    for c in range(CODES):
        cols = slice(c * W, (c + 1) * W)
        idx_ref[c * DEG : (c + 1) * DEG, :] = jnp.where(
            valid_ref[:, cols] > 0, nbr_ref[:, cols], DUMMY
        )


def indices(nbr, valid):
    return pl.pallas_call(
        index_kernel,
        out_shape=[
            jax.ShapeDtypeStruct((CODES * DEG, W), I32),
            jax.ShapeDtypeStruct((32, W), I32),
        ],
        in_specs=[vmem()] * 2,
        out_specs=[vmem()] * 2,
        compiler_params=pltpu.CompilerParams(vmem_limit_bytes=VMEM_LIMIT),
        name="indices",
    )(nbr, valid)


def layer_kernel(
    idx_ref,
    steps_ref,
    cnt_ref,
    gidx_ref,
    state_ref,
    mid_ref,
    low_ref,
    high_ref,
    efirst_ref,
    esecond_ref,
    ethird_ref,
    nfirst_ref,
    nsecond_ref,
    nthird_ref,
    out_ref,
    slab_ref,
    table,
    recv,
    ghosts,
    hidden,
    deep,
    agg,
    full,
    picked,
    where_ref,
):
    w_recv = efirst_ref[0:W, :]
    w_send = efirst_ref[W : 2 * W, :]
    w_both = jnp.concatenate([w_recv, w_send], axis=1)

    for s, p in enumerate(OUTER):
        a, b, c = p // 16, p // 4 % 4, p % 4
        if c == 0:
            slab = low_ref[a, b]
        elif c == 3:
            slab = high_ref[a, b]
        else:
            slab = mid_ref[a, b, c - 1]
        ghosts[s * SLAB : (s + 1) * SLAB, :] = slab

    def own(i, carry):
        rows = pl.ds(i * 384, 384)
        both = dot(state_ref[rows, :], w_both)
        recv[rows, :] = both[:, :W]
        table[rows, :] = both[:, W:]
        return carry

    lax.fori_loop(0, ROWS // 384, own, 0)

    def far(i, carry):
        table[pl.ds(ROWS + i * 256, 256), :] = dot(ghosts[pl.ds(i * 256, 256), :], w_send)
        return carry

    lax.fori_loop(0, GHOSTS // 256, far, 0)
    table[NODES : NODES + 8, :] = jnp.full((8, W), -MARK, F32)

    w_second = esecond_ref[...]
    sub = iota((8, W), 0)

    def sender(c, carry):
        groups = lax.shift_right_logical(cnt_ref[c, 0] + 7, 3)

        def gather(g, chunk):
            q0 = pl.multiple_of(g * 8, 8)
            base = c * (DEG * W) + q0
            mine = recv[pl.ds(pl.multiple_of(c * W + q0, 8), 8), :]
            count = lax.shift_right_logical(steps_ref[c, q0] + (CH - 1), 2)
            where_ref[g] = chunk
            where_ref[32 + g] = count

            def some(t, carry):
                first = base + t * (CH * W)
                for pair in range(CH // 2):
                    both = []
                    for k in (2 * pair, 2 * pair + 1):
                        got = None
                        for r in range(8):
                            at = idx_ref[first + (k * W + r)]
                            row = jnp.broadcast_to(table[pl.ds(at, 1), :], (8, W))
                            got = row if got is None else jnp.where(sub == r, row, got)
                        both.append(jnp.maximum(got + mine, 0.0))
                    dst = pl.multiple_of((chunk + t) * (CH * 8) + pair * 16, 16)
                    hidden[pl.ds(dst, 16), :] = jnp.concatenate(both, axis=0).astype(BF16)
                return carry

            lax.fori_loop(0, count, some, 0)
            return chunk + count

        chunks = lax.fori_loop(0, groups, gather, jnp.int32(0))

        def multiply(i, carry):
            h = hidden[pl.ds(pl.multiple_of(i * 256, 256), 256), :]
            d = jnp.maximum(dot(h, w_second), 0.0).astype(BF16).astype(F32)
            d = jnp.sum(d.reshape(8, CH, 8, W), axis=1)
            deep[pl.ds(pl.multiple_of(i * 64, 64), 64), :] = d.reshape(64, W)
            return carry

        lax.fori_loop(0, lax.shift_right_logical(chunks + 7, 3), multiply, 0)

        def collect(g, carry):
            first = where_ref[g]
            count = where_ref[32 + g]
            total = jnp.zeros((8, W), F32)
            for j in range(DEG // CH):
                piece = deep[pl.ds(pl.multiple_of((first + j) * 8, 8), 8), :]
                total = total + jnp.where(j < count, piece, 0.0)
            agg[pl.ds(pl.multiple_of(c * W + g * 8, 8), 8), :] = total
            return carry

        lax.fori_loop(0, groups, collect, 0)
        return carry

    lax.fori_loop(0, CODES, sender, 0)

    w_third = ethird_ref[...]
    n_state = nfirst_ref[0:W, :]
    n_agg = nfirst_ref[W : 2 * W, :]
    n_second = nsecond_ref[...]
    n_third = nthird_ref[...]

    def node(i, carry):
        rows = pl.ds(pl.multiple_of(i * 384, 384), 384)
        live = jnp.concatenate(
            [iota((W, W), 0) < cnt_ref[i * 3 + j, 0] for j in range(3)], axis=0
        )
        summed = jnp.where(live, agg[rows, :], 0.0)
        top = summed.astype(BF16)
        rest = (summed - top.astype(F32)).astype(BF16)
        total = (dot(top, w_third) + dot(rest, w_third)).astype(BF16)
        state = state_ref[rows, :]
        h = jnp.maximum(dot(state, n_state) + dot(total, n_agg), 0.0).astype(BF16)
        h = jnp.maximum(dot(h, n_second), 0.0).astype(BF16)
        update = dot(h, n_third)
        mean = jnp.mean(update, axis=1, keepdims=True)
        centred = update - mean
        var = jnp.mean(centred * centred, axis=1, keepdims=True)
        new = state.astype(F32) + centred * lax.rsqrt(var + 1e-05)
        new = jnp.where(live, new, 0.0)
        full[rows, :] = new
        out_ref[rows, :] = new.astype(BF16)
        return carry

    lax.fori_loop(0, ROWS // 384, node, 0)
    pick_slabs(gidx_ref, full, picked)
    slab_ref[...] = picked[...].astype(BF16)


def one_layer(idx, steps, cnt, gidx, state, mid, low, high, weights):
    return pl.pallas_call(
        layer_kernel,
        out_shape=[
            jax.ShapeDtypeStruct((ROWS, W), BF16),
            jax.ShapeDtypeStruct((8 * SLAB, W), BF16),
        ],
        in_specs=[smem()] * 4 + [vmem()] * 10,
        out_specs=[vmem()] * 2,
        scratch_shapes=[
            pltpu.VMEM((NODES + 8, W), F32),
            pltpu.VMEM((ROWS, W), F32),
            pltpu.VMEM((GHOSTS, W), BF16),
            pltpu.VMEM((3072 + 256, W), BF16),
            pltpu.VMEM((768 + 64, W), F32),
            pltpu.VMEM((ROWS, W), F32),
            pltpu.VMEM((ROWS, W), F32),
            pltpu.VMEM((8 * SLAB, W), F32),
            pltpu.SMEM((64,), I32),
        ],
        compiler_params=pltpu.CompilerParams(vmem_limit_bytes=VMEM_LIMIT),
        name="layer",
    )(idx, steps, cnt, gidx, state, mid, low, high, *weights)


def both_ways(up, down, axis):
    n = lax.axis_size(axis)
    forward = [(i, i + 1) for i in range(n - 1)]
    backward = [(b, a) for a, b in forward]
    return lax.ppermute(up, axis, forward), lax.ppermute(down, axis, backward)


def migrate(buffer):
    for dim, axis in enumerate(HALO_AXES):
        take = lambda i: lax.index_in_dim(buffer, i, dim, keepdims=True)
        low, high = both_ways(take(2), take(0), axis)
        buffer = jnp.concatenate([low, take(1), high], axis=dim)
    return buffer


def surround(slabs):
    block = slabs.reshape(2, 2, 2, SLAB, W)
    for dim, axis in enumerate(HALO_AXES[:2]):
        low, high = both_ways(
            lax.slice_in_dim(block, 1, 2, axis=dim), lax.slice_in_dim(block, 0, 1, axis=dim), axis
        )
        block = jnp.concatenate([low, block, high], axis=dim)
    low, high = both_ways(block[:, :, 1], block[:, :, 0], "gz")
    return block, low, high


def body(
    latent,
    destination,
    neighbours,
    valid,
    ghost_index,
    edge_first,
    edge_second,
    edge_third,
    node_first,
    node_second,
    node_third,
):
    dest = destination.reshape(1, 1024)
    nbr = neighbours[0, 0, 0].T
    mask = valid[0, 0, 0].T
    gidx = ghost_index.reshape(-1)
    buffer = pack(dest, latent[0, 0, 0])
    idx, steps = indices(nbr, mask)
    idx = idx.reshape(-1)
    moved = migrate(buffer.reshape(3, 3, 3, W, W))
    state, cnt, slabs = receive(gidx, moved.reshape(CODES, W, W))
    for layer in range(edge_first.shape[0]):
        weights = [
            w[layer]
            for w in (edge_first, edge_second, edge_third, node_first, node_second, node_third)
        ]
        mid, low, high = surround(slabs)
        state, slabs = one_layer(idx, steps, cnt, gidx, state, mid, low, high, weights)
    return state.reshape(1, 1, 1, ROWS, W)


def solution(mesh):
    spread = P("gx", "gy", "gz", None, None)
    return jax.shard_map(
        body,
        mesh=mesh,
        in_specs=(spread,) * 5 + (P(),) * 6,
        out_specs=spread,
        check_vma=False,
    )
```

```python
import jax
import jax.numpy as jnp
import numpy as np
from jax import lax
from jax.experimental import pallas as pl
from jax.experimental.pallas import tpu as pltpu
from jax.sharding import PartitionSpec as P

F32 = jnp.float32
BF16 = jnp.bfloat16
I32 = jnp.int32
W = 128
CODES = 27
ROWS = CODES * W
DEG = 24
SLAB = 32
OUTER = [
    p for p in range(64) if p // 16 in (0, 3) or p // 4 % 4 in (0, 3) or p % 4 in (0, 3)
]
GHOSTS = len(OUTER) * SLAB
NODES = ROWS + GHOSTS
DUMMY = NODES
MARK = 2.0**100
CH = 4
HALO_AXES = ("gx", "gy", "gz")
VMEM_LIMIT = 56 * 2**20


def dot(a, b):
    return jnp.dot(a, b, preferred_element_type=F32)


def vmem():
    return pl.BlockSpec(memory_space=pltpu.VMEM)


def smem():
    return pl.BlockSpec(memory_space=pltpu.SMEM)


def iota(shape, dim):
    return lax.broadcasted_iota(I32, shape, dim)


def pack_kernel(dest_ref, rows_ref, out_ref, slot_ref):
    n_y, n_z = 4, 8
    ix, iy, iz = (lax.axis_index(a) for a in HALO_AXES)
    tri = (iota((W, W), 0) < iota((W, W), 1)).astype(BF16)
    ones = jnp.ones((W, W), BF16)
    off = jnp.zeros((32, W), F32)
    for j in range(8):
        d = dest_ref[:, j * W : (j + 1) * W]
        code = (
            (lax.shift_right_logical(d, 5) - ix + 1) * 9
            + ((lax.shift_right_logical(d, 3) & (n_y - 1)) - iy + 1) * 3
            + ((d & (n_z - 1)) - iz + 1)
        )
        hit = iota((32, W), 0) == code
        one = jnp.where(hit, 1.0, 0.0).astype(BF16)
        before = dot(one, tri) + off
        rank = jnp.sum(jnp.where(hit, before, 0.0), axis=0, keepdims=True)
        slot_ref[:, j * W : (j + 1) * W] = code * W + rank.astype(I32)
        off = off + dot(one, ones)
    slot = slot_ref[...]
    rows = rows_ref[...]
    for c in range(CODES):
        chosen = jnp.where(slot == iota((W, 1024), 0) + c * W, 1.0, 0.0).astype(BF16)
        got = dot(chosen, rows)
        alive = iota((W, W), 0).astype(F32) < off[c : c + 1, :]
        out_ref[c] = jnp.where(alive, got, MARK).astype(BF16)


def pack(dest, rows):
    return pl.pallas_call(
        pack_kernel,
        out_shape=jax.ShapeDtypeStruct((CODES, W, W), BF16),
        in_specs=[vmem(), vmem()],
        out_specs=vmem(),
        scratch_shapes=[pltpu.VMEM((1, 1024), I32)],
        compiler_params=pltpu.CompilerParams(vmem_limit_bytes=VMEM_LIMIT),
        name="pack",
    )(dest, rows)


def receive_kernel(gidx_ref, raw_ref, state_ref, cnt_ref, slab_ref, full, picked):
    sizes = (4, 4, 8)
    pos = [lax.axis_index(a) for a in HALO_AXES]
    cnt_ref[...] = jnp.zeros_like(cnt_ref)
    for c in range(CODES):
        offs = (c // 9 - 1, c // 3 % 3 - 1, c % 3 - 1)
        inside = jnp.int32(1)
        for p, o, s in zip(pos, offs, sizes):
            if o < 0:
                inside = inside * (p > 0).astype(I32)
            if o > 0:
                inside = inside * (p < s - 1).astype(I32)
        x = raw_ref[c].astype(F32)
        alive = x < MARK * 0.5
        count = jnp.sum(jnp.where(alive, 1.0, 0.0), axis=0, keepdims=True).astype(I32)
        cnt_ref[c : c + 1, :] = count * inside
        present = iota((W, W), 0) < count * inside
        full[c * W : (c + 1) * W, :] = jnp.where(present, x, MARK)
        state_ref[c * W : (c + 1) * W, :] = jnp.where(present, x, 0.0).astype(BF16)
    pick_slabs(gidx_ref, full, picked)
    slab_ref[...] = picked[...].astype(BF16)


def pick_slabs(gidx_ref, full, picked):
    def some(b, carry):
        for r in range(16):
            picked[pl.ds(b * 16 + r, 1), :] = full[pl.ds(gidx_ref[b * 16 + r], 1), :]
        return carry

    lax.fori_loop(0, 16, some, 0)


def receive(gidx, raw):
    return pl.pallas_call(
        receive_kernel,
        out_shape=[
            jax.ShapeDtypeStruct((ROWS, W), BF16),
            jax.ShapeDtypeStruct((32, W), I32),
            jax.ShapeDtypeStruct((8 * SLAB, W), BF16),
        ],
        in_specs=[smem(), vmem()],
        out_specs=[vmem()] * 3,
        scratch_shapes=[pltpu.VMEM((ROWS, W), F32), pltpu.VMEM((8 * SLAB, W), F32)],
        compiler_params=pltpu.CompilerParams(vmem_limit_bytes=VMEM_LIMIT),
        name="receive",
    )(gidx, raw)


def sort_pairs(count):
    pairs = []
    size = 1
    while size < count:
        size *= 2
    p = 1
    while p < size:
        k = p
        while k >= 1:
            for j in range(k % p, size - k, 2 * k):
                for i in range(min(k, size - j - k)):
                    if (i + j) // (2 * p) == (i + j + k) // (2 * p) and i + j + k < count:
                        pairs.append((i + j, i + j + k))
            k //= 2
        p *= 2
    return pairs


def fill_ghosts(mid_ref, low_ref, high_ref, ghosts):
    for s, p in enumerate(OUTER):
        a, b, c = p // 16, p // 4 % 4, p % 4
        if c == 0:
            slab = low_ref[a, b]
        elif c == 3:
            slab = high_ref[a, b]
        else:
            slab = mid_ref[a, b, c - 1]
        ghosts[s * SLAB : (s + 1) * SLAB, :] = slab


def index_kernel(
    nbr_ref, valid_ref, cnt_ref, mid_ref, low_ref, high_ref, idx_ref, steps_ref, dead_ref, ghosts, held
):
    fill_ghosts(mid_ref, low_ref, high_ref, ghosts)
    alive = jnp.where(ghosts[...].astype(F32) < MARK * 0.5, 1.0, 0.0).astype(BF16)
    at = iota((W, GHOSTS), 1)
    bit = jnp.left_shift(1, at & 15).astype(F32)
    spread = jnp.where(lax.shift_right_logical(at, 4) == iota((W, GHOSTS), 0), bit, 0.0)
    words = dot(spread.astype(BF16), alive)
    eye = iota((W, W), 0) == iota((W, W), 1)
    words = jnp.sum(jnp.where(eye, words, 0.0), axis=0, keepdims=True).astype(I32)
    words = jnp.broadcast_to(words, (8, W))
    counts = cnt_ref[...]
    diag = iota((32, W), 0) == iota((32, W), 1)
    by_code = jnp.sum(jnp.where(diag, counts.astype(F32), 0.0), axis=0, keepdims=True)
    by_code = jnp.broadcast_to(by_code.astype(I32), (8, W))

    held[...] = jnp.zeros_like(held) - 1
    for c in range(CODES):
        cols = slice(c * W, (c + 1) * W)
        held[c * DEG : (c + 1) * DEG, :] = jnp.where(valid_ref[:, cols] > 0, nbr_ref[:, cols], -1)

    for b in range(4):
        here = iota((8, W), 1) < counts[b * 8 : (b + 1) * 8, :]
        keys = []
        dead = jnp.zeros((8, W), F32)
        for k in range(DEG):
            node = held[pl.ds(b * 8 * DEG + k, 8, stride=DEG), :]
            far = jnp.maximum(node - ROWS, 0)
            word = jnp.take_along_axis(words, lax.shift_right_logical(far, 4), axis=1)
            flag = lax.shift_right_logical(word, far & 15) & 1
            near = jnp.minimum(jnp.maximum(node, 0), ROWS - 1)
            limit = jnp.take_along_axis(by_code, lax.shift_right_logical(near, 7), axis=1)
            lives = jnp.where(node >= ROWS, flag, jnp.where((near & (W - 1)) < limit, 1, 0))
            real = node >= 0
            key = jnp.where(here & real & (lives > 0), node, DUMMY)
            dead = dead + jnp.where(here & real & (lives == 0), 1.0, 0.0)
            keys.append(key.astype(F32))
        for i, j in sort_pairs(DEG):
            keys[i], keys[j] = jnp.minimum(keys[i], keys[j]), jnp.maximum(keys[i], keys[j])
        used = jnp.zeros((8, W), F32)
        for k in range(DEG):
            used = used + jnp.where(keys[k] < DUMMY, 1.0, 0.0)
            idx_ref[k * 32 + b * 8 : k * 32 + (b + 1) * 8, :] = keys[k].astype(I32)
        for shift in (1, 2, 4, 8):
            used = jnp.maximum(used, pltpu.roll(used, W - shift, 1))
        steps_ref[b * 8 : (b + 1) * 8, :] = used.astype(I32)
        dead_ref[b * 8 : (b + 1) * 8, :] = dead


def indices(nbr, valid, cnt, mid, low, high):
    return pl.pallas_call(
        index_kernel,
        out_shape=[
            jax.ShapeDtypeStruct((DEG * 32, W), I32),
            jax.ShapeDtypeStruct((32, W), I32),
            jax.ShapeDtypeStruct((32, W), F32),
        ],
        in_specs=[vmem()] * 6,
        out_specs=[vmem()] * 3,
        scratch_shapes=[pltpu.VMEM((GHOSTS, W), BF16), pltpu.VMEM((32 * DEG, W), I32)],
        compiler_params=pltpu.CompilerParams(vmem_limit_bytes=VMEM_LIMIT),
        name="indices",
    )(nbr, valid, cnt, mid, low, high)


GROUP = 16
FIRST = 8
TAILS = (0, 2, 4, 6, 8, 10, 12, 16)
DUMP = ROWS


def layer_kernel(
    idx_ref,
    steps_ref,
    cnt_ref,
    gidx_ref,
    dead_ref,
    state_ref,
    mid_ref,
    low_ref,
    high_ref,
    efirst_ref,
    esecond_ref,
    ethird_ref,
    nfirst_ref,
    nsecond_ref,
    nthird_ref,
    out_ref,
    slab_ref,
    table,
    recv,
    ghosts,
    hidden,
    agg,
    full,
    picked,
):
    w_recv = efirst_ref[0:W, :]
    w_send = efirst_ref[W : 2 * W, :]
    w_both = jnp.concatenate([w_recv, w_send], axis=1)
    fill_ghosts(mid_ref, low_ref, high_ref, ghosts)

    def own(i, carry):
        rows = pl.ds(pl.multiple_of(i * 384, 384), 384)
        both = dot(state_ref[rows, :], w_both)
        recv[rows, :] = both[:, :W]
        table[rows, :] = both[:, W:]
        return carry

    lax.fori_loop(0, ROWS // 384, own, 0)

    def far(i, carry):
        x = ghosts[pl.ds(pl.multiple_of(i * 256, 256), 256), :].astype(F32)
        x = jnp.where(x < MARK * 0.5, x, 0.0).astype(BF16)
        table[pl.ds(pl.multiple_of(ROWS + i * 256, 128), 256), :] = dot(x, w_send)
        return carry

    lax.fori_loop(0, GHOSTS // 256, far, 0)
    table[NODES : NODES + 8, :] = jnp.full((8, W), -MARK, F32)

    w_second = esecond_ref[...]
    sub = iota((8, W), 0)

    def finish(h, row):
        d = jnp.maximum(dot(h, w_second), 0.0)
        agg[pl.ds(pl.multiple_of(row, GROUP), GROUP), :] = jnp.sum(
            d.reshape(DEG, GROUP, W), axis=0
        )

    def step(base, mine, k):
        both = []
        for half in range(2):
            got = None
            for r in range(8):
                at = idx_ref[base + (k * (32 * W) + half * 8 + r)]
                row = jnp.broadcast_to(table[pl.ds(at, 1), :], (8, W))
                got = row if got is None else jnp.where(sub == r, row, got)
            both.append(jnp.maximum(got + mine[half], 0.0))
        hidden[k * GROUP : (k + 1) * GROUP, :] = jnp.concatenate(both, axis=0).astype(BF16)

    def sender(c, last):
        groups = lax.shift_right_logical(cnt_ref[c, 0] + (GROUP - 1), 4)

        def gather(g, last):
            q0 = pl.multiple_of(g * GROUP, GROUP)
            base = c * W + q0
            mine = [recv[pl.ds(pl.multiple_of(base + h * 8, 8), 8), :] for h in range(2)]
            finish(hidden[...], last)
            for k in range(FIRST):
                step(base, mine, k)
            more = steps_ref[c, q0] - FIRST
            which = sum((more > t).astype(I32) for t in TAILS[:-1])

            def tail(size):
                def run():
                    for k in range(FIRST, FIRST + size):
                        step(base, mine, k)
                    if FIRST + size < DEG:
                        hidden[(FIRST + size) * GROUP :, :] = jnp.zeros(
                            ((DEG - FIRST - size) * GROUP, W), BF16
                        )

                return run

            lax.switch(which, [tail(t) for t in TAILS])
            return base

        return lax.fori_loop(0, groups, gather, last)

    last = lax.fori_loop(0, CODES, sender, jnp.int32(DUMP))
    finish(hidden[...], last)

    w_third = ethird_ref[...]
    n_state = nfirst_ref[0:W, :]
    n_agg = nfirst_ref[W : 2 * W, :]
    n_second = nsecond_ref[...]
    n_third = nthird_ref[...]
    eye = iota((W, W), 0) == iota((W, W), 1)
    ones = jnp.ones((W, W), BF16)

    def node(i, carry):
        rows = pl.ds(pl.multiple_of(i * 384, 384), 384)
        live = jnp.concatenate(
            [iota((W, W), 0) < cnt_ref[i * 3 + j, 0] for j in range(3)], axis=0
        )
        times = jnp.concatenate(
            [
                jnp.where(eye, jnp.broadcast_to(dead_ref[pl.ds(i * 3 + j, 1), :], (W, W)), 0.0)
                for j in range(3)
            ],
            axis=0,
        )
        times = dot(times.astype(BF16), ones)
        alone = jnp.maximum(recv[rows, :], 0.0).astype(BF16)
        alone = jnp.maximum(dot(alone, w_second), 0.0)
        summed = jnp.where(live, agg[rows, :] + times * alone, 0.0)
        top = summed.astype(BF16)
        rest = (summed - top.astype(F32)).astype(BF16)
        total = (dot(top, w_third) + dot(rest, w_third)).astype(BF16)
        state = state_ref[rows, :]
        h = jnp.maximum(dot(state, n_state) + dot(total, n_agg), 0.0).astype(BF16)
        h = jnp.maximum(dot(h, n_second), 0.0).astype(BF16)
        update = dot(h, n_third)
        mean = jnp.mean(update, axis=1, keepdims=True)
        centred = update - mean
        var = jnp.mean(centred * centred, axis=1, keepdims=True)
        new = state.astype(F32) + centred * lax.rsqrt(var + 1e-05)
        full[rows, :] = jnp.where(live, new, MARK)
        out_ref[rows, :] = jnp.where(live, new, 0.0).astype(BF16)
        return carry

    lax.fori_loop(0, ROWS // 384, node, 0)
    pick_slabs(gidx_ref, full, picked)
    slab_ref[...] = picked[...].astype(BF16)


def one_layer(idx, steps, cnt, gidx, dead, state, mid, low, high, weights):
    return pl.pallas_call(
        layer_kernel,
        out_shape=[
            jax.ShapeDtypeStruct((ROWS, W), BF16),
            jax.ShapeDtypeStruct((8 * SLAB, W), BF16),
        ],
        in_specs=[smem()] * 4 + [vmem()] * 11,
        out_specs=[vmem()] * 2,
        scratch_shapes=[
            pltpu.VMEM((NODES + 8, W), F32),
            pltpu.VMEM((ROWS, W), F32),
            pltpu.VMEM((GHOSTS, W), BF16),
            pltpu.VMEM((DEG * GROUP, W), BF16),
            pltpu.VMEM((ROWS + GROUP, W), F32),
            pltpu.VMEM((ROWS, W), F32),
            pltpu.VMEM((8 * SLAB, W), F32),
        ],
        compiler_params=pltpu.CompilerParams(vmem_limit_bytes=VMEM_LIMIT),
        name="layer",
    )(idx, steps, cnt, gidx, dead, state, mid, low, high, *weights)


def both_ways(up, down, axis):
    n = lax.axis_size(axis)
    forward = [(i, i + 1) for i in range(n - 1)]
    backward = [(b, a) for a, b in forward]
    return lax.ppermute(up, axis, forward), lax.ppermute(down, axis, backward)


def migrate(buffer):
    for dim, axis in enumerate(HALO_AXES):
        take = lambda i: lax.index_in_dim(buffer, i, dim, keepdims=True)
        low, high = both_ways(take(2), take(0), axis)
        buffer = jnp.concatenate([low, take(1), high], axis=dim)
    return buffer


def surround(slabs):
    block = slabs.reshape(2, 2, 2, SLAB, W)
    for dim, axis in enumerate(HALO_AXES[:2]):
        low, high = both_ways(
            lax.slice_in_dim(block, 1, 2, axis=dim), lax.slice_in_dim(block, 0, 1, axis=dim), axis
        )
        block = jnp.concatenate([low, block, high], axis=dim)
    low, high = both_ways(block[:, :, 1], block[:, :, 0], "gz")
    return block, low, high


def body(
    latent,
    destination,
    neighbours,
    valid,
    ghost_index,
    edge_first,
    edge_second,
    edge_third,
    node_first,
    node_second,
    node_third,
):
    dest = destination.reshape(1, 1024)
    nbr = neighbours[0, 0, 0].T
    mask = valid[0, 0, 0].T
    gidx = ghost_index.reshape(-1)
    buffer = pack(dest, latent[0, 0, 0])
    moved = migrate(buffer.reshape(3, 3, 3, W, W))
    state, cnt, slabs = receive(gidx, moved.reshape(CODES, W, W))
    for layer in range(edge_first.shape[0]):
        weights = [
            w[layer]
            for w in (edge_first, edge_second, edge_third, node_first, node_second, node_third)
        ]
        mid, low, high = surround(slabs)
        if layer == 0:
            idx, steps, dead = indices(nbr, mask, cnt, mid, low, high)
            idx = idx.reshape(-1)
        state, slabs = one_layer(idx, steps, cnt, gidx, dead, state, mid, low, high, weights)
    return state.reshape(1, 1, 1, ROWS, W)


def solution(mesh):
    spread = P("gx", "gy", "gz", None, None)
    return jax.shard_map(
        body,
        mesh=mesh,
        in_specs=(spread,) * 5 + (P(),) * 6,
        out_specs=spread,
        check_vma=False,
    )
```

```python
import jax
import jax.numpy as jnp
import numpy as np
from jax import lax
from jax.experimental import pallas as pl
from jax.experimental.pallas import tpu as pltpu
from jax.sharding import PartitionSpec as P

F32 = jnp.float32
BF16 = jnp.bfloat16
I32 = jnp.int32
W = 128
CODES = 27
ROWS = CODES * W
DEG = 24
SLAB = 32
OUTER = [
    p for p in range(64) if p // 16 in (0, 3) or p // 4 % 4 in (0, 3) or p % 4 in (0, 3)
]
GHOSTS = len(OUTER) * SLAB
NODES = ROWS + GHOSTS
DUMMY = NODES
MARK = 2.0**100
CH = 4
HALO_AXES = ("gx", "gy", "gz")
GRID = (4, 4, 8)
VMEM_LIMIT = 56 * 2**20


def dot(a, b):
    return jnp.dot(a, b, preferred_element_type=F32)


def vmem():
    return pl.BlockSpec(memory_space=pltpu.VMEM)


def smem():
    return pl.BlockSpec(memory_space=pltpu.SMEM)


def iota(shape, dim):
    return lax.broadcasted_iota(I32, shape, dim)


def pack_kernel(dest_ref, rows_ref, out_ref, slot_ref):
    n_y, n_z = 4, 8
    ix, iy, iz = (lax.axis_index(a) for a in HALO_AXES)
    tri = (iota((W, W), 0) < iota((W, W), 1)).astype(BF16)
    ones = jnp.ones((W, W), BF16)
    off = jnp.zeros((32, W), F32)
    for j in range(8):
        d = dest_ref[:, j * W : (j + 1) * W]
        code = (
            (lax.shift_right_logical(d, 5) - ix + 1) * 9
            + ((lax.shift_right_logical(d, 3) & (n_y - 1)) - iy + 1) * 3
            + ((d & (n_z - 1)) - iz + 1)
        )
        hit = iota((32, W), 0) == code
        one = jnp.where(hit, 1.0, 0.0).astype(BF16)
        before = dot(one, tri) + off
        rank = jnp.sum(jnp.where(hit, before, 0.0), axis=0, keepdims=True)
        slot_ref[:, j * W : (j + 1) * W] = code * W + rank.astype(I32)
        off = off + dot(one, ones)
    slot = slot_ref[...]
    rows = rows_ref[...]
    for c in range(CODES):
        chosen = jnp.where(slot == iota((W, 1024), 0) + c * W, 1.0, 0.0).astype(BF16)
        got = dot(chosen, rows)
        alive = iota((W, W), 0).astype(F32) < off[c : c + 1, :]
        out_ref[c] = jnp.where(alive, got, MARK).astype(BF16)


def pack(dest, rows):
    return pl.pallas_call(
        pack_kernel,
        out_shape=jax.ShapeDtypeStruct((CODES, W, W), BF16),
        in_specs=[vmem(), vmem()],
        out_specs=vmem(),
        scratch_shapes=[pltpu.VMEM((1, 1024), I32)],
        compiler_params=pltpu.CompilerParams(vmem_limit_bytes=VMEM_LIMIT),
        name="pack",
    )(dest, rows)


def receive_kernel(gidx_ref, raw_ref, state_ref, cnt_ref, slab_ref, full, picked):
    pos = [lax.axis_index(a) for a in HALO_AXES]
    cnt_ref[...] = jnp.zeros_like(cnt_ref)
    for c in range(CODES):
        offs = (c // 9 - 1, c // 3 % 3 - 1, c % 3 - 1)
        inside = jnp.int32(1)
        for p, o, s in zip(pos, offs, GRID):
            if o < 0:
                inside = inside * (p > 0).astype(I32)
            if o > 0:
                inside = inside * (p < s - 1).astype(I32)
        x = raw_ref[c].astype(F32)
        alive = x < MARK * 0.5
        count = jnp.sum(jnp.where(alive, 1.0, 0.0), axis=0, keepdims=True).astype(I32)
        cnt_ref[c : c + 1, :] = count * inside
        present = iota((W, W), 0) < count * inside
        full[c * W : (c + 1) * W, :] = jnp.where(present, x, MARK)
        state_ref[c * W : (c + 1) * W, :] = jnp.where(present, x, 0.0).astype(BF16)
    pick_slabs(gidx_ref, full, picked)
    slab_ref[...] = picked[...].astype(BF16)


def pick_slabs(gidx_ref, full, picked):
    def some(b, carry):
        for r in range(16):
            picked[pl.ds(b * 16 + r, 1), :] = full[pl.ds(gidx_ref[b * 16 + r], 1), :]
        return carry

    lax.fori_loop(0, 16, some, 0)


def receive(gidx, raw):
    return pl.pallas_call(
        receive_kernel,
        out_shape=[
            jax.ShapeDtypeStruct((ROWS, W), BF16),
            jax.ShapeDtypeStruct((32, W), I32),
            jax.ShapeDtypeStruct((8 * SLAB, W), BF16),
        ],
        in_specs=[smem(), vmem()],
        out_specs=[vmem()] * 3,
        scratch_shapes=[pltpu.VMEM((ROWS, W), F32), pltpu.VMEM((8 * SLAB, W), F32)],
        compiler_params=pltpu.CompilerParams(vmem_limit_bytes=VMEM_LIMIT),
        name="receive",
    )(gidx, raw)


def sort_pairs(count):
    pairs = []
    size = 1
    while size < count:
        size *= 2
    p = 1
    while p < size:
        k = p
        while k >= 1:
            for j in range(k % p, size - k, 2 * k):
                for i in range(min(k, size - j - k)):
                    if (i + j) // (2 * p) == (i + j + k) // (2 * p) and i + j + k < count:
                        pairs.append((i + j, i + j + k))
            k //= 2
        p *= 2
    return pairs


def fill_ghosts(pos_ref, mid_ref, low_ref, high_ref, ghosts):
    first = [pos_ref[i] == 0 for i in range(3)]
    final = [pos_ref[i] == n - 1 for i, n in enumerate(GRID)]
    for s, p in enumerate(OUTER):
        a, b, c = p // 16, p // 4 % 4, p % 4
        absent = None
        for i, at in enumerate((a, b, c)):
            if at in (0, 3):
                edge = first[i] if at == 0 else final[i]
                absent = edge if absent is None else absent | edge
        if c == 0:
            slab = low_ref[a, b]
        elif c == 3:
            slab = high_ref[a, b]
        else:
            slab = mid_ref[a, b, c - 1]
        slab = jnp.where(absent, MARK, slab.astype(F32)).astype(BF16)
        ghosts[s * SLAB : (s + 1) * SLAB, :] = slab


def index_kernel(
    pos_ref,
    nbr_ref,
    valid_ref,
    cnt_ref,
    mid_ref,
    low_ref,
    high_ref,
    idx_ref,
    steps_ref,
    dead_ref,
    ghosts,
    held,
):
    fill_ghosts(pos_ref, mid_ref, low_ref, high_ref, ghosts)
    alive = jnp.where(ghosts[...].astype(F32) < MARK * 0.5, 1.0, 0.0).astype(BF16)
    at = iota((W, GHOSTS), 1)
    bit = jnp.left_shift(1, at & 15).astype(F32)
    spread = jnp.where(lax.shift_right_logical(at, 4) == iota((W, GHOSTS), 0), bit, 0.0)
    words = dot(spread.astype(BF16), alive)
    eye = iota((W, W), 0) == iota((W, W), 1)
    words = jnp.sum(jnp.where(eye, words, 0.0), axis=0, keepdims=True).astype(I32)
    words = jnp.broadcast_to(words, (8, W))
    counts = cnt_ref[...]
    diag = iota((32, W), 0) == iota((32, W), 1)
    by_code = jnp.sum(jnp.where(diag, counts.astype(F32), 0.0), axis=0, keepdims=True)
    by_code = jnp.broadcast_to(by_code.astype(I32), (8, W))

    held[...] = jnp.zeros_like(held) - 1
    for c in range(CODES):
        cols = slice(c * W, (c + 1) * W)
        held[c * DEG : (c + 1) * DEG, :] = jnp.where(valid_ref[:, cols] > 0, nbr_ref[:, cols], -1)

    for b in range(4):
        here = iota((8, W), 1) < counts[b * 8 : (b + 1) * 8, :]
        keys = []
        dead = jnp.zeros((8, W), F32)
        for k in range(DEG):
            node = held[pl.ds(b * 8 * DEG + k, 8, stride=DEG), :]
            far = jnp.maximum(node - ROWS, 0)
            word = jnp.take_along_axis(words, lax.shift_right_logical(far, 4), axis=1)
            flag = lax.shift_right_logical(word, far & 15) & 1
            near = jnp.minimum(jnp.maximum(node, 0), ROWS - 1)
            limit = jnp.take_along_axis(by_code, lax.shift_right_logical(near, 7), axis=1)
            lives = jnp.where(node >= ROWS, flag, jnp.where((near & (W - 1)) < limit, 1, 0))
            real = node >= 0
            key = jnp.where(here & real & (lives > 0), node, DUMMY)
            dead = dead + jnp.where(here & real & (lives == 0), 1.0, 0.0)
            keys.append(key.astype(F32))
        for i, j in sort_pairs(DEG):
            keys[i], keys[j] = jnp.minimum(keys[i], keys[j]), jnp.maximum(keys[i], keys[j])
        used = jnp.zeros((8, W), F32)
        for k in range(DEG):
            used = used + jnp.where(keys[k] < DUMMY, 1.0, 0.0)
            idx_ref[pl.ds(b * 8 * DEG + k, 8, stride=DEG), :] = keys[k].astype(I32)
        for shift in (1, 2, 4, 8):
            used = jnp.maximum(used, pltpu.roll(used, W - shift, 1))
        steps_ref[b * 8 : (b + 1) * 8, :] = used.astype(I32)
        dead_ref[b * 8 : (b + 1) * 8, :] = dead


def indices(pos, nbr, valid, cnt, mid, low, high):
    return pl.pallas_call(
        index_kernel,
        out_shape=[
            jax.ShapeDtypeStruct((DEG * 32, W), I32),
            jax.ShapeDtypeStruct((32, W), I32),
            jax.ShapeDtypeStruct((32, W), F32),
        ],
        in_specs=[smem()] + [vmem()] * 6,
        out_specs=[vmem()] * 3,
        scratch_shapes=[pltpu.VMEM((GHOSTS, W), BF16), pltpu.VMEM((32 * DEG, W), I32)],
        compiler_params=pltpu.CompilerParams(vmem_limit_bytes=VMEM_LIMIT),
        name="indices",
    )(pos, nbr, valid, cnt, mid, low, high)


GROUP = 16
FIRST = 8
TAILS = (0, 2, 4, 6, 8, 10, 12, 16)
DUMP = ROWS
PARTS = ((0, 3), (3, 11), (11, CODES))


def layer_kernel(
    idx_hbm,
    pos_ref,
    steps_ref,
    cnt_ref,
    gidx_ref,
    dead_ref,
    state_ref,
    mid_ref,
    low_ref,
    high_ref,
    efirst_ref,
    esecond_ref,
    ethird_ref,
    nfirst_ref,
    nsecond_ref,
    nthird_ref,
    out_ref,
    slab_ref,
    table,
    recv,
    ghosts,
    hidden,
    agg,
    full,
    picked,
    idx_ref,
    sems,
):
    copies = []
    for i, (lo, hi) in enumerate(PARTS):
        words = pl.ds(lo * DEG * W, (hi - lo) * DEG * W)
        copies.append(pltpu.make_async_copy(idx_hbm.at[words], idx_ref.at[words], sems.at[i]))
        copies[-1].start()
    w_recv = efirst_ref[0:W, :]
    w_send = efirst_ref[W : 2 * W, :]
    w_both = jnp.concatenate([w_recv, w_send], axis=1)
    fill_ghosts(pos_ref, mid_ref, low_ref, high_ref, ghosts)

    def own(i, carry):
        rows = pl.ds(pl.multiple_of(i * 384, 384), 384)
        both = dot(state_ref[rows, :], w_both)
        recv[rows, :] = both[:, :W]
        table[rows, :] = both[:, W:]
        return carry

    lax.fori_loop(0, ROWS // 384, own, 0)

    def far(i, carry):
        x = ghosts[pl.ds(pl.multiple_of(i * 256, 256), 256), :].astype(F32)
        x = jnp.where(x < MARK * 0.5, x, 0.0).astype(BF16)
        table[pl.ds(pl.multiple_of(ROWS + i * 256, 128), 256), :] = dot(x, w_send)
        return carry

    lax.fori_loop(0, GHOSTS // 256, far, 0)
    table[NODES : NODES + 8, :] = jnp.full((8, W), -MARK, F32)

    w_second = esecond_ref[...]
    sub = iota((8, W), 0)

    def finish(h, row):
        d = jnp.maximum(dot(h, w_second), 0.0)
        agg[pl.ds(pl.multiple_of(row, GROUP), GROUP), :] = jnp.sum(
            d.reshape(DEG, GROUP, W), axis=0
        )

    def step(base, mine, k):
        both = []
        for half in range(2):
            got = None
            for r in range(8):
                at = idx_ref[base + (k * W + half * 8 + r)]
                row = jnp.broadcast_to(table[pl.ds(at, 1), :], (8, W))
                got = row if got is None else jnp.where(sub == r, row, got)
            both.append(jnp.maximum(got + mine[half], 0.0))
        hidden[k * GROUP : (k + 1) * GROUP, :] = jnp.concatenate(both, axis=0).astype(BF16)

    def sender(c, last):
        groups = lax.shift_right_logical(cnt_ref[c, 0] + (GROUP - 1), 4)
        for (lo, _), copy in zip(PARTS, copies):
            pl.when(c == lo)(copy.wait)

        def gather(g, last):
            q0 = pl.multiple_of(g * GROUP, GROUP)
            home = c * W + q0
            base = c * (DEG * W) + q0
            mine = [recv[pl.ds(pl.multiple_of(home + h * 8, 8), 8), :] for h in range(2)]
            finish(hidden[...], last)
            for k in range(FIRST):
                step(base, mine, k)
            more = steps_ref[c, q0] - FIRST
            which = sum((more > t).astype(I32) for t in TAILS[:-1])

            def tail(size):
                def run():
                    for k in range(FIRST, FIRST + size):
                        step(base, mine, k)
                    if FIRST + size < DEG:
                        hidden[(FIRST + size) * GROUP :, :] = jnp.zeros(
                            ((DEG - FIRST - size) * GROUP, W), BF16
                        )

                return run

            lax.switch(which, [tail(t) for t in TAILS])
            return home

        return lax.fori_loop(0, groups, gather, last)

    last = lax.fori_loop(0, CODES, sender, jnp.int32(DUMP))
    finish(hidden[...], last)

    w_third = ethird_ref[...]
    n_state = nfirst_ref[0:W, :]
    n_agg = nfirst_ref[W : 2 * W, :]
    n_second = nsecond_ref[...]
    n_third = nthird_ref[...]
    eye = iota((W, W), 0) == iota((W, W), 1)
    ones = jnp.ones((W, W), BF16)

    def node(i, carry):
        rows = pl.ds(pl.multiple_of(i * 384, 384), 384)
        live = jnp.concatenate(
            [iota((W, W), 0) < cnt_ref[i * 3 + j, 0] for j in range(3)], axis=0
        )
        times = jnp.concatenate(
            [
                jnp.where(eye, jnp.broadcast_to(dead_ref[pl.ds(i * 3 + j, 1), :], (W, W)), 0.0)
                for j in range(3)
            ],
            axis=0,
        )
        times = dot(times.astype(BF16), ones)
        alone = jnp.maximum(recv[rows, :], 0.0).astype(BF16)
        alone = jnp.maximum(dot(alone, w_second), 0.0)
        summed = jnp.where(live, agg[rows, :] + times * alone, 0.0)
        top = summed.astype(BF16)
        rest = (summed - top.astype(F32)).astype(BF16)
        total = (dot(top, w_third) + dot(rest, w_third)).astype(BF16)
        state = state_ref[rows, :]
        h = jnp.maximum(dot(state, n_state) + dot(total, n_agg), 0.0).astype(BF16)
        h = jnp.maximum(dot(h, n_second), 0.0).astype(BF16)
        update = dot(h, n_third)
        mean = jnp.mean(update, axis=1, keepdims=True)
        centred = update - mean
        var = jnp.mean(centred * centred, axis=1, keepdims=True)
        new = state.astype(F32) + centred * lax.rsqrt(var + 1e-05)
        full[rows, :] = jnp.where(live, new, MARK)
        out_ref[rows, :] = jnp.where(live, new, 0.0).astype(BF16)
        return carry

    lax.fori_loop(0, ROWS // 384, node, 0)
    pick_slabs(gidx_ref, full, picked)
    slab_ref[...] = picked[...].astype(BF16)


def one_layer(idx, pos, steps, cnt, gidx, dead, state, mid, low, high, weights):
    return pl.pallas_call(
        layer_kernel,
        out_shape=[
            jax.ShapeDtypeStruct((ROWS, W), BF16),
            jax.ShapeDtypeStruct((8 * SLAB, W), BF16),
        ],
        in_specs=[pl.BlockSpec(memory_space=pl.ANY)] + [smem()] * 4 + [vmem()] * 11,
        out_specs=[vmem()] * 2,
        scratch_shapes=[
            pltpu.VMEM((NODES + 8, W), F32),
            pltpu.VMEM((ROWS, W), F32),
            pltpu.VMEM((GHOSTS, W), BF16),
            pltpu.VMEM((DEG * GROUP, W), BF16),
            pltpu.VMEM((ROWS + GROUP, W), F32),
            pltpu.VMEM((ROWS, W), F32),
            pltpu.VMEM((8 * SLAB, W), F32),
            pltpu.SMEM((ROWS * DEG,), I32),
            pltpu.SemaphoreType.DMA((len(PARTS),)),
        ],
        compiler_params=pltpu.CompilerParams(vmem_limit_bytes=VMEM_LIMIT),
        name="layer",
    )(idx, pos, steps, cnt, gidx, dead, state, mid, low, high, *weights)


def both_ways(up, down, axis):
    n = lax.axis_size(axis)
    forward = [(i, (i + 1) % n) for i in range(n)]
    backward = [(b, a) for a, b in forward]
    return lax.ppermute(up, axis, forward), lax.ppermute(down, axis, backward)


def migrate(buffer):
    for dim, axis in enumerate(HALO_AXES):
        take = lambda i: lax.index_in_dim(buffer, i, dim, keepdims=True)
        low, high = both_ways(take(2), take(0), axis)
        buffer = jnp.concatenate([low, take(1), high], axis=dim)
    return buffer


def surround(slabs):
    block = slabs.reshape(2, 2, 2, SLAB, W)
    for dim, axis in enumerate(HALO_AXES[:2]):
        low, high = both_ways(
            lax.slice_in_dim(block, 1, 2, axis=dim), lax.slice_in_dim(block, 0, 1, axis=dim), axis
        )
        block = jnp.concatenate([low, block, high], axis=dim)
    low, high = both_ways(block[:, :, 1], block[:, :, 0], "gz")
    return block, low, high


def body(
    latent,
    destination,
    neighbours,
    valid,
    ghost_index,
    edge_first,
    edge_second,
    edge_third,
    node_first,
    node_second,
    node_third,
):
    dest = destination.reshape(1, 1024)
    nbr = neighbours[0, 0, 0].T
    mask = valid[0, 0, 0].T
    gidx = ghost_index.reshape(-1)
    pos = jnp.stack([lax.axis_index(a) for a in HALO_AXES]).astype(I32)
    buffer = pack(dest, latent[0, 0, 0])
    moved = migrate(buffer.reshape(3, 3, 3, W, W))
    state, cnt, slabs = receive(gidx, moved.reshape(CODES, W, W))
    for layer in range(edge_first.shape[0]):
        weights = [
            w[layer]
            for w in (edge_first, edge_second, edge_third, node_first, node_second, node_third)
        ]
        mid, low, high = surround(slabs)
        if layer == 0:
            idx, steps, dead = indices(pos, nbr, mask, cnt, mid, low, high)
            idx = idx.reshape(-1)
        state, slabs = one_layer(idx, pos, steps, cnt, gidx, dead, state, mid, low, high, weights)
    return state.reshape(1, 1, 1, ROWS, W)


def solution(mesh):
    spread = P("gx", "gy", "gz", None, None)
    return jax.shard_map(
        body,
        mesh=mesh,
        in_specs=(spread,) * 5 + (P(),) * 6,
        out_specs=spread,
        check_vma=False,
    )
```

```python
import jax
import jax.numpy as jnp
import numpy as np
from jax import lax
from jax.experimental import pallas as pl
from jax.experimental.pallas import tpu as pltpu
from jax.sharding import PartitionSpec as P

F32 = jnp.float32
BF16 = jnp.bfloat16
I32 = jnp.int32
W = 128
CODES = 27
ROWS = CODES * W
DEG = 24
SLAB = 32
OUTER = [
    p for p in range(64) if p // 16 in (0, 3) or p // 4 % 4 in (0, 3) or p % 4 in (0, 3)
]
GHOSTS = len(OUTER) * SLAB
NODES = ROWS + GHOSTS
DUMMY = NODES
MARK = 2.0**100
CH = 4
HALO_AXES = ("gx", "gy", "gz")
GRID = (4, 4, 8)
VMEM_LIMIT = 56 * 2**20


def dot(a, b):
    return jnp.dot(a, b, preferred_element_type=F32)


def vmem():
    return pl.BlockSpec(memory_space=pltpu.VMEM)


def smem():
    return pl.BlockSpec(memory_space=pltpu.SMEM)


def iota(shape, dim):
    return lax.broadcasted_iota(I32, shape, dim)


def pack_kernel(dest_ref, rows_ref, out_ref, slot_ref):
    n_y, n_z = 4, 8
    ix, iy, iz = (lax.axis_index(a) for a in HALO_AXES)
    tri = (iota((W, W), 0) < iota((W, W), 1)).astype(BF16)
    ones = jnp.ones((W, W), BF16)
    off = jnp.zeros((32, W), F32)
    for j in range(8):
        d = dest_ref[:, j * W : (j + 1) * W]
        code = (
            (lax.shift_right_logical(d, 5) - ix + 1) * 9
            + ((lax.shift_right_logical(d, 3) & (n_y - 1)) - iy + 1) * 3
            + ((d & (n_z - 1)) - iz + 1)
        )
        hit = iota((32, W), 0) == code
        one = jnp.where(hit, 1.0, 0.0).astype(BF16)
        before = dot(one, tri) + off
        rank = jnp.sum(jnp.where(hit, before, 0.0), axis=0, keepdims=True)
        slot_ref[:, j * W : (j + 1) * W] = code * W + rank.astype(I32)
        off = off + dot(one, ones)
    slot = slot_ref[...]
    rows = rows_ref[...]
    for c in range(CODES):
        chosen = jnp.where(slot == iota((W, 1024), 0) + c * W, 1.0, 0.0).astype(BF16)
        got = dot(chosen, rows)
        alive = iota((W, W), 0).astype(F32) < off[c : c + 1, :]
        out_ref[c] = jnp.where(alive, got, MARK).astype(BF16)


def pack(dest, rows):
    return pl.pallas_call(
        pack_kernel,
        out_shape=jax.ShapeDtypeStruct((CODES, W, W), BF16),
        in_specs=[vmem(), vmem()],
        out_specs=vmem(),
        scratch_shapes=[pltpu.VMEM((1, 1024), I32)],
        compiler_params=pltpu.CompilerParams(vmem_limit_bytes=VMEM_LIMIT),
        name="pack",
    )(dest, rows)


def receive_kernel(gidx_ref, raw_ref, state_ref, cnt_ref, slab_ref, full, picked):
    pos = [lax.axis_index(a) for a in HALO_AXES]
    cnt_ref[...] = jnp.zeros_like(cnt_ref)
    for c in range(CODES):
        offs = (c // 9 - 1, c // 3 % 3 - 1, c % 3 - 1)
        inside = jnp.int32(1)
        for p, o, s in zip(pos, offs, GRID):
            if o < 0:
                inside = inside * (p > 0).astype(I32)
            if o > 0:
                inside = inside * (p < s - 1).astype(I32)
        x = raw_ref[c].astype(F32)
        alive = x < MARK * 0.5
        count = jnp.sum(jnp.where(alive, 1.0, 0.0), axis=0, keepdims=True).astype(I32)
        cnt_ref[c : c + 1, :] = count * inside
        present = iota((W, W), 0) < count * inside
        full[c * W : (c + 1) * W, :] = jnp.where(present, x, MARK)
        state_ref[c * W : (c + 1) * W, :] = jnp.where(present, x, 0.0).astype(BF16)
    pick_slabs(gidx_ref, full, picked)
    slab_ref[...] = picked[...].astype(BF16)


def pick_slabs(gidx_ref, full, picked):
    def some(b, carry):
        for r in range(16):
            picked[pl.ds(b * 16 + r, 1), :] = full[pl.ds(gidx_ref[b * 16 + r], 1), :]
        return carry

    lax.fori_loop(0, 16, some, 0)


def receive(gidx, raw):
    return pl.pallas_call(
        receive_kernel,
        out_shape=[
            jax.ShapeDtypeStruct((ROWS, W), BF16),
            jax.ShapeDtypeStruct((32, W), I32),
            jax.ShapeDtypeStruct((8 * SLAB, W), BF16),
        ],
        in_specs=[smem(), vmem()],
        out_specs=[vmem()] * 3,
        scratch_shapes=[pltpu.VMEM((ROWS, W), F32), pltpu.VMEM((8 * SLAB, W), F32)],
        compiler_params=pltpu.CompilerParams(vmem_limit_bytes=VMEM_LIMIT),
        name="receive",
    )(gidx, raw)


def sort_pairs(count):
    pairs = []
    size = 1
    while size < count:
        size *= 2
    p = 1
    while p < size:
        k = p
        while k >= 1:
            for j in range(k % p, size - k, 2 * k):
                for i in range(min(k, size - j - k)):
                    if (i + j) // (2 * p) == (i + j + k) // (2 * p) and i + j + k < count:
                        pairs.append((i + j, i + j + k))
            k //= 2
        p *= 2
    return pairs


def fill_ghosts(pos_ref, mid_ref, low_ref, high_ref, ghosts):
    first = [pos_ref[i] == 0 for i in range(3)]
    final = [pos_ref[i] == n - 1 for i, n in enumerate(GRID)]
    for s, p in enumerate(OUTER):
        a, b, c = p // 16, p // 4 % 4, p % 4
        absent = None
        for i, at in enumerate((a, b, c)):
            if at in (0, 3):
                edge = first[i] if at == 0 else final[i]
                absent = edge if absent is None else absent | edge
        if c == 0:
            slab = low_ref[a, b]
        elif c == 3:
            slab = high_ref[a, b]
        else:
            slab = mid_ref[a, b, c - 1]
        slab = jnp.where(absent, MARK, slab.astype(F32)).astype(BF16)
        ghosts[s * SLAB : (s + 1) * SLAB, :] = slab


def index_kernel(
    pos_ref,
    nbr_ref,
    valid_ref,
    cnt_ref,
    mid_ref,
    low_ref,
    high_ref,
    idx_ref,
    steps_ref,
    dead_ref,
    ghosts,
    held,
):
    fill_ghosts(pos_ref, mid_ref, low_ref, high_ref, ghosts)
    alive = jnp.where(ghosts[...].astype(F32) < MARK * 0.5, 1.0, 0.0).astype(BF16)
    at = iota((W, GHOSTS), 1)
    bit = jnp.left_shift(1, at & 15).astype(F32)
    spread = jnp.where(lax.shift_right_logical(at, 4) == iota((W, GHOSTS), 0), bit, 0.0)
    words = dot(spread.astype(BF16), alive)
    eye = iota((W, W), 0) == iota((W, W), 1)
    words = jnp.sum(jnp.where(eye, words, 0.0), axis=0, keepdims=True).astype(I32)
    words = jnp.broadcast_to(words, (8, W))
    counts = cnt_ref[...]
    diag = iota((32, W), 0) == iota((32, W), 1)
    by_code = jnp.sum(jnp.where(diag, counts.astype(F32), 0.0), axis=0, keepdims=True)
    by_code = jnp.broadcast_to(by_code.astype(I32), (8, W))

    held[...] = jnp.zeros_like(held) - 1
    for c in range(CODES):
        cols = slice(c * W, (c + 1) * W)
        held[c * DEG : (c + 1) * DEG, :] = jnp.where(valid_ref[:, cols] > 0, nbr_ref[:, cols], -1)

    for b in range(4):
        here = iota((8, W), 1) < counts[b * 8 : (b + 1) * 8, :]
        keys = []
        dead = jnp.zeros((8, W), F32)
        for k in range(DEG):
            node = held[pl.ds(b * 8 * DEG + k, 8, stride=DEG), :]
            far = jnp.maximum(node - ROWS, 0)
            word = jnp.take_along_axis(words, lax.shift_right_logical(far, 4), axis=1)
            flag = lax.shift_right_logical(word, far & 15) & 1
            near = jnp.minimum(jnp.maximum(node, 0), ROWS - 1)
            limit = jnp.take_along_axis(by_code, lax.shift_right_logical(near, 7), axis=1)
            lives = jnp.where(node >= ROWS, flag, jnp.where((near & (W - 1)) < limit, 1, 0))
            real = node >= 0
            key = jnp.where(here & real & (lives > 0), node, DUMMY)
            dead = dead + jnp.where(here & real & (lives == 0), 1.0, 0.0)
            keys.append(key.astype(F32))
        for i, j in sort_pairs(DEG):
            keys[i], keys[j] = jnp.minimum(keys[i], keys[j]), jnp.maximum(keys[i], keys[j])
        used = jnp.zeros((8, W), F32)
        for k in range(DEG):
            used = used + jnp.where(keys[k] < DUMMY, 1.0, 0.0)
            idx_ref[pl.ds(b * 8 * DEG + k, 8, stride=DEG), :] = keys[k].astype(I32)
        for shift in (1, 2, 4, 8):
            used = jnp.maximum(used, pltpu.roll(used, W - shift, 1))
        steps_ref[b * 8 : (b + 1) * 8, :] = used.astype(I32)
        dead_ref[b * 8 : (b + 1) * 8, :] = dead


def indices(pos, nbr, valid, cnt, mid, low, high):
    return pl.pallas_call(
        index_kernel,
        out_shape=[
            jax.ShapeDtypeStruct((DEG * 32, W), I32),
            jax.ShapeDtypeStruct((32, W), I32),
            jax.ShapeDtypeStruct((32, W), F32),
        ],
        in_specs=[smem()] + [vmem()] * 6,
        out_specs=[vmem()] * 3,
        scratch_shapes=[pltpu.VMEM((GHOSTS, W), BF16), pltpu.VMEM((32 * DEG, W), I32)],
        compiler_params=pltpu.CompilerParams(vmem_limit_bytes=VMEM_LIMIT),
        name="indices",
    )(pos, nbr, valid, cnt, mid, low, high)


GROUP = 16
SPAN = 27
FIRST = 13
TAILS = (0, 1, 2, 3, 5, 7, 11)
DUMP = ROWS
PARTS = ((0, 3), (3, 11), (11, CODES))


def layer_kernel(
    idx_hbm,
    pos_ref,
    steps_ref,
    cnt_ref,
    gidx_ref,
    dead_ref,
    state_ref,
    mid_ref,
    low_ref,
    high_ref,
    efirst_ref,
    esecond_ref,
    ethird_ref,
    nfirst_ref,
    nsecond_ref,
    nthird_ref,
    out_ref,
    slab_ref,
    table,
    recv,
    ghosts,
    hidden,
    agg,
    full,
    picked,
    idx_ref,
    sems,
):
    copies = []
    for i, (lo, hi) in enumerate(PARTS):
        words = pl.ds(lo * DEG * W, (hi - lo) * DEG * W)
        copies.append(pltpu.make_async_copy(idx_hbm.at[words], idx_ref.at[words], sems.at[i]))
        copies[-1].start()
    w_recv = efirst_ref[0:W, :]
    w_send = efirst_ref[W : 2 * W, :]
    w_both = jnp.concatenate([w_recv, w_send], axis=1)
    fill_ghosts(pos_ref, mid_ref, low_ref, high_ref, ghosts)

    def own(i, carry):
        rows = pl.ds(pl.multiple_of(i * 1152, 1152), 1152)
        both = dot(state_ref[rows, :], w_both)
        recv[rows, :] = both[:, :W]
        table[rows, :] = both[:, W:]
        return carry

    lax.fori_loop(0, ROWS // 1152, own, 0)

    def far(i, carry):
        x = ghosts[pl.ds(pl.multiple_of(i * 896, 128), 896), :].astype(F32)
        x = jnp.where(x < MARK * 0.5, x, 0.0).astype(BF16)
        table[pl.ds(pl.multiple_of(ROWS + i * 896, 128), 896), :] = dot(x, w_send)
        return carry

    lax.fori_loop(0, GHOSTS // 896, far, 0)
    table[NODES : NODES + 8, :] = jnp.full((8, W), -MARK, F32)

    w_second = esecond_ref[...]
    sub = iota((8, W), 0)

    def finish(h, row):
        d = jnp.maximum(dot(h, w_second), 0.0).astype(BF16).astype(F32)
        agg[pl.ds(pl.multiple_of(row, GROUP), GROUP), :] = jnp.sum(
            d.reshape(DEG, GROUP, W), axis=0
        )

    def step(base, mine, k):
        both = []
        for half in range(2):
            got = None
            for r in range(8):
                at = idx_ref[base + (k * W + half * 8 + r)]
                row = jnp.broadcast_to(table[pl.ds(at, 1), :], (8, W))
                got = row if got is None else jnp.where(sub == r, row, got)
            both.append(jnp.maximum(got + mine[half], 0.0))
        hidden[k * GROUP : (k + 1) * GROUP, :] = jnp.concatenate(both, axis=0).astype(BF16)

    def sender(c, last):
        groups = lax.shift_right_logical(cnt_ref[c, 0] + (GROUP - 1), 4)
        for (lo, _), copy in zip(PARTS, copies):
            pl.when(c == lo)(copy.wait)

        def gather(g, last):
            q0 = pl.multiple_of(g * GROUP, GROUP)
            home = c * W + q0
            base = c * (DEG * W) + q0
            mine = [recv[pl.ds(pl.multiple_of(home + h * 8, 8), 8), :] for h in range(2)]
            finish(hidden[...], last)
            for k in range(FIRST):
                step(base, mine, k)
            more = steps_ref[c, q0] - FIRST
            which = sum((more > t).astype(I32) for t in TAILS[:-1])

            def tail(size):
                def run():
                    for k in range(FIRST, FIRST + size):
                        step(base, mine, k)
                    if FIRST + size < DEG:
                        hidden[(FIRST + size) * GROUP :, :] = jnp.zeros(
                            ((DEG - FIRST - size) * GROUP, W), BF16
                        )

                return run

            lax.switch(which, [tail(t) for t in TAILS])
            return home

        return lax.fori_loop(0, groups, gather, last)

    last = lax.fori_loop(0, CODES, sender, jnp.int32(DUMP))
    finish(hidden[...], last)

    w_third = ethird_ref[...]
    n_state = nfirst_ref[0:W, :]
    n_agg = nfirst_ref[W : 2 * W, :]
    n_second = nsecond_ref[...]
    n_third = nthird_ref[...]
    eye = iota((W, W), 0) == iota((W, W), 1)
    ones = jnp.ones((W, W), BF16)

    def node(i, carry):
        rows = pl.ds(pl.multiple_of(i * (SPAN * W), SPAN * W), SPAN * W)
        live = jnp.concatenate(
            [iota((W, W), 0) < cnt_ref[i * SPAN + j, 0] for j in range(SPAN)], axis=0
        )
        times = jnp.concatenate(
            [
                jnp.where(eye, jnp.broadcast_to(dead_ref[pl.ds(i * SPAN + j, 1), :], (W, W)), 0.0)
                for j in range(SPAN)
            ],
            axis=0,
        )
        times = dot(times.astype(BF16), ones)
        alone = jnp.maximum(recv[rows, :], 0.0).astype(BF16)
        alone = jnp.maximum(dot(alone, w_second), 0.0)
        summed = jnp.where(live, agg[rows, :] + times * alone, 0.0)
        top = summed.astype(BF16)
        rest = (summed - top.astype(F32)).astype(BF16)
        total = (dot(top, w_third) + dot(rest, w_third)).astype(BF16)
        state = state_ref[rows, :]
        h = jnp.maximum(dot(state, n_state) + dot(total, n_agg), 0.0).astype(BF16)
        h = jnp.maximum(dot(h, n_second), 0.0).astype(BF16)
        update = dot(h, n_third)
        mean = jnp.mean(update, axis=1, keepdims=True)
        centred = update - mean
        var = jnp.mean(centred * centred, axis=1, keepdims=True)
        new = state.astype(F32) + centred * lax.rsqrt(var + 1e-05)
        full[rows, :] = jnp.where(live, new, MARK)
        out_ref[rows, :] = jnp.where(live, new, 0.0).astype(BF16)
        return carry

    lax.fori_loop(0, ROWS // (SPAN * W), node, 0)
    pick_slabs(gidx_ref, full, picked)
    slab_ref[...] = picked[...].astype(BF16)


def one_layer(idx, pos, steps, cnt, gidx, dead, state, mid, low, high, weights):
    return pl.pallas_call(
        layer_kernel,
        out_shape=[
            jax.ShapeDtypeStruct((ROWS, W), BF16),
            jax.ShapeDtypeStruct((8 * SLAB, W), BF16),
        ],
        in_specs=[pl.BlockSpec(memory_space=pl.ANY)] + [smem()] * 4 + [vmem()] * 11,
        out_specs=[vmem()] * 2,
        scratch_shapes=[
            pltpu.VMEM((NODES + 8, W), F32),
            pltpu.VMEM((ROWS, W), F32),
            pltpu.VMEM((GHOSTS, W), BF16),
            pltpu.VMEM((DEG * GROUP, W), BF16),
            pltpu.VMEM((ROWS + GROUP, W), F32),
            pltpu.VMEM((ROWS, W), F32),
            pltpu.VMEM((8 * SLAB, W), F32),
            pltpu.SMEM((ROWS * DEG,), I32),
            pltpu.SemaphoreType.DMA((len(PARTS),)),
        ],
        compiler_params=pltpu.CompilerParams(vmem_limit_bytes=VMEM_LIMIT),
        name="layer",
    )(idx, pos, steps, cnt, gidx, dead, state, mid, low, high, *weights)


def both_ways(up, down, axis):
    n = lax.axis_size(axis)
    forward = [(i, (i + 1) % n) for i in range(n)]
    backward = [(b, a) for a, b in forward]
    return lax.ppermute(up, axis, forward), lax.ppermute(down, axis, backward)


def migrate(buffer):
    for dim, axis in enumerate(HALO_AXES):
        take = lambda i: lax.index_in_dim(buffer, i, dim, keepdims=True)
        low, high = both_ways(take(2), take(0), axis)
        buffer = jnp.concatenate([low, take(1), high], axis=dim)
    return buffer


def surround(slabs):
    block = slabs.reshape(2, 2, 2, SLAB, W)
    for dim, axis in enumerate(HALO_AXES[:2]):
        low, high = both_ways(
            lax.slice_in_dim(block, 1, 2, axis=dim), lax.slice_in_dim(block, 0, 1, axis=dim), axis
        )
        block = jnp.concatenate([low, block, high], axis=dim)
    low, high = both_ways(block[:, :, 1], block[:, :, 0], "gz")
    return block, low, high


def body(
    latent,
    destination,
    neighbours,
    valid,
    ghost_index,
    edge_first,
    edge_second,
    edge_third,
    node_first,
    node_second,
    node_third,
):
    dest = destination.reshape(1, 1024)
    nbr = neighbours[0, 0, 0].T
    mask = valid[0, 0, 0].T
    gidx = ghost_index.reshape(-1)
    pos = jnp.stack([lax.axis_index(a) for a in HALO_AXES]).astype(I32)
    buffer = pack(dest, latent[0, 0, 0])
    moved = migrate(buffer.reshape(3, 3, 3, W, W))
    state, cnt, slabs = receive(gidx, moved.reshape(CODES, W, W))
    for layer in range(edge_first.shape[0]):
        weights = [
            w[layer]
            for w in (edge_first, edge_second, edge_third, node_first, node_second, node_third)
        ]
        mid, low, high = surround(slabs)
        if layer == 0:
            idx, steps, dead = indices(pos, nbr, mask, cnt, mid, low, high)
            idx = idx.reshape(-1)
        state, slabs = one_layer(idx, pos, steps, cnt, gidx, dead, state, mid, low, high, weights)
    return state.reshape(1, 1, 1, ROWS, W)


def solution(mesh):
    spread = P("gx", "gy", "gz", None, None)
    return jax.shard_map(
        body,
        mesh=mesh,
        in_specs=(spread,) * 5 + (P(),) * 6,
        out_specs=spread,
        check_vma=False,
    )
```

```python
import jax
import jax.numpy as jnp
import numpy as np
from jax import lax
from jax.experimental import pallas as pl
from jax.experimental.pallas import tpu as pltpu
from jax.sharding import PartitionSpec as P

F32 = jnp.float32
BF16 = jnp.bfloat16
I32 = jnp.int32
W = 128
CODES = 27
ROWS = CODES * W
DEG = 24
SLAB = 32
OUTER = [
    p for p in range(64) if p // 16 in (0, 3) or p // 4 % 4 in (0, 3) or p % 4 in (0, 3)
]
AROUND = 6
GHOSTS = len(OUTER) * SLAB
NODES = ROWS + GHOSTS
DUMMY = NODES
MARK = 2.0**100
HALO_AXES = ("gx", "gy", "gz")
GRID = (4, 4, 8)
VMEM_LIMIT = 56 * 2**20


def dot(a, b):
    return jnp.dot(a, b, preferred_element_type=F32)


def vmem():
    return pl.BlockSpec(memory_space=pltpu.VMEM)


def smem():
    return pl.BlockSpec(memory_space=pltpu.SMEM)


def iota(shape, dim):
    return lax.broadcasted_iota(I32, shape, dim)


def pack_kernel(dest_ref, rows_ref, down_ref, mid_ref, up_ref, slot_ref):
    n_y, n_z = 4, 8
    ix, iy, iz = (lax.axis_index(a) for a in HALO_AXES)
    tri = (iota((W, W), 0) < iota((W, W), 1)).astype(BF16)
    ones = jnp.ones((W, W), BF16)
    off = jnp.zeros((32, W), F32)
    for j in range(8):
        d = dest_ref[:, j * W : (j + 1) * W]
        code = (
            (lax.shift_right_logical(d, 5) - ix + 1) * 9
            + ((lax.shift_right_logical(d, 3) & (n_y - 1)) - iy + 1) * 3
            + ((d & (n_z - 1)) - iz + 1)
        )
        hit = iota((32, W), 0) == code
        one = jnp.where(hit, 1.0, 0.0).astype(BF16)
        before = dot(one, tri) + off
        rank = jnp.sum(jnp.where(hit, before, 0.0), axis=0, keepdims=True)
        slot_ref[:, j * W : (j + 1) * W] = code * W + rank.astype(I32)
        off = off + dot(one, ones)
    slot = slot_ref[...]
    rows = rows_ref[...]
    for part, out_ref in enumerate((down_ref, mid_ref, up_ref)):
        first = part * 9 * W
        chosen = jnp.where(slot == iota((9 * W, 1024), 0) + first, 1.0, 0.0).astype(BF16)
        got = dot(chosen, rows)
        for c in range(9):
            alive = iota((W, W), 0).astype(F32) < off[part * 9 + c : part * 9 + c + 1, :]
            block = jnp.where(alive, got[c * W : (c + 1) * W, :], MARK)
            out_ref[c // 3, c % 3] = block.astype(BF16)


def pack(dest, rows):
    return pl.pallas_call(
        pack_kernel,
        out_shape=[jax.ShapeDtypeStruct((3, 3, W, W), BF16)] * 3,
        in_specs=[vmem(), vmem()],
        out_specs=[vmem()] * 3,
        scratch_shapes=[pltpu.VMEM((1, 1024), I32)],
        compiler_params=pltpu.CompilerParams(vmem_limit_bytes=VMEM_LIMIT),
        name="pack",
    )(dest, rows)


def receive_kernel(
    gidx_ref, mid_ref, low_ref, high_ref, state_ref, cnt_ref, down_ref, up_ref, full, picked
):
    pos = [lax.axis_index(a) for a in HALO_AXES]
    cnt_ref[...] = jnp.zeros_like(cnt_ref)
    for c in range(CODES):
        offs = (c // 9 - 1, c // 3 % 3 - 1, c % 3 - 1)
        inside = jnp.int32(1)
        for p, o, s in zip(pos, offs, GRID):
            if o < 0:
                inside = inside * (p > 0).astype(I32)
            if o > 0:
                inside = inside * (p < s - 1).astype(I32)
        if c % 3 == 1:
            x = mid_ref[c // 9, c // 3 % 3].astype(F32)
        else:
            x = (low_ref if c % 3 == 0 else high_ref)[c // 9, c // 3 % 3].astype(F32)
        alive = x < MARK * 0.5
        count = jnp.sum(jnp.where(alive, 1.0, 0.0), axis=0, keepdims=True).astype(I32)
        cnt_ref[c : c + 1, :] = count * inside
        present = iota((W, W), 0) < count * inside
        full[c * W : (c + 1) * W, :] = jnp.where(present, x, MARK)
        state_ref[c * W : (c + 1) * W, :] = jnp.where(present, x, 0.0).astype(BF16)
    pick_slabs(gidx_ref, full, picked, down_ref, up_ref)


def pick_slabs(gidx_ref, full, picked, down_ref, up_ref):
    def some(b, carry):
        for r in range(16):
            picked[pl.ds(b * 16 + r, 1), :] = full[pl.ds(gidx_ref[b * 16 + r], 1), :]
        return carry

    lax.fori_loop(0, 16, some, 0)
    for s in range(8):
        out_ref = up_ref if s // 4 else down_ref
        out_ref[s // 2 % 2, s % 2] = picked[s * SLAB : (s + 1) * SLAB, :].astype(BF16)


def receive(gidx, mid, low, high):
    return pl.pallas_call(
        receive_kernel,
        out_shape=[
            jax.ShapeDtypeStruct((ROWS, W), BF16),
            jax.ShapeDtypeStruct((32, W), I32),
            jax.ShapeDtypeStruct((2, 2, SLAB, W), BF16),
            jax.ShapeDtypeStruct((2, 2, SLAB, W), BF16),
        ],
        in_specs=[smem()] + [vmem()] * 3,
        out_specs=[vmem()] * 4,
        scratch_shapes=[pltpu.VMEM((ROWS, W), F32), pltpu.VMEM((8 * SLAB, W), F32)],
        compiler_params=pltpu.CompilerParams(vmem_limit_bytes=VMEM_LIMIT),
        name="receive",
    )(gidx, mid, low, high)


def sort_pairs(count):
    pairs = []
    size = 1
    while size < count:
        size *= 2
    p = 1
    while p < size:
        k = p
        while k >= 1:
            for j in range(k % p, size - k, 2 * k):
                for i in range(min(k, size - j - k)):
                    if (i + j) // (2 * p) == (i + j + k) // (2 * p) and i + j + k < count:
                        pairs.append((i + j, i + j + k))
            k //= 2
        p *= 2
    return pairs


def fill_ghosts(pos_ref, around, ghosts):
    first = [pos_ref[i] == 0 for i in range(3)]
    final = [pos_ref[i] == n - 1 for i, n in enumerate(GRID)]
    for s, p in enumerate(OUTER):
        a, b, c = p // 16, p // 4 % 4, p % 4
        absent = None
        for i, at in enumerate((a, b, c)):
            if at in (0, 3):
                edge = first[i] if at == 0 else final[i]
                absent = edge if absent is None else absent | edge
        x_low, x_high, y_low, y_high, z_low, z_high = around
        if c in (0, 3):
            slab = (z_high if c else z_low)[a, b]
        elif b in (0, 3):
            slab = (y_high if b else y_low)[a, c - 1]
        else:
            slab = (x_high if a else x_low)[b - 1, c - 1]
        slab = jnp.where(absent, MARK, slab.astype(F32)).astype(BF16)
        ghosts[s * SLAB : (s + 1) * SLAB, :] = slab


def index_kernel(
    pos_ref,
    nbr_ref,
    valid_ref,
    cnt_ref,
    *refs,
):
    around, (idx_ref, steps_ref, dead_ref, ghosts, held) = refs[:AROUND], refs[AROUND:]
    fill_ghosts(pos_ref, around, ghosts)
    alive = jnp.where(ghosts[...].astype(F32) < MARK * 0.5, 1.0, 0.0).astype(BF16)
    at = iota((W, GHOSTS), 1)
    bit = jnp.left_shift(1, at & 15).astype(F32)
    spread = jnp.where(lax.shift_right_logical(at, 4) == iota((W, GHOSTS), 0), bit, 0.0)
    words = dot(spread.astype(BF16), alive)
    eye = iota((W, W), 0) == iota((W, W), 1)
    words = jnp.sum(jnp.where(eye, words, 0.0), axis=0, keepdims=True).astype(I32)
    words = jnp.broadcast_to(words, (8, W))
    counts = cnt_ref[...]
    diag = iota((32, W), 0) == iota((32, W), 1)
    by_code = jnp.sum(jnp.where(diag, counts.astype(F32), 0.0), axis=0, keepdims=True)
    by_code = jnp.broadcast_to(by_code.astype(I32), (8, W))

    held[...] = jnp.zeros_like(held) - 1
    for c in range(CODES):
        cols = slice(c * W, (c + 1) * W)
        held[c * DEG : (c + 1) * DEG, :] = jnp.where(valid_ref[:, cols] > 0, nbr_ref[:, cols], -1)

    for b in range(4):
        here = iota((8, W), 1) < counts[b * 8 : (b + 1) * 8, :]
        keys = []
        dead = jnp.zeros((8, W), F32)
        for k in range(DEG):
            node = held[pl.ds(b * 8 * DEG + k, 8, stride=DEG), :]
            far = jnp.maximum(node - ROWS, 0)
            word = jnp.take_along_axis(words, lax.shift_right_logical(far, 4), axis=1)
            flag = lax.shift_right_logical(word, far & 15) & 1
            near = jnp.minimum(jnp.maximum(node, 0), ROWS - 1)
            limit = jnp.take_along_axis(by_code, lax.shift_right_logical(near, 7), axis=1)
            lives = jnp.where(node >= ROWS, flag, jnp.where((near & (W - 1)) < limit, 1, 0))
            real = node >= 0
            key = jnp.where(here & real & (lives > 0), node, DUMMY)
            dead = dead + jnp.where(here & real & (lives == 0), 1.0, 0.0)
            keys.append(key.astype(F32))
        for i, j in sort_pairs(DEG):
            keys[i], keys[j] = jnp.minimum(keys[i], keys[j]), jnp.maximum(keys[i], keys[j])
        used = jnp.zeros((8, W), F32)
        for k in range(DEG):
            used = used + jnp.where(keys[k] < DUMMY, 1.0, 0.0)
            idx_ref[pl.ds(b * 8 * DEG + k, 8, stride=DEG), :] = keys[k].astype(I32)
        for shift in (1, 2, 4, 8):
            used = jnp.maximum(used, pltpu.roll(used, W - shift, 1))
        steps_ref[b * 8 : (b + 1) * 8, :] = used.astype(I32)
        dead_ref[b * 8 : (b + 1) * 8, :] = dead


def indices(pos, nbr, valid, cnt, around):
    return pl.pallas_call(
        index_kernel,
        out_shape=[
            jax.ShapeDtypeStruct((DEG * 32, W), I32),
            jax.ShapeDtypeStruct((32, W), I32),
            jax.ShapeDtypeStruct((32, W), F32),
        ],
        in_specs=[smem()] + [vmem()] * (3 + AROUND),
        out_specs=[vmem()] * 3,
        scratch_shapes=[pltpu.VMEM((GHOSTS, W), BF16), pltpu.VMEM((32 * DEG, W), I32)],
        compiler_params=pltpu.CompilerParams(vmem_limit_bytes=VMEM_LIMIT),
        name="indices",
    )(pos, nbr, valid, cnt, *around)


GROUP = 16
SPAN = 27
FIRST = 13
TAILS = (0, 1, 2, 3, 5, 7, 11)
DUMP = ROWS
PARTS = ((0, 3), (3, 11), (11, CODES))


def layer_kernel(
    idx_hbm,
    pos_ref,
    steps_ref,
    cnt_ref,
    gidx_ref,
    dead_ref,
    state_ref,
    *refs,
):
    around, refs = refs[:AROUND], refs[AROUND:]
    efirst_ref, esecond_ref, ethird_ref, nfirst_ref, nsecond_ref, nthird_ref = refs[:6]
    out_ref, down_ref, up_ref = refs[6:9]
    table, recv, ghosts, hidden, agg, full, picked, idx_ref, sems = refs[9:]
    copies = []
    for i, (lo, hi) in enumerate(PARTS):
        words = pl.ds(lo * DEG * W, (hi - lo) * DEG * W)
        copies.append(pltpu.make_async_copy(idx_hbm.at[words], idx_ref.at[words], sems.at[i]))
        copies[-1].start()
    w_recv = efirst_ref[0:W, :]
    w_send = efirst_ref[W : 2 * W, :]
    w_both = jnp.concatenate([w_recv, w_send], axis=1)
    fill_ghosts(pos_ref, around, ghosts)

    def own(i, carry):
        rows = pl.ds(pl.multiple_of(i * 1152, 1152), 1152)
        both = dot(state_ref[rows, :], w_both)
        recv[rows, :] = both[:, :W]
        table[rows, :] = both[:, W:]
        return carry

    lax.fori_loop(0, ROWS // 1152, own, 0)

    def far(i, carry):
        x = ghosts[pl.ds(pl.multiple_of(i * 896, 128), 896), :].astype(F32)
        x = jnp.where(x < MARK * 0.5, x, 0.0).astype(BF16)
        table[pl.ds(pl.multiple_of(ROWS + i * 896, 128), 896), :] = dot(x, w_send)
        return carry

    lax.fori_loop(0, GHOSTS // 896, far, 0)
    table[NODES : NODES + 8, :] = jnp.full((8, W), -MARK, F32)

    w_second = esecond_ref[...]
    sub = iota((8, W), 0)

    def finish(h, row):
        d = jnp.maximum(dot(h, w_second), 0.0).astype(BF16).astype(F32)
        agg[pl.ds(pl.multiple_of(row, GROUP), GROUP), :] = jnp.sum(
            d.reshape(DEG, GROUP, W), axis=0
        )

    def step(base, mine, k):
        both = []
        for half in range(2):
            got = None
            for r in range(8):
                at = idx_ref[base + (k * W + half * 8 + r)]
                row = jnp.broadcast_to(table[pl.ds(at, 1), :], (8, W))
                got = row if got is None else jnp.where(sub == r, row, got)
            both.append(jnp.maximum(got + mine[half], 0.0))
        hidden[k * GROUP : (k + 1) * GROUP, :] = jnp.concatenate(both, axis=0).astype(BF16)

    def sender(c, last):
        groups = lax.shift_right_logical(cnt_ref[c, 0] + (GROUP - 1), 4)
        for (lo, _), copy in zip(PARTS, copies):
            pl.when(c == lo)(copy.wait)

        def gather(g, last):
            q0 = pl.multiple_of(g * GROUP, GROUP)
            home = c * W + q0
            base = c * (DEG * W) + q0
            mine = [recv[pl.ds(pl.multiple_of(home + h * 8, 8), 8), :] for h in range(2)]
            finish(hidden[...], last)
            for k in range(FIRST):
                step(base, mine, k)
            more = steps_ref[c, q0] - FIRST
            which = sum((more > t).astype(I32) for t in TAILS[:-1])

            def tail(size):
                def run():
                    for k in range(FIRST, FIRST + size):
                        step(base, mine, k)
                    if FIRST + size < DEG:
                        hidden[(FIRST + size) * GROUP :, :] = jnp.zeros(
                            ((DEG - FIRST - size) * GROUP, W), BF16
                        )

                return run

            lax.switch(which, [tail(t) for t in TAILS])
            return home

        return lax.fori_loop(0, groups, gather, last)

    last = lax.fori_loop(0, CODES, sender, jnp.int32(DUMP))
    finish(hidden[...], last)

    w_third = ethird_ref[...]
    n_state = nfirst_ref[0:W, :]
    n_agg = nfirst_ref[W : 2 * W, :]
    n_second = nsecond_ref[...]
    n_third = nthird_ref[...]
    eye = iota((W, W), 0) == iota((W, W), 1)
    ones = jnp.ones((W, W), BF16)

    def node(i, carry):
        rows = pl.ds(pl.multiple_of(i * (SPAN * W), SPAN * W), SPAN * W)
        live = jnp.concatenate(
            [iota((W, W), 0) < cnt_ref[i * SPAN + j, 0] for j in range(SPAN)], axis=0
        )
        times = jnp.concatenate(
            [
                jnp.where(eye, jnp.broadcast_to(dead_ref[pl.ds(i * SPAN + j, 1), :], (W, W)), 0.0)
                for j in range(SPAN)
            ],
            axis=0,
        )
        times = dot(times.astype(BF16), ones)
        alone = jnp.maximum(recv[rows, :], 0.0).astype(BF16)
        alone = jnp.maximum(dot(alone, w_second), 0.0).astype(BF16).astype(F32)
        summed = jnp.where(live, agg[rows, :] + times * alone, 0.0)
        top = summed.astype(BF16)
        rest = (summed - top.astype(F32)).astype(BF16)
        total = (dot(top, w_third) + dot(rest, w_third)).astype(BF16)
        state = state_ref[rows, :]
        h = jnp.maximum(dot(state, n_state) + dot(total, n_agg), 0.0).astype(BF16)
        h = jnp.maximum(dot(h, n_second), 0.0).astype(BF16)
        update = dot(h, n_third)
        mean = jnp.mean(update, axis=1, keepdims=True)
        centred = update - mean
        var = jnp.mean(centred * centred, axis=1, keepdims=True)
        new = state.astype(F32) + centred * lax.rsqrt(var + 1e-05)
        full[rows, :] = jnp.where(live, new, MARK)
        out_ref[rows, :] = jnp.where(live, new, 0.0).astype(BF16)
        return carry

    lax.fori_loop(0, ROWS // (SPAN * W), node, 0)
    pick_slabs(gidx_ref, full, picked, down_ref, up_ref)


def one_layer(idx, pos, steps, cnt, gidx, dead, state, around, weights):
    return pl.pallas_call(
        layer_kernel,
        out_shape=[
            jax.ShapeDtypeStruct((ROWS, W), BF16),
            jax.ShapeDtypeStruct((2, 2, SLAB, W), BF16),
            jax.ShapeDtypeStruct((2, 2, SLAB, W), BF16),
        ],
        in_specs=[pl.BlockSpec(memory_space=pl.ANY)] + [smem()] * 4 + [vmem()] * (8 + AROUND),
        out_specs=[vmem()] * 3,
        scratch_shapes=[
            pltpu.VMEM((NODES + 8, W), F32),
            pltpu.VMEM((ROWS, W), F32),
            pltpu.VMEM((GHOSTS, W), BF16),
            pltpu.VMEM((DEG * GROUP, W), BF16),
            pltpu.VMEM((ROWS + GROUP, W), F32),
            pltpu.VMEM((ROWS, W), F32),
            pltpu.VMEM((8 * SLAB, W), F32),
            pltpu.SMEM((ROWS * DEG,), I32),
            pltpu.SemaphoreType.DMA((len(PARTS),)),
        ],
        compiler_params=pltpu.CompilerParams(vmem_limit_bytes=VMEM_LIMIT),
        name="layer",
    )(idx, pos, steps, cnt, gidx, dead, state, *around, *weights)


def both_ways(up, down, axis):
    n = lax.axis_size(axis)
    forward = [(i, (i + 1) % n) for i in range(n)]
    backward = [(b, a) for a, b in forward]
    return lax.ppermute(up, axis, forward), lax.ppermute(down, axis, backward)


def migrate(down, mid, up):
    low, high = both_ways(up, down, "gx")
    buffer = jnp.stack([low, mid, high])
    low, high = both_ways(buffer[:, 2], buffer[:, 0], "gy")
    buffer = jnp.stack([low, buffer[:, 1], high], axis=1)
    low, high = both_ways(buffer[:, :, 2], buffer[:, :, 0], "gz")
    return buffer[:, :, 1], low, high


def surround(down, up):
    x_low, x_high = both_ways(up, down, "gx")
    rows = (x_low, down, up, x_high)
    y_low, y_high = both_ways(
        jnp.stack([r[1] for r in rows]), jnp.stack([r[0] for r in rows]), "gy"
    )

    def face(c):
        return jnp.stack(
            [jnp.stack([y_low[a, c], r[0, c], r[1, c], y_high[a, c]]) for a, r in enumerate(rows)]
        )

    z_low, z_high = both_ways(face(1), face(0), "gz")
    return x_low, x_high, y_low, y_high, z_low, z_high


def body(
    latent,
    destination,
    neighbours,
    valid,
    ghost_index,
    edge_first,
    edge_second,
    edge_third,
    node_first,
    node_second,
    node_third,
):
    dest = destination.reshape(1, 1024)
    nbr = neighbours[0, 0, 0].T
    mask = valid[0, 0, 0].T
    gidx = ghost_index.reshape(-1)
    pos = jnp.stack([lax.axis_index(a) for a in HALO_AXES]).astype(I32)
    state, cnt, down, up = receive(gidx, *migrate(*pack(dest, latent[0, 0, 0])))
    for layer in range(edge_first.shape[0]):
        weights = [
            w[layer]
            for w in (edge_first, edge_second, edge_third, node_first, node_second, node_third)
        ]
        around = surround(down, up)
        if layer == 0:
            idx, steps, dead = indices(pos, nbr, mask, cnt, around)
            idx = idx.reshape(-1)
        state, down, up = one_layer(idx, pos, steps, cnt, gidx, dead, state, around, weights)
    return state.reshape(1, 1, 1, ROWS, W)


def solution(mesh):
    spread = P("gx", "gy", "gz", None, None)
    return jax.shard_map(
        body,
        mesh=mesh,
        in_specs=(spread,) * 5 + (P(),) * 6,
        out_specs=spread,
        check_vma=False,
    )
```

```python
import jax
import jax.numpy as jnp
import numpy as np
from jax import lax
from jax.experimental import pallas as pl
from jax.experimental.pallas import tpu as pltpu
from jax.sharding import PartitionSpec as P

F32 = jnp.float32
BF16 = jnp.bfloat16
I32 = jnp.int32
W = 128
CODES = 27
ROWS = CODES * W
DEG = 24
SLAB = 32
OUTER = [
    p for p in range(64) if p // 16 in (0, 3) or p // 4 % 4 in (0, 3) or p % 4 in (0, 3)
]
AROUND = 6
GHOSTS = len(OUTER) * SLAB
NODES = ROWS + GHOSTS
DUMMY = NODES
MARK = 2.0**100
HALO_AXES = ("gx", "gy", "gz")
GRID = (4, 4, 8)
VMEM_LIMIT = 24 * 2**20


def dot(a, b):
    return jnp.dot(a, b, preferred_element_type=F32)


def vmem():
    return pl.BlockSpec(memory_space=pltpu.VMEM)


def smem():
    return pl.BlockSpec(memory_space=pltpu.SMEM)


def iota(shape, dim):
    return lax.broadcasted_iota(I32, shape, dim)


def pack_kernel(dest_ref, rows_ref, down_ref, mid_ref, up_ref, slot_ref):
    n_y, n_z = 4, 8
    ix, iy, iz = (lax.axis_index(a) for a in HALO_AXES)
    tri = (iota((W, W), 0) < iota((W, W), 1)).astype(BF16)
    ones = jnp.ones((W, W), BF16)
    off = jnp.zeros((32, W), F32)
    for j in range(8):
        d = dest_ref[:, j * W : (j + 1) * W]
        code = (
            (lax.shift_right_logical(d, 5) - ix + 1) * 9
            + ((lax.shift_right_logical(d, 3) & (n_y - 1)) - iy + 1) * 3
            + ((d & (n_z - 1)) - iz + 1)
        )
        hit = iota((32, W), 0) == code
        one = jnp.where(hit, 1.0, 0.0).astype(BF16)
        before = dot(one, tri) + off
        rank = jnp.sum(jnp.where(hit, before, 0.0), axis=0, keepdims=True)
        slot_ref[:, j * W : (j + 1) * W] = code * W + rank.astype(I32)
        off = off + dot(one, ones)
    slot = slot_ref[...]
    rows = rows_ref[...]
    for part, out_ref in enumerate((down_ref, mid_ref, up_ref)):
        first = part * 9 * W
        chosen = jnp.where(slot == iota((9 * W, 1024), 0) + first, 1.0, 0.0).astype(BF16)
        got = dot(chosen, rows)
        for c in range(9):
            alive = iota((W, W), 0).astype(F32) < off[part * 9 + c : part * 9 + c + 1, :]
            block = jnp.where(alive, got[c * W : (c + 1) * W, :], MARK)
            out_ref[c // 3, c % 3] = block.astype(BF16)


def pack(dest, rows):
    return pl.pallas_call(
        pack_kernel,
        out_shape=[jax.ShapeDtypeStruct((3, 3, W, W), BF16)] * 3,
        in_specs=[vmem(), vmem()],
        out_specs=[vmem()] * 3,
        scratch_shapes=[pltpu.VMEM((1, 1024), I32)],
        compiler_params=pltpu.CompilerParams(vmem_limit_bytes=VMEM_LIMIT),
        name="pack",
    )(dest, rows)


def receive_kernel(
    gidx_ref, mid_ref, low_ref, high_ref, state_ref, cnt_ref, down_ref, up_ref, full, picked
):
    pos = [lax.axis_index(a) for a in HALO_AXES]
    cnt_ref[...] = jnp.zeros_like(cnt_ref)
    for c in range(CODES):
        offs = (c // 9 - 1, c // 3 % 3 - 1, c % 3 - 1)
        inside = jnp.int32(1)
        for p, o, s in zip(pos, offs, GRID):
            if o < 0:
                inside = inside * (p > 0).astype(I32)
            if o > 0:
                inside = inside * (p < s - 1).astype(I32)
        if c % 3 == 1:
            x = mid_ref[c // 9, c // 3 % 3].astype(F32)
        else:
            x = (low_ref if c % 3 == 0 else high_ref)[c // 9, c // 3 % 3].astype(F32)
        alive = x < MARK * 0.5
        count = jnp.sum(jnp.where(alive, 1.0, 0.0), axis=0, keepdims=True).astype(I32)
        cnt_ref[c : c + 1, :] = count * inside
        present = iota((W, W), 0) < count * inside
        full[c * W : (c + 1) * W, :] = jnp.where(present, x, MARK)
        state_ref[c * W : (c + 1) * W, :] = jnp.where(present, x, 0.0).astype(BF16)
    pick_slabs(gidx_ref, full, picked, down_ref, up_ref)


def pick_slabs(gidx_ref, full, picked, down_ref, up_ref):
    def some(b, carry):
        for r in range(16):
            picked[pl.ds(b * 16 + r, 1), :] = full[pl.ds(gidx_ref[b * 16 + r], 1), :]
        return carry

    lax.fori_loop(0, 16, some, 0)
    for s in range(8):
        out_ref = up_ref if s // 4 else down_ref
        out_ref[s // 2 % 2, s % 2] = picked[s * SLAB : (s + 1) * SLAB, :].astype(BF16)


def receive(gidx, mid, low, high):
    return pl.pallas_call(
        receive_kernel,
        out_shape=[
            jax.ShapeDtypeStruct((ROWS, W), BF16),
            jax.ShapeDtypeStruct((32, W), I32),
            jax.ShapeDtypeStruct((2, 2, SLAB, W), BF16),
            jax.ShapeDtypeStruct((2, 2, SLAB, W), BF16),
        ],
        in_specs=[smem()] + [vmem()] * 3,
        out_specs=[vmem()] * 4,
        scratch_shapes=[pltpu.VMEM((ROWS, W), F32), pltpu.VMEM((8 * SLAB, W), F32)],
        compiler_params=pltpu.CompilerParams(vmem_limit_bytes=VMEM_LIMIT),
        name="receive",
    )(gidx, mid, low, high)


def sort_pairs(count):
    pairs = []
    size = 1
    while size < count:
        size *= 2
    p = 1
    while p < size:
        k = p
        while k >= 1:
            for j in range(k % p, size - k, 2 * k):
                for i in range(min(k, size - j - k)):
                    if (i + j) // (2 * p) == (i + j + k) // (2 * p) and i + j + k < count:
                        pairs.append((i + j, i + j + k))
            k //= 2
        p *= 2
    return pairs


def fill_ghosts(pos_ref, around, ghosts):
    first = [pos_ref[i] == 0 for i in range(3)]
    final = [pos_ref[i] == n - 1 for i, n in enumerate(GRID)]
    for s, p in enumerate(OUTER):
        a, b, c = p // 16, p // 4 % 4, p % 4
        absent = None
        for i, at in enumerate((a, b, c)):
            if at in (0, 3):
                edge = first[i] if at == 0 else final[i]
                absent = edge if absent is None else absent | edge
        x_low, x_high, y_low, y_high, z_low, z_high = around
        if c in (0, 3):
            slab = (z_high if c else z_low)[a, b]
        elif b in (0, 3):
            slab = (y_high if b else y_low)[a, c - 1]
        else:
            slab = (x_high if a else x_low)[b - 1, c - 1]
        slab = jnp.where(absent, MARK, slab.astype(F32)).astype(BF16)
        ghosts[s * SLAB : (s + 1) * SLAB, :] = slab


def index_kernel(
    pos_ref,
    nbr_ref,
    valid_ref,
    cnt_ref,
    *refs,
):
    around, (idx_ref, steps_ref, dead_ref, ghosts, held) = refs[:AROUND], refs[AROUND:]
    fill_ghosts(pos_ref, around, ghosts)
    alive = jnp.where(ghosts[...].astype(F32) < MARK * 0.5, 1.0, 0.0).astype(BF16)
    at = iota((W, GHOSTS), 1)
    bit = jnp.left_shift(1, at & 15).astype(F32)
    spread = jnp.where(lax.shift_right_logical(at, 4) == iota((W, GHOSTS), 0), bit, 0.0)
    words = dot(spread.astype(BF16), alive)
    eye = iota((W, W), 0) == iota((W, W), 1)
    words = jnp.sum(jnp.where(eye, words, 0.0), axis=0, keepdims=True).astype(I32)
    words = jnp.broadcast_to(words, (8, W))
    counts = cnt_ref[...]
    diag = iota((32, W), 0) == iota((32, W), 1)
    by_code = jnp.sum(jnp.where(diag, counts.astype(F32), 0.0), axis=0, keepdims=True)
    by_code = jnp.broadcast_to(by_code.astype(I32), (8, W))

    held[...] = jnp.zeros_like(held) - 1
    for c in range(CODES):
        cols = slice(c * W, (c + 1) * W)
        held[c * DEG : (c + 1) * DEG, :] = jnp.where(valid_ref[:, cols] > 0, nbr_ref[:, cols], -1)

    for b in range(4):
        here = iota((8, W), 1) < counts[b * 8 : (b + 1) * 8, :]
        keys = []
        dead = jnp.zeros((8, W), F32)
        for k in range(DEG):
            node = held[pl.ds(b * 8 * DEG + k, 8, stride=DEG), :]
            far = jnp.maximum(node - ROWS, 0)
            word = jnp.take_along_axis(words, lax.shift_right_logical(far, 4), axis=1)
            flag = lax.shift_right_logical(word, far & 15) & 1
            near = jnp.minimum(jnp.maximum(node, 0), ROWS - 1)
            limit = jnp.take_along_axis(by_code, lax.shift_right_logical(near, 7), axis=1)
            lives = jnp.where(node >= ROWS, flag, jnp.where((near & (W - 1)) < limit, 1, 0))
            real = node >= 0
            key = jnp.where(here & real & (lives > 0), node, DUMMY)
            dead = dead + jnp.where(here & real & (lives == 0), 1.0, 0.0)
            keys.append(key.astype(F32))
        for i, j in sort_pairs(DEG):
            keys[i], keys[j] = jnp.minimum(keys[i], keys[j]), jnp.maximum(keys[i], keys[j])
        used = jnp.zeros((8, W), F32)
        for k in range(DEG):
            used = used + jnp.where(keys[k] < DUMMY, 1.0, 0.0)
            idx_ref[pl.ds(b * 8 * DEG + k, 8, stride=DEG), :] = keys[k].astype(I32)
        for shift in (1, 2, 4, 8):
            used = jnp.maximum(used, pltpu.roll(used, W - shift, 1))
        steps_ref[b * 8 : (b + 1) * 8, :] = used.astype(I32)
        dead_ref[b * 8 : (b + 1) * 8, :] = dead


def indices(pos, nbr, valid, cnt, around):
    return pl.pallas_call(
        index_kernel,
        out_shape=[
            jax.ShapeDtypeStruct((DEG * 32, W), I32),
            jax.ShapeDtypeStruct((32, W), I32),
            jax.ShapeDtypeStruct((32, W), F32),
        ],
        in_specs=[smem()] + [vmem()] * (3 + AROUND),
        out_specs=[vmem()] * 3,
        scratch_shapes=[pltpu.VMEM((GHOSTS, W), BF16), pltpu.VMEM((32 * DEG, W), I32)],
        compiler_params=pltpu.CompilerParams(vmem_limit_bytes=VMEM_LIMIT),
        name="indices",
    )(pos, nbr, valid, cnt, *around)


GROUP = 16
SPAN = 27
FIRST = 13
TAILS = (0, 1, 2, 3, 5, 7, 11)
DUMP = ROWS
PARTS = ((0, 3), (3, 11), (11, CODES))


def layer_kernel(
    idx_hbm,
    pos_ref,
    steps_ref,
    cnt_ref,
    gidx_ref,
    dead_ref,
    state_ref,
    *refs,
):
    around, refs = refs[:AROUND], refs[AROUND:]
    efirst_ref, esecond_ref, ethird_ref, nfirst_ref, nsecond_ref, nthird_ref = refs[:6]
    out_ref, down_ref, up_ref = refs[6:9]
    table, recv, ghosts, hidden, agg, full, picked, idx_ref, sems = refs[9:]
    copies = []
    for i, (lo, hi) in enumerate(PARTS):
        words = pl.ds(lo * DEG * W, (hi - lo) * DEG * W)
        copies.append(pltpu.make_async_copy(idx_hbm.at[words], idx_ref.at[words], sems.at[i]))
        copies[-1].start()
    w_recv = efirst_ref[0:W, :]
    w_send = efirst_ref[W : 2 * W, :]
    w_both = jnp.concatenate([w_recv, w_send], axis=1)
    fill_ghosts(pos_ref, around, ghosts)

    def own(i, carry):
        rows = pl.ds(pl.multiple_of(i * 1152, 1152), 1152)
        both = dot(state_ref[rows, :], w_both)
        recv[rows, :] = both[:, :W]
        table[rows, :] = both[:, W:]
        return carry

    lax.fori_loop(0, ROWS // 1152, own, 0)

    def far(i, carry):
        x = ghosts[pl.ds(pl.multiple_of(i * 896, 128), 896), :].astype(F32)
        x = jnp.where(x < MARK * 0.5, x, 0.0).astype(BF16)
        table[pl.ds(pl.multiple_of(ROWS + i * 896, 128), 896), :] = dot(x, w_send)
        return carry

    lax.fori_loop(0, GHOSTS // 896, far, 0)
    table[NODES : NODES + 8, :] = jnp.full((8, W), -MARK, F32)

    w_second = esecond_ref[...]
    sub = iota((8, W), 0)

    def finish(h, row):
        d = jnp.maximum(dot(h, w_second), 0.0).astype(BF16).astype(F32)
        agg[pl.ds(pl.multiple_of(row, GROUP), GROUP), :] = jnp.sum(
            d.reshape(DEG, GROUP, W), axis=0
        )

    def step(base, mine, k):
        both = []
        for half in range(2):
            got = None
            for r in range(8):
                at = idx_ref[base + (k * W + half * 8 + r)]
                row = jnp.broadcast_to(table[pl.ds(at, 1), :], (8, W))
                got = row if got is None else jnp.where(sub == r, row, got)
            both.append(jnp.maximum(got + mine[half], 0.0))
        hidden[k * GROUP : (k + 1) * GROUP, :] = jnp.concatenate(both, axis=0).astype(BF16)

    def sender(c, last):
        groups = lax.shift_right_logical(cnt_ref[c, 0] + (GROUP - 1), 4)
        for (lo, _), copy in zip(PARTS, copies):
            pl.when(c == lo)(copy.wait)

        def gather(g, last):
            q0 = pl.multiple_of(g * GROUP, GROUP)
            home = c * W + q0
            base = c * (DEG * W) + q0
            mine = [recv[pl.ds(pl.multiple_of(home + h * 8, 8), 8), :] for h in range(2)]
            finish(hidden[...], last)
            for k in range(FIRST):
                step(base, mine, k)
            more = steps_ref[c, q0] - FIRST
            which = sum((more > t).astype(I32) for t in TAILS[:-1])

            def tail(size):
                def run():
                    for k in range(FIRST, FIRST + size):
                        step(base, mine, k)
                    if FIRST + size < DEG:
                        hidden[(FIRST + size) * GROUP :, :] = jnp.zeros(
                            ((DEG - FIRST - size) * GROUP, W), BF16
                        )

                return run

            lax.switch(which, [tail(t) for t in TAILS])
            return home

        return lax.fori_loop(0, groups, gather, last)

    last = lax.fori_loop(0, CODES, sender, jnp.int32(DUMP))
    finish(hidden[...], last)

    w_third = ethird_ref[...]
    n_state = nfirst_ref[0:W, :]
    n_agg = nfirst_ref[W : 2 * W, :]
    n_second = nsecond_ref[...]
    n_third = nthird_ref[...]
    eye = iota((W, W), 0) == iota((W, W), 1)
    ones = jnp.ones((W, W), BF16)

    def node(i, carry):
        rows = pl.ds(pl.multiple_of(i * (SPAN * W), SPAN * W), SPAN * W)
        live = jnp.concatenate(
            [iota((W, W), 0) < cnt_ref[i * SPAN + j, 0] for j in range(SPAN)], axis=0
        )
        times = jnp.concatenate(
            [
                jnp.where(eye, jnp.broadcast_to(dead_ref[pl.ds(i * SPAN + j, 1), :], (W, W)), 0.0)
                for j in range(SPAN)
            ],
            axis=0,
        )
        times = dot(times.astype(BF16), ones)
        alone = jnp.maximum(recv[rows, :], 0.0).astype(BF16)
        alone = jnp.maximum(dot(alone, w_second), 0.0).astype(BF16).astype(F32)
        summed = jnp.where(live, agg[rows, :] + times * alone, 0.0)
        top = summed.astype(BF16)
        rest = (summed - top.astype(F32)).astype(BF16)
        total = (dot(top, w_third) + dot(rest, w_third)).astype(BF16)
        state = state_ref[rows, :]
        h = jnp.maximum(dot(state, n_state) + dot(total, n_agg), 0.0).astype(BF16)
        h = jnp.maximum(dot(h, n_second), 0.0).astype(BF16)
        update = dot(h, n_third)
        mean = jnp.mean(update, axis=1, keepdims=True)
        centred = update - mean
        var = jnp.mean(centred * centred, axis=1, keepdims=True)
        new = state.astype(F32) + centred * lax.rsqrt(var + 1e-05)
        full[rows, :] = jnp.where(live, new, MARK)
        out_ref[rows, :] = jnp.where(live, new, 0.0).astype(BF16)
        return carry

    lax.fori_loop(0, ROWS // (SPAN * W), node, 0)
    pick_slabs(gidx_ref, full, picked, down_ref, up_ref)


def one_layer(idx, pos, steps, cnt, gidx, dead, state, around, weights):
    return pl.pallas_call(
        layer_kernel,
        out_shape=[
            jax.ShapeDtypeStruct((ROWS, W), BF16),
            jax.ShapeDtypeStruct((2, 2, SLAB, W), BF16),
            jax.ShapeDtypeStruct((2, 2, SLAB, W), BF16),
        ],
        in_specs=[pl.BlockSpec(memory_space=pl.ANY)] + [smem()] * 4 + [vmem()] * (8 + AROUND),
        out_specs=[vmem()] * 3,
        scratch_shapes=[
            pltpu.VMEM((NODES + 8, W), F32),
            pltpu.VMEM((ROWS, W), F32),
            pltpu.VMEM((GHOSTS, W), BF16),
            pltpu.VMEM((DEG * GROUP, W), BF16),
            pltpu.VMEM((ROWS + GROUP, W), F32),
            pltpu.VMEM((ROWS, W), F32),
            pltpu.VMEM((8 * SLAB, W), F32),
            pltpu.SMEM((ROWS * DEG,), I32),
            pltpu.SemaphoreType.DMA((len(PARTS),)),
        ],
        compiler_params=pltpu.CompilerParams(vmem_limit_bytes=VMEM_LIMIT),
        name="layer",
    )(idx, pos, steps, cnt, gidx, dead, state, *around, *weights)


def both_ways(up, down, axis):
    n = lax.axis_size(axis)
    forward = [(i, (i + 1) % n) for i in range(n)]
    backward = [(b, a) for a, b in forward]
    return lax.ppermute(up, axis, forward), lax.ppermute(down, axis, backward)


def migrate(down, mid, up):
    low, high = both_ways(up, down, "gx")
    buffer = jnp.stack([low, mid, high])
    low, high = both_ways(buffer[:, 2], buffer[:, 0], "gy")
    buffer = jnp.stack([low, buffer[:, 1], high], axis=1)
    low, high = both_ways(buffer[:, :, 2], buffer[:, :, 0], "gz")
    return buffer[:, :, 1], low, high


def surround(down, up):
    x_low, x_high = both_ways(up, down, "gx")
    rows = (x_low, down, up, x_high)
    y_low, y_high = both_ways(
        jnp.stack([r[1] for r in rows]), jnp.stack([r[0] for r in rows]), "gy"
    )

    def face(c):
        return jnp.stack(
            [jnp.stack([y_low[a, c], r[0, c], r[1, c], y_high[a, c]]) for a, r in enumerate(rows)]
        )

    z_low, z_high = both_ways(face(1), face(0), "gz")
    return x_low, x_high, y_low, y_high, z_low, z_high


def body(
    latent,
    destination,
    neighbours,
    valid,
    ghost_index,
    edge_first,
    edge_second,
    edge_third,
    node_first,
    node_second,
    node_third,
):
    dest = destination.reshape(1, 1024)
    nbr = neighbours[0, 0, 0].T
    mask = valid[0, 0, 0].T
    gidx = ghost_index.reshape(-1)
    pos = jnp.stack([lax.axis_index(a) for a in HALO_AXES]).astype(I32)
    state, cnt, down, up = receive(gidx, *migrate(*pack(dest, latent[0, 0, 0])))
    for layer in range(edge_first.shape[0]):
        weights = [
            w[layer]
            for w in (edge_first, edge_second, edge_third, node_first, node_second, node_third)
        ]
        around = surround(down, up)
        if layer == 0:
            idx, steps, dead = indices(pos, nbr, mask, cnt, around)
            idx = idx.reshape(-1)
        state, down, up = one_layer(idx, pos, steps, cnt, gidx, dead, state, around, weights)
    return state.reshape(1, 1, 1, ROWS, W)


def solution(mesh):
    spread = P("gx", "gy", "gz", None, None)
    return jax.shard_map(
        body,
        mesh=mesh,
        in_specs=(spread,) * 5 + (P(),) * 6,
        out_specs=spread,
        check_vma=False,
    )
```

```python
import jax
import jax.numpy as jnp
import numpy as np
from jax import lax
from jax.experimental import pallas as pl
from jax.experimental.pallas import tpu as pltpu
from jax.sharding import PartitionSpec as P

F32 = jnp.float32
BF16 = jnp.bfloat16
I32 = jnp.int32
W = 128
CODES = 27
ROWS = CODES * W
DEG = 24
PAIRS = DEG // 2
SLAB = 32
OUTER = [
    p for p in range(64) if p // 16 in (0, 3) or p // 4 % 4 in (0, 3) or p % 4 in (0, 3)
]
AROUND = 6
GHOSTS = len(OUTER) * SLAB
NODES = ROWS + GHOSTS
DUMMY = NODES
MARK = 2.0**100
HALO_AXES = ("gx", "gy", "gz")
GRID = (4, 4, 8)
VMEM_LIMIT = 24 * 2**20


def dot(a, b):
    return jnp.dot(a, b, preferred_element_type=F32)


def vmem():
    return pl.BlockSpec(memory_space=pltpu.VMEM)


def smem():
    return pl.BlockSpec(memory_space=pltpu.SMEM)


def iota(shape, dim):
    return lax.broadcasted_iota(I32, shape, dim)


def pack_kernel(dest_ref, rows_ref, down_ref, mid_ref, up_ref, slot_ref):
    n_y, n_z = 4, 8
    ix, iy, iz = (lax.axis_index(a) for a in HALO_AXES)
    tri = (iota((W, W), 0) < iota((W, W), 1)).astype(BF16)
    ones = jnp.ones((W, W), BF16)
    off = jnp.zeros((32, W), F32)
    for j in range(8):
        d = dest_ref[:, j * W : (j + 1) * W]
        code = (
            (lax.shift_right_logical(d, 5) - ix + 1) * 9
            + ((lax.shift_right_logical(d, 3) & (n_y - 1)) - iy + 1) * 3
            + ((d & (n_z - 1)) - iz + 1)
        )
        hit = iota((32, W), 0) == code
        one = jnp.where(hit, 1.0, 0.0).astype(BF16)
        before = dot(one, tri) + off
        rank = jnp.sum(jnp.where(hit, before, 0.0), axis=0, keepdims=True)
        slot_ref[:, j * W : (j + 1) * W] = code * W + rank.astype(I32)
        off = off + dot(one, ones)
    slot = slot_ref[...]
    rows = rows_ref[...]
    for part, out_ref in enumerate((down_ref, mid_ref, up_ref)):
        first = part * 9 * W
        chosen = jnp.where(slot == iota((9 * W, 1024), 0) + first, 1.0, 0.0).astype(BF16)
        got = dot(chosen, rows)
        for c in range(9):
            alive = iota((W, W), 0).astype(F32) < off[part * 9 + c : part * 9 + c + 1, :]
            block = jnp.where(alive, got[c * W : (c + 1) * W, :], MARK)
            out_ref[c // 3, c % 3] = block.astype(BF16)


def pack(dest, rows):
    return pl.pallas_call(
        pack_kernel,
        out_shape=[jax.ShapeDtypeStruct((3, 3, W, W), BF16)] * 3,
        in_specs=[vmem(), vmem()],
        out_specs=[vmem()] * 3,
        scratch_shapes=[pltpu.VMEM((1, 1024), I32)],
        compiler_params=pltpu.CompilerParams(vmem_limit_bytes=VMEM_LIMIT),
        name="pack",
    )(dest, rows)


def receive_kernel(
    gidx_ref, mid_ref, low_ref, high_ref, state_ref, cnt_ref, down_ref, up_ref, full, picked
):
    pos = [lax.axis_index(a) for a in HALO_AXES]
    cnt_ref[...] = jnp.zeros_like(cnt_ref)
    for c in range(CODES):
        offs = (c // 9 - 1, c // 3 % 3 - 1, c % 3 - 1)
        inside = jnp.int32(1)
        for p, o, s in zip(pos, offs, GRID):
            if o < 0:
                inside = inside * (p > 0).astype(I32)
            if o > 0:
                inside = inside * (p < s - 1).astype(I32)
        if c % 3 == 1:
            x = mid_ref[c // 9, c // 3 % 3].astype(F32)
        else:
            x = (low_ref if c % 3 == 0 else high_ref)[c // 9, c // 3 % 3].astype(F32)
        alive = x < MARK * 0.5
        count = jnp.sum(jnp.where(alive, 1.0, 0.0), axis=0, keepdims=True).astype(I32)
        cnt_ref[c : c + 1, :] = count * inside
        present = iota((W, W), 0) < count * inside
        full[c * W : (c + 1) * W, :] = jnp.where(present, x, MARK)
        state_ref[c * W : (c + 1) * W, :] = jnp.where(present, x, 0.0).astype(BF16)
    pick_slabs(gidx_ref, full, picked, down_ref, up_ref)


def pick_slabs(gidx_ref, full, picked, down_ref, up_ref):
    def some(b, carry):
        for r in range(16):
            picked[pl.ds(b * 16 + r, 1), :] = full[pl.ds(gidx_ref[b * 16 + r], 1), :]
        return carry

    lax.fori_loop(0, 16, some, 0)
    for s in range(8):
        out_ref = up_ref if s // 4 else down_ref
        out_ref[s // 2 % 2, s % 2] = picked[s * SLAB : (s + 1) * SLAB, :].astype(BF16)


def receive(gidx, mid, low, high):
    return pl.pallas_call(
        receive_kernel,
        out_shape=[
            jax.ShapeDtypeStruct((ROWS, W), BF16),
            jax.ShapeDtypeStruct((32, W), I32),
            jax.ShapeDtypeStruct((2, 2, SLAB, W), BF16),
            jax.ShapeDtypeStruct((2, 2, SLAB, W), BF16),
        ],
        in_specs=[smem()] + [vmem()] * 3,
        out_specs=[vmem()] * 4,
        scratch_shapes=[pltpu.VMEM((ROWS, W), F32), pltpu.VMEM((8 * SLAB, W), F32)],
        compiler_params=pltpu.CompilerParams(vmem_limit_bytes=VMEM_LIMIT),
        name="receive",
    )(gidx, mid, low, high)


def sort_pairs(count):
    pairs = []
    size = 1
    while size < count:
        size *= 2
    p = 1
    while p < size:
        k = p
        while k >= 1:
            for j in range(k % p, size - k, 2 * k):
                for i in range(min(k, size - j - k)):
                    if (i + j) // (2 * p) == (i + j + k) // (2 * p) and i + j + k < count:
                        pairs.append((i + j, i + j + k))
            k //= 2
        p *= 2
    return pairs


def fill_ghosts(pos_ref, around, ghosts):
    first = [pos_ref[i] == 0 for i in range(3)]
    final = [pos_ref[i] == n - 1 for i, n in enumerate(GRID)]
    for s, p in enumerate(OUTER):
        a, b, c = p // 16, p // 4 % 4, p % 4
        absent = None
        for i, at in enumerate((a, b, c)):
            if at in (0, 3):
                edge = first[i] if at == 0 else final[i]
                absent = edge if absent is None else absent | edge
        x_low, x_high, y_low, y_high, z_low, z_high = around
        if c in (0, 3):
            slab = (z_high if c else z_low)[a, b]
        elif b in (0, 3):
            slab = (y_high if b else y_low)[a, c - 1]
        else:
            slab = (x_high if a else x_low)[b - 1, c - 1]
        slab = jnp.where(absent, MARK, slab.astype(F32)).astype(BF16)
        ghosts[s * SLAB : (s + 1) * SLAB, :] = slab


def index_kernel(
    pos_ref,
    nbr_ref,
    valid_ref,
    cnt_ref,
    *refs,
):
    around, (idx_ref, steps_ref, times_ref, ghosts, held) = refs[:AROUND], refs[AROUND:]
    fill_ghosts(pos_ref, around, ghosts)
    alive = jnp.where(ghosts[...].astype(F32) < MARK * 0.5, 1.0, 0.0).astype(BF16)
    at = iota((W, GHOSTS), 1)
    bit = jnp.left_shift(1, at & 15).astype(F32)
    spread = jnp.where(lax.shift_right_logical(at, 4) == iota((W, GHOSTS), 0), bit, 0.0)
    words = dot(spread.astype(BF16), alive)
    eye = iota((W, W), 0) == iota((W, W), 1)
    words = jnp.sum(jnp.where(eye, words, 0.0), axis=0, keepdims=True).astype(I32)
    words = jnp.broadcast_to(words, (8, W))
    counts = cnt_ref[...]
    diag = iota((32, W), 0) == iota((32, W), 1)
    by_code = jnp.sum(jnp.where(diag, counts.astype(F32), 0.0), axis=0, keepdims=True)
    by_code = jnp.broadcast_to(by_code.astype(I32), (8, W))

    held[...] = jnp.zeros_like(held) - 1
    for c in range(CODES):
        cols = slice(c * W, (c + 1) * W)
        held[c * DEG : (c + 1) * DEG, :] = jnp.where(valid_ref[:, cols] > 0, nbr_ref[:, cols], -1)

    for b in range(4):
        here = iota((8, W), 1) < counts[b * 8 : (b + 1) * 8, :]
        keys = []
        dead = jnp.zeros((8, W), F32)
        for k in range(DEG):
            node = held[pl.ds(b * 8 * DEG + k, 8, stride=DEG), :]
            far = jnp.maximum(node - ROWS, 0)
            word = jnp.take_along_axis(words, lax.shift_right_logical(far, 4), axis=1)
            flag = lax.shift_right_logical(word, far & 15) & 1
            near = jnp.minimum(jnp.maximum(node, 0), ROWS - 1)
            limit = jnp.take_along_axis(by_code, lax.shift_right_logical(near, 7), axis=1)
            lives = jnp.where(node >= ROWS, flag, jnp.where((near & (W - 1)) < limit, 1, 0))
            real = node >= 0
            key = jnp.where(here & real & (lives > 0), node, DUMMY)
            dead = dead + jnp.where(here & real & (lives == 0), 1.0, 0.0)
            keys.append(key.astype(F32))
        for i, j in sort_pairs(DEG):
            keys[i], keys[j] = jnp.minimum(keys[i], keys[j]), jnp.maximum(keys[i], keys[j])
        used = jnp.zeros((8, W), F32)
        for k in range(DEG):
            used = used + jnp.where(keys[k] < DUMMY, 1.0, 0.0)
        for j in range(PAIRS):
            word = keys[2 * j].astype(I32) + keys[2 * j + 1].astype(I32) * 65536
            idx_ref[pl.ds(b * 8 * PAIRS + j, 8, stride=PAIRS), :] = word
        for shift in (1, 2, 4, 8):
            used = jnp.maximum(used, pltpu.roll(used, W - shift, 1))
        steps_ref[b * 8 : (b + 1) * 8, :] = used.astype(I32)
        for c in range(b * 8, min(b * 8 + 8, CODES)):
            row = jnp.broadcast_to(dead[c - b * 8 : c - b * 8 + 1, :], (W, W))
            lone = jnp.where(eye, row, 0.0).astype(BF16)
            times_ref[c * W : (c + 1) * W, :] = dot(lone, jnp.ones((W, W), BF16)).astype(BF16)


def indices(pos, nbr, valid, cnt, around):
    return pl.pallas_call(
        index_kernel,
        out_shape=[
            jax.ShapeDtypeStruct((PAIRS * 32, W), I32),
            jax.ShapeDtypeStruct((32, W), I32),
            jax.ShapeDtypeStruct((ROWS, W), BF16),
        ],
        in_specs=[smem()] + [vmem()] * (3 + AROUND),
        out_specs=[vmem()] * 3,
        scratch_shapes=[pltpu.VMEM((GHOSTS, W), BF16), pltpu.VMEM((32 * DEG, W), I32)],
        compiler_params=pltpu.CompilerParams(vmem_limit_bytes=VMEM_LIMIT),
        name="indices",
    )(pos, nbr, valid, cnt, *around)


GROUP = 16
SPAN = 27
FIRST = 12
TAILS = (0, 2, 4, 6, 8, 12)
DUMP = ROWS
PARTS = ((0, 3), (3, 11), (11, CODES))


def project_kernel(state_ref, efirst_ref, table_ref, recv_ref):
    w_both = jnp.concatenate([efirst_ref[0:W, :], efirst_ref[W : 2 * W, :]], axis=1)

    def own(i, carry):
        rows = pl.ds(pl.multiple_of(i * 1152, 1152), 1152)
        both = dot(state_ref[rows, :], w_both)
        recv_ref[rows, :] = both[:, :W]
        table_ref[rows, :] = both[:, W:]
        return carry

    lax.fori_loop(0, ROWS // 1152, own, 0)
    table_ref[NODES : NODES + 8, :] = jnp.full((8, W), -MARK, F32)


def project(state, efirst):
    return pl.pallas_call(
        project_kernel,
        out_shape=[
            jax.ShapeDtypeStruct((NODES + 8, W), F32),
            jax.ShapeDtypeStruct((ROWS, W), F32),
        ],
        in_specs=[vmem()] * 2,
        out_specs=[vmem()] * 2,
        compiler_params=pltpu.CompilerParams(vmem_limit_bytes=VMEM_LIMIT),
        name="project",
    )(state, efirst)


def lone_kernel(state_ref, recv_ref, esecond_ref, nfirst_ref, alone_ref, first_ref):
    w_second = esecond_ref[...]
    n_state = nfirst_ref[0:W, :]

    def some(i, carry):
        rows = pl.ds(pl.multiple_of(i * 1152, 1152), 1152)
        alone = jnp.maximum(recv_ref[rows, :], 0.0).astype(BF16)
        alone_ref[rows, :] = jnp.maximum(dot(alone, w_second), 0.0).astype(BF16)
        first_ref[rows, :] = dot(state_ref[rows, :], n_state)
        return carry

    lax.fori_loop(0, ROWS // 1152, some, 0)


def lone(state, recv, esecond, nfirst):
    return pl.pallas_call(
        lone_kernel,
        out_shape=[
            jax.ShapeDtypeStruct((ROWS, W), BF16),
            jax.ShapeDtypeStruct((ROWS, W), F32),
        ],
        in_specs=[vmem()] * 4,
        out_specs=[vmem()] * 2,
        compiler_params=pltpu.CompilerParams(vmem_limit_bytes=VMEM_LIMIT),
        name="lone",
    )(state, recv, esecond, nfirst)


def layer_kernel(
    idx_hbm,
    pos_ref,
    steps_ref,
    cnt_ref,
    gidx_ref,
    table_in,
    recv,
    alone_ref,
    first_ref,
    times_ref,
    state_ref,
    *refs,
):
    around, refs = refs[:AROUND], refs[AROUND:]
    efirst_ref, esecond_ref, ethird_ref, nfirst_ref, nsecond_ref, nthird_ref = refs[:6]
    table, out_ref, down_ref, up_ref = refs[6:10]
    ghosts, hidden, agg, full, picked, idx_ref, sems = refs[10:]
    del table_in
    copies = []
    for i, (lo, hi) in enumerate(PARTS):
        words = pl.ds(lo * PAIRS * W, (hi - lo) * PAIRS * W)
        copies.append(pltpu.make_async_copy(idx_hbm.at[words], idx_ref.at[words], sems.at[i]))
        copies[-1].start()
    w_send = efirst_ref[W : 2 * W, :]
    fill_ghosts(pos_ref, around, ghosts)

    def far(i, carry):
        x = ghosts[pl.ds(pl.multiple_of(i * 896, 128), 896), :].astype(F32)
        x = jnp.where(x < MARK * 0.5, x, 0.0).astype(BF16)
        table[pl.ds(pl.multiple_of(ROWS + i * 896, 128), 896), :] = dot(x, w_send)
        return carry

    lax.fori_loop(0, GHOSTS // 896, far, 0)

    w_second = esecond_ref[...]
    sub = iota((8, W), 0)

    def finish(h, row):
        d = jnp.maximum(dot(h, w_second), 0.0).astype(BF16).astype(F32)
        agg[pl.ds(pl.multiple_of(row, GROUP), GROUP), :] = jnp.sum(
            d.reshape(DEG, GROUP, W), axis=0
        )

    def steps(base, mine, lo, hi):
        for j in range(lo // 2, (hi + 1) // 2):
            ks = [k for k in (2 * j, 2 * j + 1) if lo <= k < hi]
            got = {}
            for half in range(2):
                for r in range(8):
                    word = idx_ref[base + (j * W + half * 8 + r)]
                    for k in ks:
                        at = word & 65535 if k % 2 == 0 else lax.shift_right_logical(word, 16)
                        row = jnp.broadcast_to(table[pl.ds(at, 1), :], (8, W))
                        got[k, half] = row if r == 0 else jnp.where(sub == r, row, got[k, half])
            for k in ks:
                both = [jnp.maximum(got[k, half] + mine[half], 0.0) for half in range(2)]
                hidden[k * GROUP : (k + 1) * GROUP, :] = jnp.concatenate(both, axis=0).astype(BF16)

    def sender(c, last):
        groups = lax.shift_right_logical(cnt_ref[c, 0] + (GROUP - 1), 4)
        for (lo, _), copy in zip(PARTS, copies):
            pl.when(c == lo)(copy.wait)

        def gather(g, last):
            q0 = pl.multiple_of(g * GROUP, GROUP)
            home = c * W + q0
            base = c * (PAIRS * W) + q0
            mine = [recv[pl.ds(pl.multiple_of(home + h * 8, 8), 8), :] for h in range(2)]
            finish(hidden[...], last)
            steps(base, mine, 0, FIRST)
            more = steps_ref[c, q0] - FIRST
            which = sum((more > t).astype(I32) for t in TAILS[:-1])

            def tail(size):
                def run():
                    steps(base, mine, FIRST, FIRST + size)
                    if FIRST + size < DEG:
                        hidden[(FIRST + size) * GROUP :, :] = jnp.zeros(
                            ((DEG - FIRST - size) * GROUP, W), BF16
                        )

                return run

            lax.switch(which, [tail(t) for t in TAILS])
            return home

        return lax.fori_loop(0, groups, gather, last)

    last = lax.fori_loop(0, CODES, sender, jnp.int32(DUMP))
    finish(hidden[...], last)

    w_third = ethird_ref[...]
    n_agg = nfirst_ref[W : 2 * W, :]
    n_second = nsecond_ref[...]
    n_third = nthird_ref[...]

    def node(i, carry):
        rows = pl.ds(pl.multiple_of(i * (SPAN * W), SPAN * W), SPAN * W)
        live = jnp.concatenate(
            [iota((W, W), 0) < cnt_ref[i * SPAN + j, 0] for j in range(SPAN)], axis=0
        )
        lone_part = times_ref[rows, :].astype(F32) * alone_ref[rows, :].astype(F32)
        summed = jnp.where(live, agg[rows, :] + lone_part, 0.0)
        top = summed.astype(BF16)
        rest = (summed - top.astype(F32)).astype(BF16)
        total = (dot(top, w_third) + dot(rest, w_third)).astype(BF16)
        state = state_ref[rows, :]
        h = jnp.maximum(first_ref[rows, :] + dot(total, n_agg), 0.0).astype(BF16)
        h = jnp.maximum(dot(h, n_second), 0.0).astype(BF16)
        update = dot(h, n_third)
        mean = jnp.mean(update, axis=1, keepdims=True)
        centred = update - mean
        var = jnp.mean(centred * centred, axis=1, keepdims=True)
        new = state.astype(F32) + centred * lax.rsqrt(var + 1e-05)
        full[rows, :] = jnp.where(live, new, MARK)
        out_ref[rows, :] = jnp.where(live, new, 0.0).astype(BF16)
        return carry

    lax.fori_loop(0, ROWS // (SPAN * W), node, 0)
    pick_slabs(gidx_ref, full, picked, down_ref, up_ref)


def one_layer(idx, pos, steps, cnt, gidx, own, times, state, around, weights):
    return pl.pallas_call(
        layer_kernel,
        out_shape=[
            jax.ShapeDtypeStruct((NODES + 8, W), F32),
            jax.ShapeDtypeStruct((ROWS, W), BF16),
            jax.ShapeDtypeStruct((2, 2, SLAB, W), BF16),
            jax.ShapeDtypeStruct((2, 2, SLAB, W), BF16),
        ],
        in_specs=[pl.BlockSpec(memory_space=pl.ANY)] + [smem()] * 4 + [vmem()] * (12 + AROUND),
        out_specs=[vmem()] * 4,
        input_output_aliases={5: 0},
        scratch_shapes=[
            pltpu.VMEM((GHOSTS, W), BF16),
            pltpu.VMEM((DEG * GROUP, W), BF16),
            pltpu.VMEM((ROWS + GROUP, W), F32),
            pltpu.VMEM((ROWS, W), F32),
            pltpu.VMEM((8 * SLAB, W), F32),
            pltpu.SMEM((ROWS * PAIRS,), I32),
            pltpu.SemaphoreType.DMA((len(PARTS),)),
        ],
        compiler_params=pltpu.CompilerParams(vmem_limit_bytes=VMEM_LIMIT),
        name="layer",
    )(idx, pos, steps, cnt, gidx, *own, times, state, *around, *weights)[1:]


def both_ways(up, down, axis):
    n = lax.axis_size(axis)
    forward = [(i, (i + 1) % n) for i in range(n)]
    backward = [(b, a) for a, b in forward]
    return lax.ppermute(up, axis, forward), lax.ppermute(down, axis, backward)


def migrate(down, mid, up):
    low, high = both_ways(up, down, "gx")
    buffer = jnp.stack([low, mid, high])
    low, high = both_ways(buffer[:, 2], buffer[:, 0], "gy")
    buffer = jnp.stack([low, buffer[:, 1], high], axis=1)
    low, high = both_ways(buffer[:, :, 2], buffer[:, :, 0], "gz")
    return buffer[:, :, 1], low, high


def surround(down, up):
    x_low, x_high = both_ways(up, down, "gx")
    rows = (x_low, down, up, x_high)
    y_low, y_high = both_ways(
        jnp.stack([r[1] for r in rows]), jnp.stack([r[0] for r in rows]), "gy"
    )

    def face(c):
        return jnp.stack(
            [jnp.stack([y_low[a, c], r[0, c], r[1, c], y_high[a, c]]) for a, r in enumerate(rows)]
        )

    z_low, z_high = both_ways(face(1), face(0), "gz")
    return x_low, x_high, y_low, y_high, z_low, z_high


def body(
    latent,
    destination,
    neighbours,
    valid,
    ghost_index,
    edge_first,
    edge_second,
    edge_third,
    node_first,
    node_second,
    node_third,
):
    dest = destination.reshape(1, 1024)
    nbr = neighbours[0, 0, 0].T
    mask = valid[0, 0, 0].T
    gidx = ghost_index.reshape(-1)
    pos = jnp.stack([lax.axis_index(a) for a in HALO_AXES]).astype(I32)
    state, cnt, down, up = receive(gidx, *migrate(*pack(dest, latent[0, 0, 0])))
    for layer in range(edge_first.shape[0]):
        weights = [
            w[layer]
            for w in (edge_first, edge_second, edge_third, node_first, node_second, node_third)
        ]
        table, recv = project(state, weights[0])
        own = (table, recv, *lone(state, recv, weights[1], weights[3]))
        around = surround(down, up)
        if layer == 0:
            idx, steps, times = indices(pos, nbr, mask, cnt, around)
            idx = idx.reshape(-1)
        state, down, up = one_layer(
            idx, pos, steps, cnt, gidx, own, times, state, around, weights
        )
    return state.reshape(1, 1, 1, ROWS, W)


def solution(mesh):
    spread = P("gx", "gy", "gz", None, None)
    return jax.shard_map(
        body,
        mesh=mesh,
        in_specs=(spread,) * 5 + (P(),) * 6,
        out_specs=spread,
        check_vma=False,
    )
```

```python
import jax
import jax.numpy as jnp
import numpy as np
from jax import lax
from jax.experimental import pallas as pl
from jax.experimental.pallas import tpu as pltpu
from jax.sharding import PartitionSpec as P

F32 = jnp.float32
BF16 = jnp.bfloat16
I32 = jnp.int32
W = 128
CODES = 27
ROWS = CODES * W
DEG = 24
SLAB = 32
OUTER = [
    p for p in range(64) if p // 16 in (0, 3) or p // 4 % 4 in (0, 3) or p % 4 in (0, 3)
]
AROUND = 6
GHOSTS = len(OUTER) * SLAB
NODES = ROWS + GHOSTS
DUMMY = NODES
MARK = 2.0**100
HALO_AXES = ("gx", "gy", "gz")
GRID = (4, 4, 8)
VMEM_LIMIT = 24 * 2**20


def dot(a, b):
    return jnp.dot(a, b, preferred_element_type=F32)


def vmem():
    return pl.BlockSpec(memory_space=pltpu.VMEM)


def smem():
    return pl.BlockSpec(memory_space=pltpu.SMEM)


def iota(shape, dim):
    return lax.broadcasted_iota(I32, shape, dim)


def pack_kernel(dest_ref, rows_ref, down_ref, mid_ref, up_ref, slot_ref):
    n_y, n_z = 4, 8
    ix, iy, iz = (lax.axis_index(a) for a in HALO_AXES)
    tri = (iota((W, W), 0) < iota((W, W), 1)).astype(BF16)
    ones = jnp.ones((W, W), BF16)
    off = jnp.zeros((32, W), F32)
    for j in range(8):
        d = dest_ref[:, j * W : (j + 1) * W]
        code = (
            (lax.shift_right_logical(d, 5) - ix + 1) * 9
            + ((lax.shift_right_logical(d, 3) & (n_y - 1)) - iy + 1) * 3
            + ((d & (n_z - 1)) - iz + 1)
        )
        hit = iota((32, W), 0) == code
        one = jnp.where(hit, 1.0, 0.0).astype(BF16)
        before = dot(one, tri) + off
        rank = jnp.sum(jnp.where(hit, before, 0.0), axis=0, keepdims=True)
        slot_ref[:, j * W : (j + 1) * W] = code * W + rank.astype(I32)
        off = off + dot(one, ones)
    slot = slot_ref[...]
    rows = rows_ref[...]
    for part, out_ref in enumerate((down_ref, mid_ref, up_ref)):
        first = part * 9 * W
        chosen = jnp.where(slot == iota((9 * W, 1024), 0) + first, 1.0, 0.0).astype(BF16)
        got = dot(chosen, rows)
        for c in range(9):
            alive = iota((W, W), 0).astype(F32) < off[part * 9 + c : part * 9 + c + 1, :]
            block = jnp.where(alive, got[c * W : (c + 1) * W, :], MARK)
            out_ref[c // 3, c % 3] = block.astype(BF16)


def pack(dest, rows):
    return pl.pallas_call(
        pack_kernel,
        out_shape=[jax.ShapeDtypeStruct((3, 3, W, W), BF16)] * 3,
        in_specs=[vmem(), vmem()],
        out_specs=[vmem()] * 3,
        scratch_shapes=[pltpu.VMEM((1, 1024), I32)],
        compiler_params=pltpu.CompilerParams(vmem_limit_bytes=VMEM_LIMIT),
        name="pack",
    )(dest, rows)


def receive_kernel(
    gidx_ref, mid_ref, low_ref, high_ref, state_ref, cnt_ref, down_ref, up_ref, full, picked
):
    pos = [lax.axis_index(a) for a in HALO_AXES]
    cnt_ref[...] = jnp.zeros_like(cnt_ref)
    for c in range(CODES):
        offs = (c // 9 - 1, c // 3 % 3 - 1, c % 3 - 1)
        inside = jnp.int32(1)
        for p, o, s in zip(pos, offs, GRID):
            if o < 0:
                inside = inside * (p > 0).astype(I32)
            if o > 0:
                inside = inside * (p < s - 1).astype(I32)
        if c % 3 == 1:
            x = mid_ref[c // 9, c // 3 % 3].astype(F32)
        else:
            x = (low_ref if c % 3 == 0 else high_ref)[c // 9, c // 3 % 3].astype(F32)
        alive = x < MARK * 0.5
        count = jnp.sum(jnp.where(alive, 1.0, 0.0), axis=0, keepdims=True).astype(I32)
        cnt_ref[c : c + 1, :] = count * inside
        present = iota((W, W), 0) < count * inside
        full[c * W : (c + 1) * W, :] = jnp.where(present, x, MARK)
        state_ref[c * W : (c + 1) * W, :] = jnp.where(present, x, 0.0).astype(BF16)
    pick_slabs(gidx_ref, full, picked, down_ref, up_ref)


def pick_slabs(gidx_ref, full, picked, down_ref, up_ref):
    def some(b, carry):
        for r in range(16):
            picked[pl.ds(b * 16 + r, 1), :] = full[pl.ds(gidx_ref[b * 16 + r], 1), :]
        return carry

    lax.fori_loop(0, 16, some, 0)
    for s in range(8):
        out_ref = up_ref if s // 4 else down_ref
        out_ref[s // 2 % 2, s % 2] = picked[s * SLAB : (s + 1) * SLAB, :].astype(BF16)


def receive(gidx, mid, low, high):
    return pl.pallas_call(
        receive_kernel,
        out_shape=[
            jax.ShapeDtypeStruct((ROWS, W), BF16),
            jax.ShapeDtypeStruct((32, W), I32),
            jax.ShapeDtypeStruct((2, 2, SLAB, W), BF16),
            jax.ShapeDtypeStruct((2, 2, SLAB, W), BF16),
        ],
        in_specs=[smem()] + [vmem()] * 3,
        out_specs=[vmem()] * 4,
        scratch_shapes=[pltpu.VMEM((ROWS, W), F32), pltpu.VMEM((8 * SLAB, W), F32)],
        compiler_params=pltpu.CompilerParams(vmem_limit_bytes=VMEM_LIMIT),
        name="receive",
    )(gidx, mid, low, high)


def sort_pairs(count):
    pairs = []
    size = 1
    while size < count:
        size *= 2
    p = 1
    while p < size:
        k = p
        while k >= 1:
            for j in range(k % p, size - k, 2 * k):
                for i in range(min(k, size - j - k)):
                    if (i + j) // (2 * p) == (i + j + k) // (2 * p) and i + j + k < count:
                        pairs.append((i + j, i + j + k))
            k //= 2
        p *= 2
    return pairs


def fill_ghosts(pos_ref, around, ghosts):
    first = [pos_ref[i] == 0 for i in range(3)]
    final = [pos_ref[i] == n - 1 for i, n in enumerate(GRID)]
    for s, p in enumerate(OUTER):
        a, b, c = p // 16, p // 4 % 4, p % 4
        absent = None
        for i, at in enumerate((a, b, c)):
            if at in (0, 3):
                edge = first[i] if at == 0 else final[i]
                absent = edge if absent is None else absent | edge
        x_low, x_high, y_low, y_high, z_low, z_high = around
        if c in (0, 3):
            slab = (z_high if c else z_low)[a, b]
        elif b in (0, 3):
            slab = (y_high if b else y_low)[a, c - 1]
        else:
            slab = (x_high if a else x_low)[b - 1, c - 1]
        slab = jnp.where(absent, MARK, slab.astype(F32)).astype(BF16)
        ghosts[s * SLAB : (s + 1) * SLAB, :] = slab


def index_kernel(
    pos_ref,
    nbr_ref,
    valid_ref,
    cnt_ref,
    *refs,
):
    around, (idx_ref, steps_ref, times_ref, ghosts, held) = refs[:AROUND], refs[AROUND:]
    fill_ghosts(pos_ref, around, ghosts)
    alive = jnp.where(ghosts[...].astype(F32) < MARK * 0.5, 1.0, 0.0).astype(BF16)
    at = iota((W, GHOSTS), 1)
    bit = jnp.left_shift(1, at & 15).astype(F32)
    spread = jnp.where(lax.shift_right_logical(at, 4) == iota((W, GHOSTS), 0), bit, 0.0)
    words = dot(spread.astype(BF16), alive)
    eye = iota((W, W), 0) == iota((W, W), 1)
    words = jnp.sum(jnp.where(eye, words, 0.0), axis=0, keepdims=True).astype(I32)
    words = jnp.broadcast_to(words, (8, W))
    counts = cnt_ref[...]
    diag = iota((32, W), 0) == iota((32, W), 1)
    by_code = jnp.sum(jnp.where(diag, counts.astype(F32), 0.0), axis=0, keepdims=True)
    by_code = jnp.broadcast_to(by_code.astype(I32), (8, W))

    held[...] = jnp.zeros_like(held) - 1
    for c in range(CODES):
        cols = slice(c * W, (c + 1) * W)
        held[c * DEG : (c + 1) * DEG, :] = jnp.where(valid_ref[:, cols] > 0, nbr_ref[:, cols], -1)

    for b in range(4):
        here = iota((8, W), 1) < counts[b * 8 : (b + 1) * 8, :]
        keys = []
        dead = jnp.zeros((8, W), F32)
        for k in range(DEG):
            node = held[pl.ds(b * 8 * DEG + k, 8, stride=DEG), :]
            far = jnp.maximum(node - ROWS, 0)
            word = jnp.take_along_axis(words, lax.shift_right_logical(far, 4), axis=1)
            flag = lax.shift_right_logical(word, far & 15) & 1
            near = jnp.minimum(jnp.maximum(node, 0), ROWS - 1)
            limit = jnp.take_along_axis(by_code, lax.shift_right_logical(near, 7), axis=1)
            lives = jnp.where(node >= ROWS, flag, jnp.where((near & (W - 1)) < limit, 1, 0))
            real = node >= 0
            key = jnp.where(here & real & (lives > 0), node, DUMMY)
            dead = dead + jnp.where(here & real & (lives == 0), 1.0, 0.0)
            keys.append(key.astype(F32))
        for i, j in sort_pairs(DEG):
            keys[i], keys[j] = jnp.minimum(keys[i], keys[j]), jnp.maximum(keys[i], keys[j])
        used = jnp.zeros((8, W), F32)
        for k in range(DEG):
            used = used + jnp.where(keys[k] < DUMMY, 1.0, 0.0)
            idx_ref[pl.ds(b * 8 * DEG + k, 8, stride=DEG), :] = keys[k].astype(I32)
        for shift in (1, 2, 4, 8):
            used = jnp.maximum(used, pltpu.roll(used, W - shift, 1))
        steps_ref[b * 8 : (b + 1) * 8, :] = used.astype(I32)
        for c in range(b * 8, min(b * 8 + 8, CODES)):
            row = jnp.broadcast_to(dead[c - b * 8 : c - b * 8 + 1, :], (W, W))
            lone = jnp.where(eye, row, 0.0).astype(BF16)
            times_ref[c * W : (c + 1) * W, :] = dot(lone, jnp.ones((W, W), BF16)).astype(BF16)


def indices(pos, nbr, valid, cnt, around):
    return pl.pallas_call(
        index_kernel,
        out_shape=[
            jax.ShapeDtypeStruct((DEG * 32, W), I32),
            jax.ShapeDtypeStruct((32, W), I32),
            jax.ShapeDtypeStruct((ROWS, W), BF16),
        ],
        in_specs=[smem()] + [vmem()] * (3 + AROUND),
        out_specs=[vmem()] * 3,
        scratch_shapes=[pltpu.VMEM((GHOSTS, W), BF16), pltpu.VMEM((32 * DEG, W), I32)],
        compiler_params=pltpu.CompilerParams(vmem_limit_bytes=VMEM_LIMIT),
        name="indices",
    )(pos, nbr, valid, cnt, *around)


GROUP = 16
SPAN = 27
FIRST = 13
TAILS = (0, 1, 2, 3, 5, 7, 11)
DUMP = ROWS
PARTS = ((0, 3), (3, 11), (11, CODES))


def project_kernel(state_ref, efirst_ref, table_ref, recv_ref):
    w_both = jnp.concatenate([efirst_ref[0:W, :], efirst_ref[W : 2 * W, :]], axis=1)

    def own(i, carry):
        rows = pl.ds(pl.multiple_of(i * 1152, 1152), 1152)
        both = dot(state_ref[rows, :], w_both)
        recv_ref[rows, :] = both[:, :W]
        table_ref[rows, :] = both[:, W:]
        return carry

    lax.fori_loop(0, ROWS // 1152, own, 0)
    table_ref[NODES : NODES + 8, :] = jnp.full((8, W), -MARK, F32)


def project(state, efirst):
    return pl.pallas_call(
        project_kernel,
        out_shape=[
            jax.ShapeDtypeStruct((NODES + 8, W), F32),
            jax.ShapeDtypeStruct((ROWS, W), F32),
        ],
        in_specs=[vmem()] * 2,
        out_specs=[vmem()] * 2,
        compiler_params=pltpu.CompilerParams(vmem_limit_bytes=VMEM_LIMIT),
        name="project",
    )(state, efirst)


def lone_kernel(state_ref, recv_ref, esecond_ref, nfirst_ref, alone_ref, first_ref):
    w_second = esecond_ref[...]
    n_state = nfirst_ref[0:W, :]

    def some(i, carry):
        rows = pl.ds(pl.multiple_of(i * 1152, 1152), 1152)
        alone = jnp.maximum(recv_ref[rows, :], 0.0).astype(BF16)
        alone_ref[rows, :] = jnp.maximum(dot(alone, w_second), 0.0).astype(BF16)
        first_ref[rows, :] = dot(state_ref[rows, :], n_state)
        return carry

    lax.fori_loop(0, ROWS // 1152, some, 0)


def lone(state, recv, esecond, nfirst):
    return pl.pallas_call(
        lone_kernel,
        out_shape=[
            jax.ShapeDtypeStruct((ROWS, W), BF16),
            jax.ShapeDtypeStruct((ROWS, W), F32),
        ],
        in_specs=[vmem()] * 4,
        out_specs=[vmem()] * 2,
        compiler_params=pltpu.CompilerParams(vmem_limit_bytes=VMEM_LIMIT),
        name="lone",
    )(state, recv, esecond, nfirst)


def layer_kernel(
    idx_hbm,
    pos_ref,
    steps_ref,
    cnt_ref,
    gidx_ref,
    table_in,
    recv,
    alone_ref,
    first_ref,
    times_ref,
    state_ref,
    *refs,
):
    around, refs = refs[:AROUND], refs[AROUND:]
    efirst_ref, esecond_ref, ethird_ref, nfirst_ref, nsecond_ref, nthird_ref = refs[:6]
    table, out_ref, down_ref, up_ref = refs[6:10]
    ghosts, hidden, agg, full, picked, idx_ref, homes, sems = refs[10:]
    del table_in
    copies = []
    for i, (lo, hi) in enumerate(PARTS):
        words = pl.ds(lo * DEG * W, (hi - lo) * DEG * W)
        copies.append(pltpu.make_async_copy(idx_hbm.at[words], idx_ref.at[words], sems.at[i]))
        copies[-1].start()
    w_send = efirst_ref[W : 2 * W, :]
    fill_ghosts(pos_ref, around, ghosts)

    def far(i, carry):
        x = ghosts[pl.ds(pl.multiple_of(i * 896, 128), 896), :].astype(F32)
        x = jnp.where(x < MARK * 0.5, x, 0.0).astype(BF16)
        table[pl.ds(pl.multiple_of(ROWS + i * 896, 128), 896), :] = dot(x, w_send)
        return carry

    lax.fori_loop(0, GHOSTS // 896, far, 0)

    w_second = esecond_ref[...]
    sub = iota((8, W), 0)

    def listed(c, n):
        for g in range(W // GROUP):
            homes[n + g] = c * W + g * GROUP
        return n + lax.shift_right_logical(cnt_ref[c, 0] + (GROUP - 1), 4)

    starts = [jnp.int32(0)]
    for lo, hi in PARTS:
        starts.append(lax.fori_loop(lo, hi, listed, starts[-1]))
    total = starts[-1]
    homes[total] = homes[jnp.maximum(total - 1, 0)]
    rounds = lax.shift_right_logical(total + 1, 1)
    turns = [jnp.minimum(lax.shift_right_logical(n, 1), rounds) for n in starts[:-1]]

    def finish(h, rows):
        d = jnp.maximum(dot(h, w_second), 0.0).astype(BF16).astype(F32)
        d = jnp.sum(d.reshape(2, DEG, GROUP, W), axis=1)
        for slot, row in enumerate(rows):
            agg[pl.ds(pl.multiple_of(row, GROUP), GROUP), :] = d[slot]

    def step(slot, base, mine, k):
        both = []
        for half in range(2):
            got = None
            for r in range(8):
                at = idx_ref[base + (k * W + half * 8 + r)]
                row = jnp.broadcast_to(table[pl.ds(at, 1), :], (8, W))
                got = row if got is None else jnp.where(sub == r, row, got)
            both.append(jnp.maximum(got + mine[half], 0.0))
        at = (slot * DEG + k) * GROUP
        hidden[at : at + GROUP, :] = jnp.concatenate(both, axis=0).astype(BF16)

    def gather(i, last):
        for turn, copy in zip(turns, copies):
            pl.when(i == turn)(copy.wait)
        rows = [pl.multiple_of(homes[2 * i + slot], GROUP) for slot in range(2)]
        codes = [lax.shift_right_logical(row, 7) for row in rows]
        bases = [row + code * ((DEG - 1) * W) for row, code in zip(rows, codes)]
        mines = [
            [recv[pl.ds(pl.multiple_of(row + h * 8, 8), 8), :] for h in range(2)] for row in rows
        ]
        finish(hidden[...], last)
        for slot in range(2):
            for k in range(FIRST):
                step(slot, bases[slot], mines[slot], k)
        for slot in range(2):
            more = steps_ref[codes[slot], rows[slot] & (W - 1)] - FIRST
            which = sum((more > t).astype(I32) for t in TAILS[:-1])

            def tail(size, slot=slot):
                def run():
                    for k in range(FIRST, FIRST + size):
                        step(slot, bases[slot], mines[slot], k)
                    if FIRST + size < DEG:
                        rest = (DEG - FIRST - size) * GROUP
                        end = (slot + 1) * DEG * GROUP
                        hidden[end - rest : end, :] = jnp.zeros((rest, W), BF16)

                return run

            lax.switch(which, [tail(t) for t in TAILS])
        return tuple(rows)

    last = lax.fori_loop(0, rounds, gather, (jnp.int32(DUMP), jnp.int32(DUMP)))
    for turn, copy in zip(turns, copies):
        pl.when(turn == rounds)(copy.wait)
    finish(hidden[...], last)

    w_third = ethird_ref[...]
    n_agg = nfirst_ref[W : 2 * W, :]
    n_second = nsecond_ref[...]
    n_third = nthird_ref[...]

    def node(i, carry):
        rows = pl.ds(pl.multiple_of(i * (SPAN * W), SPAN * W), SPAN * W)
        live = jnp.concatenate(
            [iota((W, W), 0) < cnt_ref[i * SPAN + j, 0] for j in range(SPAN)], axis=0
        )
        lone_part = times_ref[rows, :].astype(F32) * alone_ref[rows, :].astype(F32)
        summed = jnp.where(live, agg[rows, :] + lone_part, 0.0)
        top = summed.astype(BF16)
        rest = (summed - top.astype(F32)).astype(BF16)
        total = (dot(top, w_third) + dot(rest, w_third)).astype(BF16)
        state = state_ref[rows, :]
        h = jnp.maximum(first_ref[rows, :] + dot(total, n_agg), 0.0).astype(BF16)
        h = jnp.maximum(dot(h, n_second), 0.0).astype(BF16)
        update = dot(h, n_third)
        mean = jnp.mean(update, axis=1, keepdims=True)
        centred = update - mean
        var = jnp.mean(centred * centred, axis=1, keepdims=True)
        new = state.astype(F32) + centred * lax.rsqrt(var + 1e-05)
        full[rows, :] = jnp.where(live, new, MARK)
        out_ref[rows, :] = jnp.where(live, new, 0.0).astype(BF16)
        return carry

    lax.fori_loop(0, ROWS // (SPAN * W), node, 0)
    pick_slabs(gidx_ref, full, picked, down_ref, up_ref)


def one_layer(idx, pos, steps, cnt, gidx, own, times, state, around, weights):
    return pl.pallas_call(
        layer_kernel,
        out_shape=[
            jax.ShapeDtypeStruct((NODES + 8, W), F32),
            jax.ShapeDtypeStruct((ROWS, W), BF16),
            jax.ShapeDtypeStruct((2, 2, SLAB, W), BF16),
            jax.ShapeDtypeStruct((2, 2, SLAB, W), BF16),
        ],
        in_specs=[pl.BlockSpec(memory_space=pl.ANY)] + [smem()] * 4 + [vmem()] * (12 + AROUND),
        out_specs=[vmem()] * 4,
        input_output_aliases={5: 0},
        scratch_shapes=[
            pltpu.VMEM((GHOSTS, W), BF16),
            pltpu.VMEM((2 * DEG * GROUP, W), BF16),
            pltpu.VMEM((ROWS + GROUP, W), F32),
            pltpu.VMEM((ROWS, W), F32),
            pltpu.VMEM((8 * SLAB, W), F32),
            pltpu.SMEM((ROWS * DEG,), I32),
            pltpu.SMEM((256,), I32),
            pltpu.SemaphoreType.DMA((len(PARTS),)),
        ],
        compiler_params=pltpu.CompilerParams(vmem_limit_bytes=VMEM_LIMIT),
        name="layer",
    )(idx, pos, steps, cnt, gidx, *own, times, state, *around, *weights)[1:]


def both_ways(up, down, axis):
    n = lax.axis_size(axis)
    forward = [(i, (i + 1) % n) for i in range(n)]
    backward = [(b, a) for a, b in forward]
    return lax.ppermute(up, axis, forward), lax.ppermute(down, axis, backward)


def migrate(down, mid, up):
    low, high = both_ways(up, down, "gx")
    buffer = jnp.stack([low, mid, high])
    low, high = both_ways(buffer[:, 2], buffer[:, 0], "gy")
    buffer = jnp.stack([low, buffer[:, 1], high], axis=1)
    low, high = both_ways(buffer[:, :, 2], buffer[:, :, 0], "gz")
    return buffer[:, :, 1], low, high


def surround(down, up):
    x_low, x_high = both_ways(up, down, "gx")
    rows = (x_low, down, up, x_high)
    y_low, y_high = both_ways(
        jnp.stack([r[1] for r in rows]), jnp.stack([r[0] for r in rows]), "gy"
    )

    def face(c):
        return jnp.stack(
            [jnp.stack([y_low[a, c], r[0, c], r[1, c], y_high[a, c]]) for a, r in enumerate(rows)]
        )

    z_low, z_high = both_ways(face(1), face(0), "gz")
    return x_low, x_high, y_low, y_high, z_low, z_high


def body(
    latent,
    destination,
    neighbours,
    valid,
    ghost_index,
    edge_first,
    edge_second,
    edge_third,
    node_first,
    node_second,
    node_third,
):
    dest = destination.reshape(1, 1024)
    nbr = neighbours[0, 0, 0].T
    mask = valid[0, 0, 0].T
    gidx = ghost_index.reshape(-1)
    pos = jnp.stack([lax.axis_index(a) for a in HALO_AXES]).astype(I32)
    state, cnt, down, up = receive(gidx, *migrate(*pack(dest, latent[0, 0, 0])))
    for layer in range(edge_first.shape[0]):
        weights = [
            w[layer]
            for w in (edge_first, edge_second, edge_third, node_first, node_second, node_third)
        ]
        table, recv = project(state, weights[0])
        own = (table, recv, *lone(state, recv, weights[1], weights[3]))
        around = surround(down, up)
        if layer == 0:
            idx, steps, times = indices(pos, nbr, mask, cnt, around)
            idx = idx.reshape(-1)
        state, down, up = one_layer(
            idx, pos, steps, cnt, gidx, own, times, state, around, weights
        )
    return state.reshape(1, 1, 1, ROWS, W)


def solution(mesh):
    spread = P("gx", "gy", "gz", None, None)
    return jax.shard_map(
        body,
        mesh=mesh,
        in_specs=(spread,) * 5 + (P(),) * 6,
        out_specs=spread,
        check_vma=False,
    )
```

```python
import jax
import jax.numpy as jnp
import numpy as np
from jax import lax
from jax.experimental import pallas as pl
from jax.experimental.pallas import tpu as pltpu
from jax.sharding import PartitionSpec as P

F32 = jnp.float32
BF16 = jnp.bfloat16
I32 = jnp.int32
W = 128
CODES = 27
ROWS = CODES * W
DEG = 24
SLAB = 32
OUTER = [
    p for p in range(64) if p // 16 in (0, 3) or p // 4 % 4 in (0, 3) or p % 4 in (0, 3)
]
AROUND = 6
GHOSTS = len(OUTER) * SLAB
NODES = ROWS + GHOSTS
DUMMY = NODES
MARK = 2.0**100
HALO_AXES = ("gx", "gy", "gz")
GRID = (4, 4, 8)
VMEM_LIMIT = 24 * 2**20


def dot(a, b):
    return jnp.dot(a, b, preferred_element_type=F32)


def vmem():
    return pl.BlockSpec(memory_space=pltpu.VMEM)


def smem():
    return pl.BlockSpec(memory_space=pltpu.SMEM)


def iota(shape, dim):
    return lax.broadcasted_iota(I32, shape, dim)


def pack_kernel(dest_ref, rows_hbm, down_ref, mid_ref, up_ref, slot_ref, rows_ref, sem):
    fetch = pltpu.make_async_copy(rows_hbm, rows_ref, sem)
    fetch.start()
    n_y, n_z = 4, 8
    ix, iy, iz = (lax.axis_index(a) for a in HALO_AXES)
    tri = (iota((W, W), 0) < iota((W, W), 1)).astype(BF16)
    ones = jnp.ones((W, W), BF16)
    off = jnp.zeros((32, W), F32)
    for j in range(8):
        d = dest_ref[:, j * W : (j + 1) * W]
        code = (
            (lax.shift_right_logical(d, 5) - ix + 1) * 9
            + ((lax.shift_right_logical(d, 3) & (n_y - 1)) - iy + 1) * 3
            + ((d & (n_z - 1)) - iz + 1)
        )
        hit = iota((32, W), 0) == code
        one = jnp.where(hit, 1.0, 0.0).astype(BF16)
        before = dot(one, tri) + off
        rank = jnp.sum(jnp.where(hit, before, 0.0), axis=0, keepdims=True)
        slot_ref[:, j * W : (j + 1) * W] = code * W + rank.astype(I32)
        off = off + dot(one, ones)
    slot = slot_ref[...]
    fetch.wait()
    rows = rows_ref[...]
    for part, out_ref in enumerate((down_ref, mid_ref, up_ref)):
        first = part * 9 * W
        chosen = jnp.where(slot == iota((9 * W, 1024), 0) + first, 1.0, 0.0).astype(BF16)
        got = dot(chosen, rows)
        for c in range(9):
            alive = iota((W, W), 0).astype(F32) < off[part * 9 + c : part * 9 + c + 1, :]
            block = jnp.where(alive, got[c * W : (c + 1) * W, :], MARK)
            out_ref[c // 3, c % 3] = block.astype(BF16)


def pack(dest, rows):
    return pl.pallas_call(
        pack_kernel,
        out_shape=[jax.ShapeDtypeStruct((3, 3, W, W), BF16)] * 3,
        in_specs=[vmem(), pl.BlockSpec(memory_space=pltpu.HBM)],
        out_specs=[vmem()] * 3,
        scratch_shapes=[
            pltpu.VMEM((1, 1024), I32),
            pltpu.VMEM((1024, W), BF16),
            pltpu.SemaphoreType.DMA,
        ],
        compiler_params=pltpu.CompilerParams(vmem_limit_bytes=VMEM_LIMIT),
        name="pack",
    )(dest, rows)


def receive_kernel(
    gidx_ref, mid_ref, low_ref, high_ref, state_ref, cnt_ref, down_ref, up_ref, full, picked
):
    pos = [lax.axis_index(a) for a in HALO_AXES]
    cnt_ref[...] = jnp.zeros_like(cnt_ref)
    for c in range(CODES):
        offs = (c // 9 - 1, c // 3 % 3 - 1, c % 3 - 1)
        inside = jnp.int32(1)
        for p, o, s in zip(pos, offs, GRID):
            if o < 0:
                inside = inside * (p > 0).astype(I32)
            if o > 0:
                inside = inside * (p < s - 1).astype(I32)
        if c % 3 == 1:
            x = mid_ref[c // 9, c // 3 % 3].astype(F32)
        else:
            x = (low_ref if c % 3 == 0 else high_ref)[c // 9, c // 3 % 3].astype(F32)
        alive = x < MARK * 0.5
        count = jnp.sum(jnp.where(alive, 1.0, 0.0), axis=0, keepdims=True).astype(I32)
        cnt_ref[c : c + 1, :] = count * inside
        present = iota((W, W), 0) < count * inside
        full[c * W : (c + 1) * W, :] = jnp.where(present, x, MARK)
        state_ref[c * W : (c + 1) * W, :] = jnp.where(present, x, 0.0).astype(BF16)
    pick_slabs(gidx_ref, full, picked, down_ref, up_ref)


def pick_slabs(gidx_ref, full, picked, down_ref, up_ref):
    def some(b, carry):
        for r in range(16):
            picked[pl.ds(b * 16 + r, 1), :] = full[pl.ds(gidx_ref[b * 16 + r], 1), :]
        return carry

    lax.fori_loop(0, 16, some, 0)
    for s in range(8):
        out_ref = up_ref if s // 4 else down_ref
        out_ref[s // 2 % 2, s % 2] = picked[s * SLAB : (s + 1) * SLAB, :].astype(BF16)


def receive(gidx, mid, low, high):
    return pl.pallas_call(
        receive_kernel,
        out_shape=[
            jax.ShapeDtypeStruct((ROWS, W), BF16),
            jax.ShapeDtypeStruct((32, W), I32),
            jax.ShapeDtypeStruct((2, 2, SLAB, W), BF16),
            jax.ShapeDtypeStruct((2, 2, SLAB, W), BF16),
        ],
        in_specs=[smem()] + [vmem()] * 3,
        out_specs=[vmem()] * 4,
        scratch_shapes=[pltpu.VMEM((ROWS, W), F32), pltpu.VMEM((8 * SLAB, W), F32)],
        compiler_params=pltpu.CompilerParams(vmem_limit_bytes=VMEM_LIMIT),
        name="receive",
    )(gidx, mid, low, high)


def sort_pairs(count):
    pairs = []
    size = 1
    while size < count:
        size *= 2
    p = 1
    while p < size:
        k = p
        while k >= 1:
            for j in range(k % p, size - k, 2 * k):
                for i in range(min(k, size - j - k)):
                    if (i + j) // (2 * p) == (i + j + k) // (2 * p) and i + j + k < count:
                        pairs.append((i + j, i + j + k))
            k //= 2
        p *= 2
    return pairs


def fill_ghosts(pos_ref, around, ghosts):
    first = [pos_ref[i] == 0 for i in range(3)]
    final = [pos_ref[i] == n - 1 for i, n in enumerate(GRID)]
    for s, p in enumerate(OUTER):
        a, b, c = p // 16, p // 4 % 4, p % 4
        absent = None
        for i, at in enumerate((a, b, c)):
            if at in (0, 3):
                edge = first[i] if at == 0 else final[i]
                absent = edge if absent is None else absent | edge
        x_low, x_high, y_low, y_high, z_low, z_high = around
        if c in (0, 3):
            slab = (z_high if c else z_low)[a, b]
        elif b in (0, 3):
            slab = (y_high if b else y_low)[a, c - 1]
        else:
            slab = (x_high if a else x_low)[b - 1, c - 1]
        slab = jnp.where(absent, MARK, slab.astype(F32)).astype(BF16)
        ghosts[s * SLAB : (s + 1) * SLAB, :] = slab


def index_kernel(
    pos_ref,
    nbr_ref,
    valid_ref,
    cnt_ref,
    *refs,
):
    around, (idx_ref, steps_ref, times_ref, ghosts, held) = refs[:AROUND], refs[AROUND:]
    fill_ghosts(pos_ref, around, ghosts)
    alive = jnp.where(ghosts[...].astype(F32) < MARK * 0.5, 1.0, 0.0).astype(BF16)
    at = iota((W, GHOSTS), 1)
    bit = jnp.left_shift(1, at & 15).astype(F32)
    spread = jnp.where(lax.shift_right_logical(at, 4) == iota((W, GHOSTS), 0), bit, 0.0)
    words = dot(spread.astype(BF16), alive)
    eye = iota((W, W), 0) == iota((W, W), 1)
    words = jnp.sum(jnp.where(eye, words, 0.0), axis=0, keepdims=True).astype(I32)
    words = jnp.broadcast_to(words, (8, W))
    counts = cnt_ref[...]
    diag = iota((32, W), 0) == iota((32, W), 1)
    by_code = jnp.sum(jnp.where(diag, counts.astype(F32), 0.0), axis=0, keepdims=True)
    by_code = jnp.broadcast_to(by_code.astype(I32), (8, W))

    held[...] = jnp.zeros_like(held) - 1
    for c in range(CODES):
        cols = slice(c * W, (c + 1) * W)
        held[c * DEG : (c + 1) * DEG, :] = jnp.where(valid_ref[:, cols] > 0, nbr_ref[:, cols], -1)

    for b in range(4):
        here = iota((8, W), 1) < counts[b * 8 : (b + 1) * 8, :]
        keys = []
        dead = jnp.zeros((8, W), F32)
        for k in range(DEG):
            node = held[pl.ds(b * 8 * DEG + k, 8, stride=DEG), :]
            far = jnp.maximum(node - ROWS, 0)
            word = jnp.take_along_axis(words, lax.shift_right_logical(far, 4), axis=1)
            flag = lax.shift_right_logical(word, far & 15) & 1
            near = jnp.minimum(jnp.maximum(node, 0), ROWS - 1)
            limit = jnp.take_along_axis(by_code, lax.shift_right_logical(near, 7), axis=1)
            lives = jnp.where(node >= ROWS, flag, jnp.where((near & (W - 1)) < limit, 1, 0))
            real = node >= 0
            key = jnp.where(here & real & (lives > 0), node, DUMMY)
            dead = dead + jnp.where(here & real & (lives == 0), 1.0, 0.0)
            keys.append(key.astype(F32))
        for i, j in sort_pairs(DEG):
            keys[i], keys[j] = jnp.minimum(keys[i], keys[j]), jnp.maximum(keys[i], keys[j])
        used = jnp.zeros((8, W), F32)
        for k in range(DEG):
            used = used + jnp.where(keys[k] < DUMMY, 1.0, 0.0)
            idx_ref[pl.ds(b * 8 * DEG + k, 8, stride=DEG), :] = keys[k].astype(I32)
        for shift in (1, 2, 4):
            used = jnp.maximum(used, pltpu.roll(used, W - shift, 1))
        steps_ref[b * 8 : (b + 1) * 8, :] = used.astype(I32)
        for c in range(b * 8, min(b * 8 + 8, CODES)):
            row = jnp.broadcast_to(dead[c - b * 8 : c - b * 8 + 1, :], (W, W))
            lone = jnp.where(eye, row, 0.0).astype(BF16)
            times_ref[c * W : (c + 1) * W, :] = dot(lone, jnp.ones((W, W), BF16)).astype(BF16)


def indices(pos, nbr, valid, cnt, around):
    return pl.pallas_call(
        index_kernel,
        out_shape=[
            jax.ShapeDtypeStruct((DEG * 32, W), I32),
            jax.ShapeDtypeStruct((32, W), I32),
            jax.ShapeDtypeStruct((ROWS, W), BF16),
        ],
        in_specs=[smem()] + [vmem()] * (3 + AROUND),
        out_specs=[vmem()] * 3,
        scratch_shapes=[pltpu.VMEM((GHOSTS, W), BF16), pltpu.VMEM((32 * DEG, W), I32)],
        compiler_params=pltpu.CompilerParams(vmem_limit_bytes=VMEM_LIMIT),
        name="indices",
    )(pos, nbr, valid, cnt, *around)


GROUP = 16
SPAN = 27
FIRST = 12
TAILS = (0, 1, 2, 3, 4, 6, 8, 12)
DUMP = ROWS
PARTS = ((0, 3), (3, 11), (11, CODES))


def project_kernel(state_ref, efirst_ref, table_ref, recv_ref):
    w_both = jnp.concatenate([efirst_ref[0:W, :], efirst_ref[W : 2 * W, :]], axis=1)

    def own(i, carry):
        rows = pl.ds(pl.multiple_of(i * 1152, 1152), 1152)
        both = dot(state_ref[rows, :], w_both)
        recv_ref[rows, :] = both[:, :W]
        table_ref[rows, :] = both[:, W:]
        return carry

    lax.fori_loop(0, ROWS // 1152, own, 0)
    table_ref[NODES : NODES + 8, :] = jnp.full((8, W), -MARK, F32)


def project(state, efirst):
    return pl.pallas_call(
        project_kernel,
        out_shape=[
            jax.ShapeDtypeStruct((NODES + 8, W), F32),
            jax.ShapeDtypeStruct((ROWS, W), F32),
        ],
        in_specs=[vmem()] * 2,
        out_specs=[vmem()] * 2,
        compiler_params=pltpu.CompilerParams(vmem_limit_bytes=VMEM_LIMIT),
        name="project",
    )(state, efirst)


def lone_kernel(state_ref, recv_ref, esecond_ref, nfirst_ref, alone_ref, first_ref):
    w_second = esecond_ref[...]
    n_state = nfirst_ref[0:W, :]

    def some(i, carry):
        rows = pl.ds(pl.multiple_of(i * 1152, 1152), 1152)
        alone = jnp.maximum(recv_ref[rows, :], 0.0).astype(BF16)
        alone_ref[rows, :] = jnp.maximum(dot(alone, w_second), 0.0).astype(BF16)
        first_ref[rows, :] = dot(state_ref[rows, :], n_state)
        return carry

    lax.fori_loop(0, ROWS // 1152, some, 0)


def lone(state, recv, esecond, nfirst):
    return pl.pallas_call(
        lone_kernel,
        out_shape=[
            jax.ShapeDtypeStruct((ROWS, W), BF16),
            jax.ShapeDtypeStruct((ROWS, W), F32),
        ],
        in_specs=[vmem()] * 4,
        out_specs=[vmem()] * 2,
        compiler_params=pltpu.CompilerParams(vmem_limit_bytes=VMEM_LIMIT),
        name="lone",
    )(state, recv, esecond, nfirst)


def layer_kernel(
    idx_hbm,
    pos_ref,
    steps_ref,
    cnt_ref,
    gidx_ref,
    table_in,
    recv,
    alone_ref,
    first_ref,
    times_ref,
    state_ref,
    *refs,
):
    around, refs = refs[:AROUND], refs[AROUND:]
    efirst_ref, esecond_ref, ethird_ref, nfirst_ref, nsecond_ref, nthird_ref = refs[:6]
    table, out_ref, down_ref, up_ref = refs[6:10]
    ghosts, hidden, agg, full, picked, idx_ref, homes, sems = refs[10:]
    del table_in
    copies = []
    for i, (lo, hi) in enumerate(PARTS):
        words = pl.ds(lo * DEG * W, (hi - lo) * DEG * W)
        copies.append(pltpu.make_async_copy(idx_hbm.at[words], idx_ref.at[words], sems.at[i]))
        copies[-1].start()
    w_send = efirst_ref[W : 2 * W, :]
    fill_ghosts(pos_ref, around, ghosts)

    def far(i, carry):
        x = ghosts[pl.ds(pl.multiple_of(i * 896, 128), 896), :].astype(F32)
        x = jnp.where(x < MARK * 0.5, x, 0.0).astype(BF16)
        table[pl.ds(pl.multiple_of(ROWS + i * 896, 128), 896), :] = dot(x, w_send)
        return carry

    lax.fori_loop(0, GHOSTS // 896, far, 0)

    w_second = esecond_ref[...]
    sub = iota((8, W), 0)

    def listed(c, n):
        for g in range(W // 8):
            homes[n + g] = c * W + g * 8
        return n + lax.shift_right_logical(cnt_ref[c, 0] + 7, 3)

    starts = [jnp.int32(0)]
    for lo, hi in PARTS:
        starts.append(lax.fori_loop(lo, hi, listed, starts[-1]))
    total = starts[-1]
    for extra in range(3):
        homes[total + extra] = homes[jnp.maximum(total - 1, 0)]
    rounds = lax.shift_right_logical(total + 3, 2)
    turns = [jnp.minimum(lax.shift_right_logical(n, 2), rounds) for n in starts[:-1]]

    def finish(h, rows):
        d = jnp.maximum(dot(h, w_second), 0.0).astype(BF16).astype(F32)
        d = jnp.sum(d.reshape(2, DEG, GROUP, W), axis=1)
        for u, row in enumerate(rows):
            piece = d[u // 2, (u % 2) * 8 : (u % 2) * 8 + 8, :]
            agg[pl.ds(pl.multiple_of(row, 8), 8), :] = piece

    def step(slot, bases, mines, k):
        both = []
        for half in range(2):
            base, mine = bases[2 * slot + half], mines[2 * slot + half]
            got = None
            for r in range(8):
                at = idx_ref[base + (k * W + r)]
                row = jnp.broadcast_to(table[pl.ds(at, 1), :], (8, W))
                got = row if got is None else jnp.where(sub == r, row, got)
            both.append(jnp.maximum(got + mine, 0.0))
        at = (slot * DEG + k) * GROUP
        hidden[at : at + GROUP, :] = jnp.concatenate(both, axis=0).astype(BF16)

    def gather(i, last):
        for turn, copy in zip(turns, copies):
            pl.when(i == turn)(copy.wait)
        rows = [pl.multiple_of(homes[4 * i + u], 8) for u in range(4)]
        codes = [lax.shift_right_logical(row, 7) for row in rows]
        bases = [row + code * ((DEG - 1) * W) for row, code in zip(rows, codes)]
        mines = [recv[pl.ds(row, 8), :] for row in rows]
        needs = [steps_ref[code, row & (W - 1)] for row, code in zip(rows, codes)]
        finish(hidden[...], last)
        for slot in range(2):
            for k in range(FIRST):
                step(slot, bases, mines, k)
        for slot in range(2):
            more = jnp.maximum(needs[2 * slot], needs[2 * slot + 1]) - FIRST
            which = sum((more > t).astype(I32) for t in TAILS[:-1])

            def tail(size, slot=slot):
                def run():
                    for k in range(FIRST, FIRST + size):
                        step(slot, bases, mines, k)
                    if FIRST + size < DEG:
                        rest = (DEG - FIRST - size) * GROUP
                        end = (slot + 1) * DEG * GROUP
                        hidden[end - rest : end, :] = jnp.zeros((rest, W), BF16)

                return run

            lax.switch(which, [tail(t) for t in TAILS])
        return tuple(rows)

    last = lax.fori_loop(0, rounds, gather, (jnp.int32(DUMP),) * 4)
    for turn, copy in zip(turns, copies):
        pl.when(turn == rounds)(copy.wait)
    finish(hidden[...], last)

    w_third = ethird_ref[...]
    n_agg = nfirst_ref[W : 2 * W, :]
    n_second = nsecond_ref[...]
    n_third = nthird_ref[...]

    def node(i, carry):
        rows = pl.ds(pl.multiple_of(i * (SPAN * W), SPAN * W), SPAN * W)
        live = jnp.concatenate(
            [iota((W, W), 0) < cnt_ref[i * SPAN + j, 0] for j in range(SPAN)], axis=0
        )
        lone_part = times_ref[rows, :].astype(F32) * alone_ref[rows, :].astype(F32)
        summed = jnp.where(live, agg[rows, :] + lone_part, 0.0)
        top = summed.astype(BF16)
        rest = (summed - top.astype(F32)).astype(BF16)
        total = (dot(top, w_third) + dot(rest, w_third)).astype(BF16)
        state = state_ref[rows, :]
        h = jnp.maximum(first_ref[rows, :] + dot(total, n_agg), 0.0).astype(BF16)
        h = jnp.maximum(dot(h, n_second), 0.0).astype(BF16)
        update = dot(h, n_third)
        mean = jnp.mean(update, axis=1, keepdims=True)
        centred = update - mean
        var = jnp.mean(centred * centred, axis=1, keepdims=True)
        new = state.astype(F32) + centred * lax.rsqrt(var + 1e-05)
        full[rows, :] = jnp.where(live, new, MARK)
        out_ref[rows, :] = jnp.where(live, new, 0.0).astype(BF16)
        return carry

    lax.fori_loop(0, ROWS // (SPAN * W), node, 0)
    pick_slabs(gidx_ref, full, picked, down_ref, up_ref)


def one_layer(idx, pos, steps, cnt, gidx, own, times, state, around, weights):
    return pl.pallas_call(
        layer_kernel,
        out_shape=[
            jax.ShapeDtypeStruct((NODES + 8, W), F32),
            jax.ShapeDtypeStruct((ROWS, W), BF16),
            jax.ShapeDtypeStruct((2, 2, SLAB, W), BF16),
            jax.ShapeDtypeStruct((2, 2, SLAB, W), BF16),
        ],
        in_specs=[pl.BlockSpec(memory_space=pl.ANY)] + [smem()] * 4 + [vmem()] * (12 + AROUND),
        out_specs=[vmem()] * 4,
        input_output_aliases={5: 0},
        scratch_shapes=[
            pltpu.VMEM((GHOSTS, W), BF16),
            pltpu.VMEM((2 * DEG * GROUP, W), BF16),
            pltpu.VMEM((ROWS + GROUP, W), F32),
            pltpu.VMEM((ROWS, W), F32),
            pltpu.VMEM((8 * SLAB, W), F32),
            pltpu.SMEM((ROWS * DEG,), I32),
            pltpu.SMEM((512,), I32),
            pltpu.SemaphoreType.DMA((len(PARTS),)),
        ],
        compiler_params=pltpu.CompilerParams(vmem_limit_bytes=VMEM_LIMIT),
        name="layer",
    )(idx, pos, steps, cnt, gidx, *own, times, state, *around, *weights)[1:]


def both_ways(up, down, axis):
    n = lax.axis_size(axis)
    forward = [(i, (i + 1) % n) for i in range(n)]
    backward = [(b, a) for a, b in forward]
    return lax.ppermute(up, axis, forward), lax.ppermute(down, axis, backward)


def migrate(down, mid, up):
    low, high = both_ways(up, down, "gx")
    buffer = jnp.stack([low, mid, high])
    low, high = both_ways(buffer[:, 2], buffer[:, 0], "gy")
    buffer = jnp.stack([low, buffer[:, 1], high], axis=1)
    low, high = both_ways(buffer[:, :, 2], buffer[:, :, 0], "gz")
    return buffer[:, :, 1], low, high


def surround(down, up):
    x_low, x_high = both_ways(up, down, "gx")
    rows = (x_low, down, up, x_high)
    y_low, y_high = both_ways(
        jnp.stack([r[1] for r in rows]), jnp.stack([r[0] for r in rows]), "gy"
    )

    def face(c):
        return jnp.stack(
            [jnp.stack([y_low[a, c], r[0, c], r[1, c], y_high[a, c]]) for a, r in enumerate(rows)]
        )

    z_low, z_high = both_ways(face(1), face(0), "gz")
    return x_low, x_high, y_low, y_high, z_low, z_high


def body(
    latent,
    destination,
    neighbours,
    valid,
    ghost_index,
    edge_first,
    edge_second,
    edge_third,
    node_first,
    node_second,
    node_third,
):
    dest = destination.reshape(1, 1024)
    nbr = neighbours[0, 0, 0].T
    mask = valid[0, 0, 0].T
    gidx = ghost_index.reshape(-1)
    pos = jnp.stack([lax.axis_index(a) for a in HALO_AXES]).astype(I32)
    state, cnt, down, up = receive(gidx, *migrate(*pack(dest, latent[0, 0, 0])))
    for layer in range(edge_first.shape[0]):
        weights = [
            w[layer]
            for w in (edge_first, edge_second, edge_third, node_first, node_second, node_third)
        ]
        table, recv = project(state, weights[0])
        own = (table, recv, *lone(state, recv, weights[1], weights[3]))
        around = surround(down, up)
        if layer == 0:
            idx, steps, times = indices(pos, nbr, mask, cnt, around)
            idx = idx.reshape(-1)
        state, down, up = one_layer(
            idx, pos, steps, cnt, gidx, own, times, state, around, weights
        )
    return state.reshape(1, 1, 1, ROWS, W)


def solution(mesh):
    spread = P("gx", "gy", "gz", None, None)
    return jax.shard_map(
        body,
        mesh=mesh,
        in_specs=(spread,) * 5 + (P(),) * 6,
        out_specs=spread,
        check_vma=False,
    )
```

```python
import jax
import jax.numpy as jnp
import numpy as np
from jax import lax
from jax.experimental import pallas as pl
from jax.experimental.pallas import tpu as pltpu
from jax.sharding import PartitionSpec as P

F32 = jnp.float32
BF16 = jnp.bfloat16
I32 = jnp.int32
W = 128
CODES = 27
ROWS = CODES * W
DEG = 24
SLAB = 32
OUTER = [
    p for p in range(64) if p // 16 in (0, 3) or p // 4 % 4 in (0, 3) or p % 4 in (0, 3)
]
AROUND = 6
GHOSTS = len(OUTER) * SLAB
NODES = ROWS + GHOSTS
DUMMY = NODES
MARK = 2.0**100
HALO_AXES = ("gx", "gy", "gz")
GRID = (4, 4, 8)
VMEM_LIMIT = 24 * 2**20


def dot(a, b):
    return jnp.dot(a, b, preferred_element_type=F32)


def vmem():
    return pl.BlockSpec(memory_space=pltpu.VMEM)


def smem():
    return pl.BlockSpec(memory_space=pltpu.SMEM)


def iota(shape, dim):
    return lax.broadcasted_iota(I32, shape, dim)


def pack_kernel(dest_ref, rows_hbm, down_ref, mid_ref, up_ref, slot_ref, rows_ref, sem):
    fetch = pltpu.make_async_copy(rows_hbm, rows_ref, sem)
    fetch.start()
    n_y, n_z = 4, 8
    ix, iy, iz = (lax.axis_index(a) for a in HALO_AXES)
    tri = (iota((W, W), 0) < iota((W, W), 1)).astype(BF16)
    ones = jnp.ones((W, W), BF16)
    off = jnp.zeros((32, W), F32)
    for j in range(8):
        d = dest_ref[:, j * W : (j + 1) * W]
        code = (
            (lax.shift_right_logical(d, 5) - ix + 1) * 9
            + ((lax.shift_right_logical(d, 3) & (n_y - 1)) - iy + 1) * 3
            + ((d & (n_z - 1)) - iz + 1)
        )
        hit = iota((32, W), 0) == code
        one = jnp.where(hit, 1.0, 0.0).astype(BF16)
        before = dot(one, tri) + off
        rank = jnp.sum(jnp.where(hit, before, 0.0), axis=0, keepdims=True)
        slot_ref[:, j * W : (j + 1) * W] = code * W + rank.astype(I32)
        off = off + dot(one, ones)
    slot = slot_ref[...]
    fetch.wait()
    rows = rows_ref[...]
    for part, out_ref in enumerate((down_ref, mid_ref, up_ref)):
        first = part * 9 * W
        chosen = jnp.where(slot == iota((9 * W, 1024), 0) + first, 1.0, 0.0).astype(BF16)
        got = dot(chosen, rows)
        for c in range(9):
            alive = iota((W, W), 0).astype(F32) < off[part * 9 + c : part * 9 + c + 1, :]
            block = jnp.where(alive, got[c * W : (c + 1) * W, :], MARK)
            out_ref[c // 3, c % 3] = block.astype(BF16)


def pack(dest, rows):
    return pl.pallas_call(
        pack_kernel,
        out_shape=[jax.ShapeDtypeStruct((3, 3, W, W), BF16)] * 3,
        in_specs=[vmem(), pl.BlockSpec(memory_space=pltpu.HBM)],
        out_specs=[vmem()] * 3,
        scratch_shapes=[
            pltpu.VMEM((1, 1024), I32),
            pltpu.VMEM((1024, W), BF16),
            pltpu.SemaphoreType.DMA,
        ],
        compiler_params=pltpu.CompilerParams(vmem_limit_bytes=VMEM_LIMIT),
        name="pack",
    )(dest, rows)


def receive_kernel(
    gidx_ref, mid_ref, low_ref, high_ref, state_ref, cnt_ref, down_ref, up_ref, full, picked
):
    pos = [lax.axis_index(a) for a in HALO_AXES]
    cnt_ref[...] = jnp.zeros_like(cnt_ref)
    for c in range(CODES):
        offs = (c // 9 - 1, c // 3 % 3 - 1, c % 3 - 1)
        inside = jnp.int32(1)
        for p, o, s in zip(pos, offs, GRID):
            if o < 0:
                inside = inside * (p > 0).astype(I32)
            if o > 0:
                inside = inside * (p < s - 1).astype(I32)
        if c % 3 == 1:
            x = mid_ref[c // 9, c // 3 % 3].astype(F32)
        else:
            x = (low_ref if c % 3 == 0 else high_ref)[c // 9, c // 3 % 3].astype(F32)
        alive = x < MARK * 0.5
        count = jnp.sum(jnp.where(alive, 1.0, 0.0), axis=0, keepdims=True).astype(I32)
        cnt_ref[c : c + 1, :] = count * inside
        present = iota((W, W), 0) < count * inside
        full[c * W : (c + 1) * W, :] = jnp.where(present, x, MARK)
        state_ref[c * W : (c + 1) * W, :] = jnp.where(present, x, 0.0).astype(BF16)
    pick_slabs(gidx_ref, full, picked, down_ref, up_ref)


def pick_slabs(gidx_ref, full, picked, down_ref, up_ref):
    def some(b, carry):
        for r in range(16):
            picked[pl.ds(b * 16 + r, 1), :] = full[pl.ds(gidx_ref[b * 16 + r], 1), :]
        return carry

    lax.fori_loop(0, 16, some, 0)
    for s in range(8):
        out_ref = up_ref if s // 4 else down_ref
        out_ref[s // 2 % 2, s % 2] = picked[s * SLAB : (s + 1) * SLAB, :].astype(BF16)


def receive(gidx, mid, low, high):
    return pl.pallas_call(
        receive_kernel,
        out_shape=[
            jax.ShapeDtypeStruct((ROWS, W), BF16),
            jax.ShapeDtypeStruct((32, W), I32),
            jax.ShapeDtypeStruct((2, 2, SLAB, W), BF16),
            jax.ShapeDtypeStruct((2, 2, SLAB, W), BF16),
        ],
        in_specs=[smem()] + [vmem()] * 3,
        out_specs=[vmem()] * 4,
        scratch_shapes=[pltpu.VMEM((ROWS, W), F32), pltpu.VMEM((8 * SLAB, W), F32)],
        compiler_params=pltpu.CompilerParams(vmem_limit_bytes=VMEM_LIMIT),
        name="receive",
    )(gidx, mid, low, high)


def sort_pairs(count):
    pairs = []
    size = 1
    while size < count:
        size *= 2
    p = 1
    while p < size:
        k = p
        while k >= 1:
            for j in range(k % p, size - k, 2 * k):
                for i in range(min(k, size - j - k)):
                    if (i + j) // (2 * p) == (i + j + k) // (2 * p) and i + j + k < count:
                        pairs.append((i + j, i + j + k))
            k //= 2
        p *= 2
    return pairs


def fill_ghosts(pos_ref, around, ghosts):
    first = [pos_ref[i] == 0 for i in range(3)]
    final = [pos_ref[i] == n - 1 for i, n in enumerate(GRID)]
    for s, p in enumerate(OUTER):
        a, b, c = p // 16, p // 4 % 4, p % 4
        absent = None
        for i, at in enumerate((a, b, c)):
            if at in (0, 3):
                edge = first[i] if at == 0 else final[i]
                absent = edge if absent is None else absent | edge
        x_low, x_high, y_low, y_high, z_low, z_high = around
        if c in (0, 3):
            slab = (z_high if c else z_low)[a, b]
        elif b in (0, 3):
            slab = (y_high if b else y_low)[a, c - 1]
        else:
            slab = (x_high if a else x_low)[b - 1, c - 1]
        slab = jnp.where(absent, MARK, slab.astype(F32)).astype(BF16)
        ghosts[s * SLAB : (s + 1) * SLAB, :] = slab


EMPTY = -2
NONE = -1


def near_kernel(nbr_ref, valid_ref, cnt_ref, held_ref):
    counts = cnt_ref[...]
    diag = iota((32, W), 0) == iota((32, W), 1)
    by_code = jnp.sum(jnp.where(diag, counts.astype(F32), 0.0), axis=0, keepdims=True)
    by_code = jnp.broadcast_to(by_code.astype(I32), (DEG, W))
    held_ref[CODES * DEG :, :] = jnp.full(((32 - CODES) * DEG, W), NONE, I32)
    for c in range(CODES):
        cols = slice(c * W, (c + 1) * W)
        node = nbr_ref[:, cols]
        near = jnp.minimum(jnp.maximum(node, 0), ROWS - 1)
        limit = jnp.take_along_axis(by_code, lax.shift_right_logical(near, 7), axis=1)
        node = jnp.where((node < ROWS) & ((near & (W - 1)) >= limit), EMPTY, node)
        here = iota((DEG, W), 1) < counts[c : c + 1, :]
        held_ref[c * DEG : (c + 1) * DEG, :] = jnp.where(
            here & (valid_ref[:, cols] > 0), node, NONE
        )


def near_nodes(nbr, valid, cnt):
    return pl.pallas_call(
        near_kernel,
        out_shape=jax.ShapeDtypeStruct((32 * DEG, W), I32),
        in_specs=[vmem()] * 3,
        out_specs=vmem(),
        compiler_params=pltpu.CompilerParams(vmem_limit_bytes=VMEM_LIMIT),
        name="near_nodes",
    )(nbr, valid, cnt)


def index_kernel(pos_ref, held, *refs):
    around, (idx_ref, steps_ref, times_ref, ghosts) = refs[:AROUND], refs[AROUND:]
    fill_ghosts(pos_ref, around, ghosts)
    alive = jnp.where(ghosts[...].astype(F32) < MARK * 0.5, 1.0, 0.0).astype(BF16)
    at = iota((W, GHOSTS), 1)
    bit = jnp.left_shift(1, at & 15).astype(F32)
    spread = jnp.where(lax.shift_right_logical(at, 4) == iota((W, GHOSTS), 0), bit, 0.0)
    words = dot(spread.astype(BF16), alive)
    eye = iota((W, W), 0) == iota((W, W), 1)
    words = jnp.sum(jnp.where(eye, words, 0.0), axis=0, keepdims=True).astype(I32)
    words = jnp.broadcast_to(words, (8, W))
    for b in range(4):
        keys = []
        dead = jnp.zeros((8, W), F32)
        for k in range(DEG):
            node = held[pl.ds(b * 8 * DEG + k, 8, stride=DEG), :]
            far = jnp.maximum(node - ROWS, 0)
            word = jnp.take_along_axis(words, lax.shift_right_logical(far, 4), axis=1)
            flag = lax.shift_right_logical(word, far & 15) & 1
            lives = (node >= 0) & ((node < ROWS) | (flag > 0))
            key = jnp.where(lives, node, DUMMY)
            dead = dead + jnp.where((node == EMPTY) | ((node >= ROWS) & (flag == 0)), 1.0, 0.0)
            keys.append(key.astype(F32))
        for i, j in sort_pairs(DEG):
            keys[i], keys[j] = jnp.minimum(keys[i], keys[j]), jnp.maximum(keys[i], keys[j])
        used = jnp.zeros((8, W), F32)
        for k in range(DEG):
            used = used + jnp.where(keys[k] < DUMMY, 1.0, 0.0)
            idx_ref[pl.ds(b * 8 * DEG + k, 8, stride=DEG), :] = keys[k].astype(I32)
        for shift in (1, 2, 4):
            used = jnp.maximum(used, pltpu.roll(used, W - shift, 1))
        steps_ref[b * 8 : (b + 1) * 8, :] = used.astype(I32)
        for c in range(b * 8, min(b * 8 + 8, CODES)):
            row = jnp.broadcast_to(dead[c - b * 8 : c - b * 8 + 1, :], (W, W))
            lone = jnp.where(eye, row, 0.0).astype(BF16)
            times_ref[c * W : (c + 1) * W, :] = dot(lone, jnp.ones((W, W), BF16)).astype(BF16)


def indices(pos, held, around):
    return pl.pallas_call(
        index_kernel,
        out_shape=[
            jax.ShapeDtypeStruct((DEG * 32, W), I32),
            jax.ShapeDtypeStruct((32, W), I32),
            jax.ShapeDtypeStruct((ROWS, W), BF16),
        ],
        in_specs=[smem()] + [vmem()] * (1 + AROUND),
        out_specs=[vmem()] * 3,
        scratch_shapes=[pltpu.VMEM((GHOSTS, W), BF16)],
        compiler_params=pltpu.CompilerParams(vmem_limit_bytes=VMEM_LIMIT),
        name="indices",
    )(pos, held, *around)


GROUP = 16
SPAN = 27
FIRST = 12
TAILS = (0, 1, 2, 3, 4, 6, 8, 12)
DUMP = ROWS
PARTS = ((0, 3), (3, 11), (11, CODES))


def project_kernel(state_ref, efirst_ref, table_ref, recv_ref):
    w_both = jnp.concatenate([efirst_ref[0:W, :], efirst_ref[W : 2 * W, :]], axis=1)

    def own(i, carry):
        rows = pl.ds(pl.multiple_of(i * 1152, 1152), 1152)
        both = dot(state_ref[rows, :], w_both)
        recv_ref[rows, :] = both[:, :W]
        table_ref[rows, :] = both[:, W:]
        return carry

    lax.fori_loop(0, ROWS // 1152, own, 0)
    table_ref[NODES : NODES + 8, :] = jnp.full((8, W), -MARK, F32)


def project(state, efirst):
    return pl.pallas_call(
        project_kernel,
        out_shape=[
            jax.ShapeDtypeStruct((NODES + 8, W), F32),
            jax.ShapeDtypeStruct((ROWS, W), F32),
        ],
        in_specs=[vmem()] * 2,
        out_specs=[vmem()] * 2,
        compiler_params=pltpu.CompilerParams(vmem_limit_bytes=VMEM_LIMIT),
        name="project",
    )(state, efirst)


def lone_kernel(state_ref, recv_ref, esecond_ref, nfirst_ref, alone_ref, first_ref):
    w_second = esecond_ref[...]
    n_state = nfirst_ref[0:W, :]

    def some(i, carry):
        rows = pl.ds(pl.multiple_of(i * 1152, 1152), 1152)
        alone = jnp.maximum(recv_ref[rows, :], 0.0).astype(BF16)
        alone_ref[rows, :] = jnp.maximum(dot(alone, w_second), 0.0).astype(BF16)
        first_ref[rows, :] = dot(state_ref[rows, :], n_state)
        return carry

    lax.fori_loop(0, ROWS // 1152, some, 0)


def lone(state, recv, esecond, nfirst):
    return pl.pallas_call(
        lone_kernel,
        out_shape=[
            jax.ShapeDtypeStruct((ROWS, W), BF16),
            jax.ShapeDtypeStruct((ROWS, W), F32),
        ],
        in_specs=[vmem()] * 4,
        out_specs=[vmem()] * 2,
        compiler_params=pltpu.CompilerParams(vmem_limit_bytes=VMEM_LIMIT),
        name="lone",
    )(state, recv, esecond, nfirst)


def layer_kernel(
    idx_hbm,
    pos_ref,
    steps_ref,
    cnt_ref,
    gidx_ref,
    table_in,
    recv,
    alone_ref,
    first_ref,
    times_ref,
    state_ref,
    *refs,
):
    around, refs = refs[:AROUND], refs[AROUND:]
    efirst_ref, esecond_ref, ethird_ref, nfirst_ref, nsecond_ref, nthird_ref = refs[:6]
    table, out_ref, down_ref, up_ref = refs[6:10]
    ghosts, hidden, agg, full, picked, idx_ref, homes, sems = refs[10:]
    del table_in
    copies = []
    for i, (lo, hi) in enumerate(PARTS):
        words = pl.ds(lo * DEG * W, (hi - lo) * DEG * W)
        copies.append(pltpu.make_async_copy(idx_hbm.at[words], idx_ref.at[words], sems.at[i]))
        copies[-1].start()
    w_send = efirst_ref[W : 2 * W, :]
    fill_ghosts(pos_ref, around, ghosts)

    def far(i, carry):
        x = ghosts[pl.ds(pl.multiple_of(i * 896, 128), 896), :].astype(F32)
        x = jnp.where(x < MARK * 0.5, x, 0.0).astype(BF16)
        table[pl.ds(pl.multiple_of(ROWS + i * 896, 128), 896), :] = dot(x, w_send)
        return carry

    lax.fori_loop(0, GHOSTS // 896, far, 0)

    w_second = esecond_ref[...]
    sub = iota((8, W), 0)

    def listed(c, n):
        for g in range(W // 8):
            homes[n + g] = c * W + g * 8
        return n + lax.shift_right_logical(cnt_ref[c, 0] + 7, 3)

    starts = [jnp.int32(0)]
    for lo, hi in PARTS:
        starts.append(lax.fori_loop(lo, hi, listed, starts[-1]))
    total = starts[-1]
    for extra in range(3):
        homes[total + extra] = homes[jnp.maximum(total - 1, 0)]
    rounds = lax.shift_right_logical(total + 3, 2)
    turns = [jnp.minimum(lax.shift_right_logical(n, 2), rounds) for n in starts[:-1]]

    def finish(h, rows):
        d = jnp.maximum(dot(h, w_second), 0.0).astype(BF16).astype(F32)
        d = jnp.sum(d.reshape(2, DEG, GROUP, W), axis=1)
        for u, row in enumerate(rows):
            piece = d[u // 2, (u % 2) * 8 : (u % 2) * 8 + 8, :]
            agg[pl.ds(pl.multiple_of(row, 8), 8), :] = piece

    def step(slot, bases, mines, k):
        both = []
        for half in range(2):
            base, mine = bases[2 * slot + half], mines[2 * slot + half]
            got = None
            for r in range(8):
                at = idx_ref[base + (k * W + r)]
                row = jnp.broadcast_to(table[pl.ds(at, 1), :], (8, W))
                got = row if got is None else jnp.where(sub == r, row, got)
            both.append(jnp.maximum(got + mine, 0.0))
        at = (slot * DEG + k) * GROUP
        hidden[at : at + GROUP, :] = jnp.concatenate(both, axis=0).astype(BF16)

    def gather(i, last):
        for turn, copy in zip(turns, copies):
            pl.when(i == turn)(copy.wait)
        rows = [pl.multiple_of(homes[4 * i + u], 8) for u in range(4)]
        codes = [lax.shift_right_logical(row, 7) for row in rows]
        bases = [row + code * ((DEG - 1) * W) for row, code in zip(rows, codes)]
        mines = [recv[pl.ds(row, 8), :] for row in rows]
        needs = [steps_ref[code, row & (W - 1)] for row, code in zip(rows, codes)]
        finish(hidden[...], last)
        for slot in range(2):
            for k in range(FIRST):
                step(slot, bases, mines, k)
        for slot in range(2):
            more = jnp.maximum(needs[2 * slot], needs[2 * slot + 1]) - FIRST
            which = sum((more > t).astype(I32) for t in TAILS[:-1])

            def tail(size, slot=slot):
                def run():
                    for k in range(FIRST, FIRST + size):
                        step(slot, bases, mines, k)
                    if FIRST + size < DEG:
                        rest = (DEG - FIRST - size) * GROUP
                        end = (slot + 1) * DEG * GROUP
                        hidden[end - rest : end, :] = jnp.zeros((rest, W), BF16)

                return run

            lax.switch(which, [tail(t) for t in TAILS])
        return tuple(rows)

    last = lax.fori_loop(0, rounds, gather, (jnp.int32(DUMP),) * 4)
    for turn, copy in zip(turns, copies):
        pl.when(turn == rounds)(copy.wait)
    finish(hidden[...], last)

    w_twice = jnp.concatenate([ethird_ref[...], ethird_ref[...]], axis=0)
    n_agg = nfirst_ref[W : 2 * W, :]
    n_second = nsecond_ref[...]
    n_third = nthird_ref[...]

    def node(i, carry):
        rows = pl.ds(pl.multiple_of(i * (SPAN * W), SPAN * W), SPAN * W)
        live = jnp.concatenate(
            [iota((W, W), 0) < cnt_ref[i * SPAN + j, 0] for j in range(SPAN)], axis=0
        )
        lone_part = times_ref[rows, :].astype(F32) * alone_ref[rows, :].astype(F32)
        summed = jnp.where(live, agg[rows, :] + lone_part, 0.0)
        top = summed.astype(BF16)
        rest = (summed - top.astype(F32)).astype(BF16)
        both = jnp.concatenate([top, rest], axis=1)
        total = dot(both, w_twice).astype(BF16)
        state = state_ref[rows, :]
        h = jnp.maximum(first_ref[rows, :] + dot(total, n_agg), 0.0).astype(BF16)
        h = jnp.maximum(dot(h, n_second), 0.0).astype(BF16)
        update = dot(h, n_third)
        mean = jnp.mean(update, axis=1, keepdims=True)
        centred = update - mean
        var = jnp.mean(centred * centred, axis=1, keepdims=True)
        new = state.astype(F32) + centred * lax.rsqrt(var + 1e-05)
        full[rows, :] = jnp.where(live, new, MARK)
        out_ref[rows, :] = jnp.where(live, new, 0.0).astype(BF16)
        return carry

    lax.fori_loop(0, ROWS // (SPAN * W), node, 0)
    pick_slabs(gidx_ref, full, picked, down_ref, up_ref)


def one_layer(idx, pos, steps, cnt, gidx, own, times, state, around, weights):
    return pl.pallas_call(
        layer_kernel,
        out_shape=[
            jax.ShapeDtypeStruct((NODES + 8, W), F32),
            jax.ShapeDtypeStruct((ROWS, W), BF16),
            jax.ShapeDtypeStruct((2, 2, SLAB, W), BF16),
            jax.ShapeDtypeStruct((2, 2, SLAB, W), BF16),
        ],
        in_specs=[pl.BlockSpec(memory_space=pl.ANY)] + [smem()] * 4 + [vmem()] * (12 + AROUND),
        out_specs=[vmem()] * 4,
        input_output_aliases={5: 0},
        scratch_shapes=[
            pltpu.VMEM((GHOSTS, W), BF16),
            pltpu.VMEM((2 * DEG * GROUP, W), BF16),
            pltpu.VMEM((ROWS + GROUP, W), F32),
            pltpu.VMEM((ROWS, W), F32),
            pltpu.VMEM((8 * SLAB, W), F32),
            pltpu.SMEM((ROWS * DEG,), I32),
            pltpu.SMEM((512,), I32),
            pltpu.SemaphoreType.DMA((len(PARTS),)),
        ],
        compiler_params=pltpu.CompilerParams(vmem_limit_bytes=VMEM_LIMIT),
        name="layer",
    )(idx, pos, steps, cnt, gidx, *own, times, state, *around, *weights)[1:]


def both_ways(up, down, axis):
    n = lax.axis_size(axis)
    forward = [(i, (i + 1) % n) for i in range(n)]
    backward = [(b, a) for a, b in forward]
    return lax.ppermute(up, axis, forward), lax.ppermute(down, axis, backward)


def migrate(down, mid, up):
    low, high = both_ways(up, down, "gx")
    buffer = jnp.stack([low, mid, high])
    low, high = both_ways(buffer[:, 2], buffer[:, 0], "gy")
    buffer = jnp.stack([low, buffer[:, 1], high], axis=1)
    low, high = both_ways(buffer[:, :, 2], buffer[:, :, 0], "gz")
    return buffer[:, :, 1], low, high


def surround(down, up):
    x_low, x_high = both_ways(up, down, "gx")
    rows = (x_low, down, up, x_high)
    y_low, y_high = both_ways(
        jnp.stack([r[1] for r in rows]), jnp.stack([r[0] for r in rows]), "gy"
    )

    def face(c):
        return jnp.stack(
            [jnp.stack([y_low[a, c], r[0, c], r[1, c], y_high[a, c]]) for a, r in enumerate(rows)]
        )

    z_low, z_high = both_ways(face(1), face(0), "gz")
    return x_low, x_high, y_low, y_high, z_low, z_high


def body(
    latent,
    destination,
    neighbours,
    valid,
    ghost_index,
    edge_first,
    edge_second,
    edge_third,
    node_first,
    node_second,
    node_third,
):
    dest = destination.reshape(1, 1024)
    nbr = neighbours[0, 0, 0].T
    mask = valid[0, 0, 0].T
    gidx = ghost_index.reshape(-1)
    pos = jnp.stack([lax.axis_index(a) for a in HALO_AXES]).astype(I32)
    state, cnt, down, up = receive(gidx, *migrate(*pack(dest, latent[0, 0, 0])))
    for layer in range(edge_first.shape[0]):
        weights = [
            w[layer]
            for w in (edge_first, edge_second, edge_third, node_first, node_second, node_third)
        ]
        table, recv = project(state, weights[0])
        own = (table, recv, *lone(state, recv, weights[1], weights[3]))
        around = surround(down, up)
        if layer == 0:
            idx, steps, times = indices(pos, near_nodes(nbr, mask, cnt), around)
            idx = idx.reshape(-1)
        state, down, up = one_layer(
            idx, pos, steps, cnt, gidx, own, times, state, around, weights
        )
    return state.reshape(1, 1, 1, ROWS, W)


def solution(mesh):
    spread = P("gx", "gy", "gz", None, None)
    return jax.shard_map(
        body,
        mesh=mesh,
        in_specs=(spread,) * 5 + (P(),) * 6,
        out_specs=spread,
        check_vma=False,
    )
```

```python
import functools

import jax
import jax.numpy as jnp
import numpy as np
from jax import lax
from jax.experimental import pallas as pl
from jax.experimental.pallas import tpu as pltpu
from jax.sharding import PartitionSpec as P

F32 = jnp.float32
BF16 = jnp.bfloat16
I32 = jnp.int32
W = 128
CODES = 27
ROWS = CODES * W
DEG = 24
SLAB = 32
OUTER = [
    p for p in range(64) if p // 16 in (0, 3) or p // 4 % 4 in (0, 3) or p % 4 in (0, 3)
]
AROUND = 6
GHOSTS = len(OUTER) * SLAB
NODES = ROWS + GHOSTS
DUMMY = NODES
MARK = 2.0**100
HALO_AXES = ("gx", "gy", "gz")
GRID = (4, 4, 8)
VMEM_LIMIT = 24 * 2**20


def dot(a, b):
    return jnp.dot(a, b, preferred_element_type=F32)


def vmem():
    return pl.BlockSpec(memory_space=pltpu.VMEM)


def smem():
    return pl.BlockSpec(memory_space=pltpu.SMEM)


def iota(shape, dim):
    return lax.broadcasted_iota(I32, shape, dim)


def pack_kernel(dest_ref, rows_hbm, down_ref, mid_ref, up_ref, slot_ref, rows_ref, sem):
    fetch = pltpu.make_async_copy(rows_hbm, rows_ref, sem)
    fetch.start()
    n_y, n_z = 4, 8
    ix, iy, iz = (lax.axis_index(a) for a in HALO_AXES)
    tri = (iota((W, W), 0) < iota((W, W), 1)).astype(BF16)
    ones = jnp.ones((W, W), BF16)
    off = jnp.zeros((32, W), F32)
    for j in range(8):
        d = dest_ref[:, j * W : (j + 1) * W]
        code = (
            (lax.shift_right_logical(d, 5) - ix + 1) * 9
            + ((lax.shift_right_logical(d, 3) & (n_y - 1)) - iy + 1) * 3
            + ((d & (n_z - 1)) - iz + 1)
        )
        hit = iota((32, W), 0) == code
        one = jnp.where(hit, 1.0, 0.0).astype(BF16)
        before = dot(one, tri) + off
        rank = jnp.sum(jnp.where(hit, before, 0.0), axis=0, keepdims=True)
        slot_ref[:, j * W : (j + 1) * W] = code * W + rank.astype(I32)
        off = off + dot(one, ones)
    slot = slot_ref[...]
    fetch.wait()
    rows = rows_ref[...]
    for part, out_ref in enumerate((down_ref, mid_ref, up_ref)):
        first = part * 9 * W
        chosen = jnp.where(slot == iota((9 * W, 1024), 0) + first, 1.0, 0.0).astype(BF16)
        got = dot(chosen, rows)
        for c in range(9):
            alive = iota((W, W), 0).astype(F32) < off[part * 9 + c : part * 9 + c + 1, :]
            block = jnp.where(alive, got[c * W : (c + 1) * W, :], MARK)
            out_ref[c // 3, c % 3] = block.astype(BF16)


def pack(dest, rows):
    return pl.pallas_call(
        pack_kernel,
        out_shape=[jax.ShapeDtypeStruct((3, 3, W, W), BF16)] * 3,
        in_specs=[vmem(), pl.BlockSpec(memory_space=pltpu.HBM)],
        out_specs=[vmem()] * 3,
        scratch_shapes=[
            pltpu.VMEM((1, 1024), I32),
            pltpu.VMEM((1024, W), BF16),
            pltpu.SemaphoreType.DMA,
        ],
        compiler_params=pltpu.CompilerParams(vmem_limit_bytes=VMEM_LIMIT),
        name="pack",
    )(dest, rows)


def receive_kernel(
    gidx_ref, mid_ref, low_ref, high_ref, state_ref, cnt_ref, down_ref, up_ref, full, picked
):
    pos = [lax.axis_index(a) for a in HALO_AXES]
    cnt_ref[...] = jnp.zeros_like(cnt_ref)
    for c in range(CODES):
        offs = (c // 9 - 1, c // 3 % 3 - 1, c % 3 - 1)
        inside = jnp.int32(1)
        for p, o, s in zip(pos, offs, GRID):
            if o < 0:
                inside = inside * (p > 0).astype(I32)
            if o > 0:
                inside = inside * (p < s - 1).astype(I32)
        if c % 3 == 1:
            x = mid_ref[c // 9, c // 3 % 3].astype(F32)
        else:
            x = (low_ref if c % 3 == 0 else high_ref)[c // 9, c // 3 % 3].astype(F32)
        alive = x < MARK * 0.5
        count = jnp.sum(jnp.where(alive, 1.0, 0.0), axis=0, keepdims=True).astype(I32)
        cnt_ref[c : c + 1, :] = count * inside
        present = iota((W, W), 0) < count * inside
        full[c * W : (c + 1) * W, :] = jnp.where(present, x, MARK)
        state_ref[c * W : (c + 1) * W, :] = jnp.where(present, x, 0.0).astype(BF16)
    pick_slabs(gidx_ref, full, picked, down_ref, up_ref)


def pick_slabs(gidx_ref, full, picked, down_ref, up_ref):
    def some(b, carry):
        for r in range(16):
            picked[pl.ds(b * 16 + r, 1), :] = full[pl.ds(gidx_ref[b * 16 + r], 1), :]
        return carry

    lax.fori_loop(0, 16, some, 0)
    for s in range(8):
        out_ref = up_ref if s // 4 else down_ref
        out_ref[s // 2 % 2, s % 2] = picked[s * SLAB : (s + 1) * SLAB, :].astype(BF16)


def receive(gidx, mid, low, high):
    return pl.pallas_call(
        receive_kernel,
        out_shape=[
            jax.ShapeDtypeStruct((ROWS, W), BF16),
            jax.ShapeDtypeStruct((32, W), I32),
            jax.ShapeDtypeStruct((2, 2, SLAB, W), BF16),
            jax.ShapeDtypeStruct((2, 2, SLAB, W), BF16),
        ],
        in_specs=[smem()] + [vmem()] * 3,
        out_specs=[vmem()] * 4,
        scratch_shapes=[pltpu.VMEM((ROWS, W), F32), pltpu.VMEM((8 * SLAB, W), F32)],
        compiler_params=pltpu.CompilerParams(vmem_limit_bytes=VMEM_LIMIT),
        name="receive",
    )(gidx, mid, low, high)


def sort_pairs(count):
    pairs = []
    size = 1
    while size < count:
        size *= 2
    p = 1
    while p < size:
        k = p
        while k >= 1:
            for j in range(k % p, size - k, 2 * k):
                for i in range(min(k, size - j - k)):
                    if (i + j) // (2 * p) == (i + j + k) // (2 * p) and i + j + k < count:
                        pairs.append((i + j, i + j + k))
            k //= 2
        p *= 2
    return pairs


def fill_ghosts(pos_ref, around, ghosts):
    first = [pos_ref[i] == 0 for i in range(3)]
    final = [pos_ref[i] == n - 1 for i, n in enumerate(GRID)]
    for s, p in enumerate(OUTER):
        a, b, c = p // 16, p // 4 % 4, p % 4
        absent = None
        for i, at in enumerate((a, b, c)):
            if at in (0, 3):
                edge = first[i] if at == 0 else final[i]
                absent = edge if absent is None else absent | edge
        x_low, x_high, y_low, y_high, z_low, z_high = around
        if c in (0, 3):
            slab = (z_high if c else z_low)[a, b]
        elif b in (0, 3):
            slab = (y_high if b else y_low)[a, c - 1]
        else:
            slab = (x_high if a else x_low)[b - 1, c - 1]
        slab = jnp.where(absent, MARK, slab.astype(F32)).astype(BF16)
        ghosts[s * SLAB : (s + 1) * SLAB, :] = slab


EMPTY = -2
NONE = -1


def near_kernel(nbr_ref, valid_ref, cnt_ref, held_ref):
    counts = cnt_ref[...]
    diag = iota((32, W), 0) == iota((32, W), 1)
    by_code = jnp.sum(jnp.where(diag, counts.astype(F32), 0.0), axis=0, keepdims=True)
    by_code = jnp.broadcast_to(by_code.astype(I32), (DEG, W))
    held_ref[CODES * DEG :, :] = jnp.full(((32 - CODES) * DEG, W), NONE, I32)
    for c in range(CODES):
        cols = slice(c * W, (c + 1) * W)
        node = nbr_ref[:, cols]
        near = jnp.minimum(jnp.maximum(node, 0), ROWS - 1)
        limit = jnp.take_along_axis(by_code, lax.shift_right_logical(near, 7), axis=1)
        node = jnp.where((node < ROWS) & ((near & (W - 1)) >= limit), EMPTY, node)
        here = iota((DEG, W), 1) < counts[c : c + 1, :]
        held_ref[c * DEG : (c + 1) * DEG, :] = jnp.where(
            here & (valid_ref[:, cols] > 0), node, NONE
        )


def near_nodes(nbr, valid, cnt):
    return pl.pallas_call(
        near_kernel,
        out_shape=jax.ShapeDtypeStruct((32 * DEG, W), I32),
        in_specs=[vmem()] * 3,
        out_specs=vmem(),
        compiler_params=pltpu.CompilerParams(vmem_limit_bytes=VMEM_LIMIT),
        name="near_nodes",
    )(nbr, valid, cnt)


def index_kernel(pos_ref, held, *refs):
    around, (idx_ref, steps_ref, times_ref, ghosts) = refs[:AROUND], refs[AROUND:]
    fill_ghosts(pos_ref, around, ghosts)
    alive = jnp.where(ghosts[...].astype(F32) < MARK * 0.5, 1.0, 0.0).astype(BF16)
    at = iota((W, GHOSTS), 1)
    bit = jnp.left_shift(1, at & 15).astype(F32)
    spread = jnp.where(lax.shift_right_logical(at, 4) == iota((W, GHOSTS), 0), bit, 0.0)
    words = dot(spread.astype(BF16), alive)
    eye = iota((W, W), 0) == iota((W, W), 1)
    words = jnp.sum(jnp.where(eye, words, 0.0), axis=0, keepdims=True).astype(I32)
    words = jnp.broadcast_to(words, (8, W))
    for b in range(4):
        keys = []
        dead = jnp.zeros((8, W), F32)
        for k in range(DEG):
            node = held[pl.ds(b * 8 * DEG + k, 8, stride=DEG), :]
            far = jnp.maximum(node - ROWS, 0)
            word = jnp.take_along_axis(words, lax.shift_right_logical(far, 4), axis=1)
            flag = lax.shift_right_logical(word, far & 15) & 1
            lives = (node >= 0) & ((node < ROWS) | (flag > 0))
            key = jnp.where(lives, node, DUMMY)
            dead = dead + jnp.where((node == EMPTY) | ((node >= ROWS) & (flag == 0)), 1.0, 0.0)
            keys.append(key.astype(F32))
        for i, j in sort_pairs(DEG):
            keys[i], keys[j] = jnp.minimum(keys[i], keys[j]), jnp.maximum(keys[i], keys[j])
        used = jnp.zeros((8, W), F32)
        for k in range(DEG):
            used = used + jnp.where(keys[k] < DUMMY, 1.0, 0.0)
            idx_ref[pl.ds(b * 8 * DEG + k, 8, stride=DEG), :] = keys[k].astype(I32)
        for shift in (1, 2, 4):
            used = jnp.maximum(used, pltpu.roll(used, W - shift, 1))
        steps_ref[b * 8 : (b + 1) * 8, :] = used.astype(I32)
        for c in range(b * 8, min(b * 8 + 8, CODES)):
            row = jnp.broadcast_to(dead[c - b * 8 : c - b * 8 + 1, :], (W, W))
            lone = jnp.where(eye, row, 0.0).astype(BF16)
            times_ref[c * W : (c + 1) * W, :] = dot(lone, jnp.ones((W, W), BF16)).astype(BF16)


def indices(pos, held, around):
    return pl.pallas_call(
        index_kernel,
        out_shape=[
            jax.ShapeDtypeStruct((DEG * 32, W), I32),
            jax.ShapeDtypeStruct((32, W), I32),
            jax.ShapeDtypeStruct((ROWS, W), BF16),
        ],
        in_specs=[smem()] + [vmem()] * (1 + AROUND),
        out_specs=[vmem()] * 3,
        scratch_shapes=[pltpu.VMEM((GHOSTS, W), BF16)],
        compiler_params=pltpu.CompilerParams(vmem_limit_bytes=VMEM_LIMIT),
        name="indices",
    )(pos, held, *around)


GROUP = 16
SPAN = 27
FIRST = 12
TAILS = (0, 1, 2, 3, 4, 6, 8, 12)
DUMP = ROWS
PARTS = ((0, 3), (3, 11), (11, CODES))


def project_kernel(state_ref, efirst_ref, table_ref, recv_ref):
    w_both = jnp.concatenate([efirst_ref[0:W, :], efirst_ref[W : 2 * W, :]], axis=1)

    def own(i, carry):
        rows = pl.ds(pl.multiple_of(i * 1152, 1152), 1152)
        both = dot(state_ref[rows, :], w_both)
        recv_ref[rows, :] = both[:, :W]
        table_ref[rows, :] = both[:, W:]
        return carry

    lax.fori_loop(0, ROWS // 1152, own, 0)
    table_ref[NODES : NODES + 8, :] = jnp.full((8, W), -MARK, F32)


def project(state, efirst):
    return pl.pallas_call(
        project_kernel,
        out_shape=[
            jax.ShapeDtypeStruct((NODES + 8, W), F32),
            jax.ShapeDtypeStruct((ROWS, W), F32),
        ],
        in_specs=[vmem()] * 2,
        out_specs=[vmem()] * 2,
        compiler_params=pltpu.CompilerParams(vmem_limit_bytes=VMEM_LIMIT),
        name="project",
    )(state, efirst)


def lone_kernel(state_ref, recv_ref, esecond_ref, nfirst_ref, alone_ref, first_ref):
    w_second = esecond_ref[...]
    n_state = nfirst_ref[0:W, :]

    def some(i, carry):
        rows = pl.ds(pl.multiple_of(i * 1152, 1152), 1152)
        alone = jnp.maximum(recv_ref[rows, :], 0.0).astype(BF16)
        alone_ref[rows, :] = jnp.maximum(dot(alone, w_second), 0.0).astype(BF16)
        first_ref[rows, :] = dot(state_ref[rows, :], n_state)
        return carry

    lax.fori_loop(0, ROWS // 1152, some, 0)


def lone(state, recv, esecond, nfirst):
    return pl.pallas_call(
        lone_kernel,
        out_shape=[
            jax.ShapeDtypeStruct((ROWS, W), BF16),
            jax.ShapeDtypeStruct((ROWS, W), F32),
        ],
        in_specs=[vmem()] * 4,
        out_specs=[vmem()] * 2,
        compiler_params=pltpu.CompilerParams(vmem_limit_bytes=VMEM_LIMIT),
        name="lone",
    )(state, recv, esecond, nfirst)


def layer_kernel(
    final,
    idx_hbm,
    pos_ref,
    steps_ref,
    cnt_ref,
    gidx_ref,
    table_in,
    recv,
    alone_ref,
    first_ref,
    times_ref,
    state_ref,
    *refs,
):
    around, refs = refs[:AROUND], refs[AROUND:]
    efirst_ref, esecond_ref, ethird_ref, nfirst_ref, nsecond_ref, nthird_ref = refs[:6]
    table, out_ref = refs[6:8]
    slabs, refs = ((), refs[8:]) if final else (refs[8:10], refs[10:])
    ghosts, hidden, agg, full, picked, idx_ref, homes, sems = refs
    del table_in
    copies = []
    for i, (lo, hi) in enumerate(PARTS):
        words = pl.ds(lo * DEG * W, (hi - lo) * DEG * W)
        copies.append(pltpu.make_async_copy(idx_hbm.at[words], idx_ref.at[words], sems.at[i]))
        copies[-1].start()
    w_send = efirst_ref[W : 2 * W, :]
    fill_ghosts(pos_ref, around, ghosts)

    def far(i, carry):
        x = ghosts[pl.ds(pl.multiple_of(i * 896, 128), 896), :].astype(F32)
        x = jnp.where(x < MARK * 0.5, x, 0.0).astype(BF16)
        table[pl.ds(pl.multiple_of(ROWS + i * 896, 128), 896), :] = dot(x, w_send)
        return carry

    lax.fori_loop(0, GHOSTS // 896, far, 0)

    w_second = esecond_ref[...]
    sub = iota((8, W), 0)

    def listed(c, n):
        for g in range(W // 8):
            homes[n + g] = c * W + g * 8
        return n + lax.shift_right_logical(cnt_ref[c, 0] + 7, 3)

    starts = [jnp.int32(0)]
    for lo, hi in PARTS:
        starts.append(lax.fori_loop(lo, hi, listed, starts[-1]))
    total = starts[-1]
    for extra in range(3):
        homes[total + extra] = homes[jnp.maximum(total - 1, 0)]
    rounds = lax.shift_right_logical(total + 3, 2)
    turns = [jnp.minimum(lax.shift_right_logical(n, 2), rounds) for n in starts[:-1]]

    def finish(h, rows):
        d = jnp.maximum(dot(h, w_second), 0.0).astype(BF16).astype(F32)
        d = jnp.sum(d.reshape(2, DEG, GROUP, W), axis=1)
        for u, row in enumerate(rows):
            piece = d[u // 2, (u % 2) * 8 : (u % 2) * 8 + 8, :]
            agg[pl.ds(pl.multiple_of(row, 8), 8), :] = piece

    def step(slot, bases, mines, k):
        both = []
        for half in range(2):
            base, mine = bases[2 * slot + half], mines[2 * slot + half]
            got = None
            for r in range(8):
                at = idx_ref[base + (k * W + r)]
                row = jnp.broadcast_to(table[pl.ds(at, 1), :], (8, W))
                got = row if got is None else jnp.where(sub == r, row, got)
            both.append(jnp.maximum(got + mine, 0.0))
        at = (slot * DEG + k) * GROUP
        hidden[at : at + GROUP, :] = jnp.concatenate(both, axis=0).astype(BF16)

    def gather(i, last):
        for turn, copy in zip(turns, copies):
            pl.when(i == turn)(copy.wait)
        rows = [pl.multiple_of(homes[4 * i + u], 8) for u in range(4)]
        codes = [lax.shift_right_logical(row, 7) for row in rows]
        bases = [row + code * ((DEG - 1) * W) for row, code in zip(rows, codes)]
        mines = [recv[pl.ds(row, 8), :] for row in rows]
        needs = [steps_ref[code, row & (W - 1)] for row, code in zip(rows, codes)]
        finish(hidden[...], last)
        for slot in range(2):
            for k in range(FIRST):
                step(slot, bases, mines, k)
        for slot in range(2):
            more = jnp.maximum(needs[2 * slot], needs[2 * slot + 1]) - FIRST
            which = sum((more > t).astype(I32) for t in TAILS[:-1])

            def tail(size, slot=slot):
                def run():
                    for k in range(FIRST, FIRST + size):
                        step(slot, bases, mines, k)
                    if FIRST + size < DEG:
                        rest = (DEG - FIRST - size) * GROUP
                        end = (slot + 1) * DEG * GROUP
                        hidden[end - rest : end, :] = jnp.zeros((rest, W), BF16)

                return run

            lax.switch(which, [tail(t) for t in TAILS])
        return tuple(rows)

    last = lax.fori_loop(0, rounds, gather, (jnp.int32(DUMP),) * 4)
    for turn, copy in zip(turns, copies):
        pl.when(turn == rounds)(copy.wait)
    finish(hidden[...], last)

    w_twice = jnp.concatenate([ethird_ref[...], ethird_ref[...]], axis=0)
    n_agg = nfirst_ref[W : 2 * W, :]
    n_second = nsecond_ref[...]
    n_third = nthird_ref[...]

    def node(i, carry):
        rows = pl.ds(pl.multiple_of(i * (SPAN * W), SPAN * W), SPAN * W)
        live = jnp.concatenate(
            [iota((W, W), 0) < cnt_ref[i * SPAN + j, 0] for j in range(SPAN)], axis=0
        )
        lone_part = times_ref[rows, :].astype(F32) * alone_ref[rows, :].astype(F32)
        summed = jnp.where(live, agg[rows, :] + lone_part, 0.0)
        top = summed.astype(BF16)
        rest = (summed - top.astype(F32)).astype(BF16)
        both = jnp.concatenate([top, rest], axis=1)
        total = dot(both, w_twice).astype(BF16)
        state = state_ref[rows, :]
        h = jnp.maximum(first_ref[rows, :] + dot(total, n_agg), 0.0).astype(BF16)
        h = jnp.maximum(dot(h, n_second), 0.0).astype(BF16)
        update = dot(h, n_third)
        mean = jnp.mean(update, axis=1, keepdims=True)
        centred = update - mean
        var = jnp.mean(centred * centred, axis=1, keepdims=True)
        new = state.astype(F32) + centred * lax.rsqrt(var + 1e-05)
        if not final:
            full[rows, :] = jnp.where(live, new, MARK)
        out_ref[rows, :] = jnp.where(live, new, 0.0).astype(BF16)
        return carry

    lax.fori_loop(0, ROWS // (SPAN * W), node, 0)
    if not final:
        pick_slabs(gidx_ref, full, picked, *slabs)


def one_layer(final, idx, pos, steps, cnt, gidx, own, times, state, around, weights):
    return pl.pallas_call(
        functools.partial(layer_kernel, final),
        out_shape=[
            jax.ShapeDtypeStruct((NODES + 8, W), F32),
            jax.ShapeDtypeStruct((ROWS, W), BF16),
        ]
        + [jax.ShapeDtypeStruct((2, 2, SLAB, W), BF16)] * (0 if final else 2),
        in_specs=[pl.BlockSpec(memory_space=pl.ANY)] + [smem()] * 4 + [vmem()] * (12 + AROUND),
        out_specs=[vmem()] * (2 if final else 4),
        input_output_aliases={5: 0},
        scratch_shapes=[
            pltpu.VMEM((GHOSTS, W), BF16),
            pltpu.VMEM((2 * DEG * GROUP, W), BF16),
            pltpu.VMEM((ROWS + GROUP, W), F32),
            pltpu.VMEM((ROWS, W), F32),
            pltpu.VMEM((8 * SLAB, W), F32),
            pltpu.SMEM((ROWS * DEG,), I32),
            pltpu.SMEM((512,), I32),
            pltpu.SemaphoreType.DMA((len(PARTS),)),
        ],
        compiler_params=pltpu.CompilerParams(vmem_limit_bytes=VMEM_LIMIT),
        name="layer",
    )(idx, pos, steps, cnt, gidx, *own, times, state, *around, *weights)[1:]


def both_ways(up, down, axis):
    n = lax.axis_size(axis)
    forward = [(i, (i + 1) % n) for i in range(n)]
    backward = [(b, a) for a, b in forward]
    return lax.ppermute(up, axis, forward), lax.ppermute(down, axis, backward)


def migrate(down, mid, up):
    low, high = both_ways(up, down, "gx")
    buffer = jnp.stack([low, mid, high])
    low, high = both_ways(buffer[:, 2], buffer[:, 0], "gy")
    buffer = jnp.stack([low, buffer[:, 1], high], axis=1)
    low, high = both_ways(buffer[:, :, 2], buffer[:, :, 0], "gz")
    return buffer[:, :, 1], low, high


def surround(down, up):
    x_low, x_high = both_ways(up, down, "gx")
    rows = (x_low, down, up, x_high)
    y_low, y_high = both_ways(
        jnp.stack([r[1] for r in rows]), jnp.stack([r[0] for r in rows]), "gy"
    )

    def face(c):
        return jnp.stack(
            [jnp.stack([y_low[a, c], r[0, c], r[1, c], y_high[a, c]]) for a, r in enumerate(rows)]
        )

    z_low, z_high = both_ways(face(1), face(0), "gz")
    return x_low, x_high, y_low, y_high, z_low, z_high


def body(
    latent,
    destination,
    neighbours,
    valid,
    ghost_index,
    edge_first,
    edge_second,
    edge_third,
    node_first,
    node_second,
    node_third,
):
    dest = destination.reshape(1, 1024)
    nbr = neighbours[0, 0, 0].T
    mask = valid[0, 0, 0].T
    gidx = ghost_index.reshape(-1)
    pos = jnp.stack([lax.axis_index(a) for a in HALO_AXES]).astype(I32)
    state, cnt, *sent = receive(gidx, *migrate(*pack(dest, latent[0, 0, 0])))
    for layer in range(edge_first.shape[0]):
        weights = [
            w[layer]
            for w in (edge_first, edge_second, edge_third, node_first, node_second, node_third)
        ]
        table, recv = project(state, weights[0])
        own = (table, recv, *lone(state, recv, weights[1], weights[3]))
        around = surround(*sent)
        if layer == 0:
            idx, steps, times = indices(pos, near_nodes(nbr, mask, cnt), around)
            idx = idx.reshape(-1)
        final = layer == edge_first.shape[0] - 1
        state, *sent = one_layer(
            final, idx, pos, steps, cnt, gidx, own, times, state, around, weights
        )
    return state.reshape(1, 1, 1, ROWS, W)


def solution(mesh):
    spread = P("gx", "gy", "gz", None, None)
    return jax.shard_map(
        body,
        mesh=mesh,
        in_specs=(spread,) * 5 + (P(),) * 6,
        out_specs=spread,
        check_vma=False,
    )
```

```python
import functools

import jax
import jax.numpy as jnp
import numpy as np
from jax import lax
from jax.experimental import pallas as pl
from jax.experimental.pallas import tpu as pltpu
from jax.sharding import PartitionSpec as P

F32 = jnp.float32
BF16 = jnp.bfloat16
I32 = jnp.int32
W = 128
CODES = 27
ROWS = CODES * W
DEG = 24
SLAB = 32
OUTER = [
    p for p in range(64) if p // 16 in (0, 3) or p // 4 % 4 in (0, 3) or p % 4 in (0, 3)
]
AROUND = 6
GHOSTS = len(OUTER) * SLAB
NODES = ROWS + GHOSTS
DUMMY = NODES
MARK = 2.0**100
HALO_AXES = ("gx", "gy", "gz")
GRID = (4, 4, 8)
VMEM_LIMIT = 24 * 2**20


def dot(a, b):
    return jnp.dot(a, b, preferred_element_type=F32)


def vmem():
    return pl.BlockSpec(memory_space=pltpu.VMEM)


def smem():
    return pl.BlockSpec(memory_space=pltpu.SMEM)


def iota(shape, dim):
    return lax.broadcasted_iota(I32, shape, dim)


def pack_kernel(dest_ref, rows_hbm, down_ref, mid_ref, up_ref, slot_ref, rows_ref, sem):
    fetch = pltpu.make_async_copy(rows_hbm, rows_ref, sem)
    fetch.start()
    n_y, n_z = 4, 8
    ix, iy, iz = (lax.axis_index(a) for a in HALO_AXES)
    tri = (iota((W, W), 0) < iota((W, W), 1)).astype(BF16)
    ones = jnp.ones((W, W), BF16)
    off = jnp.zeros((32, W), F32)
    for j in range(8):
        d = dest_ref[:, j * W : (j + 1) * W]
        code = (
            (lax.shift_right_logical(d, 5) - ix + 1) * 9
            + ((lax.shift_right_logical(d, 3) & (n_y - 1)) - iy + 1) * 3
            + ((d & (n_z - 1)) - iz + 1)
        )
        hit = iota((32, W), 0) == code
        one = jnp.where(hit, 1.0, 0.0).astype(BF16)
        before = dot(one, tri) + off
        rank = jnp.sum(jnp.where(hit, before, 0.0), axis=0, keepdims=True)
        slot_ref[:, j * W : (j + 1) * W] = code * W + rank.astype(I32)
        off = off + dot(one, ones)
    slot = slot_ref[...]
    fetch.wait()
    rows = rows_ref[...]
    for part, out_ref in enumerate((down_ref, mid_ref, up_ref)):
        first = part * 9 * W
        chosen = jnp.where(slot == iota((9 * W, 1024), 0) + first, 1.0, 0.0).astype(BF16)
        got = dot(chosen, rows)
        for c in range(9):
            alive = iota((W, W), 0).astype(F32) < off[part * 9 + c : part * 9 + c + 1, :]
            block = jnp.where(alive, got[c * W : (c + 1) * W, :], MARK)
            out_ref[c // 3, c % 3] = block.astype(BF16)


def pack(dest, rows):
    return pl.pallas_call(
        pack_kernel,
        out_shape=[jax.ShapeDtypeStruct((3, 3, W, W), BF16)] * 3,
        in_specs=[vmem(), pl.BlockSpec(memory_space=pltpu.HBM)],
        out_specs=[vmem()] * 3,
        scratch_shapes=[
            pltpu.VMEM((1, 1024), I32),
            pltpu.VMEM((1024, W), BF16),
            pltpu.SemaphoreType.DMA,
        ],
        compiler_params=pltpu.CompilerParams(vmem_limit_bytes=VMEM_LIMIT),
        name="pack",
    )(dest, rows)


def receive_kernel(
    gidx_ref, mid_ref, low_ref, high_ref, state_ref, cnt_ref, down_ref, up_ref, full, picked
):
    pos = [lax.axis_index(a) for a in HALO_AXES]
    cnt_ref[...] = jnp.zeros_like(cnt_ref)
    for c in range(CODES):
        offs = (c // 9 - 1, c // 3 % 3 - 1, c % 3 - 1)
        inside = jnp.int32(1)
        for p, o, s in zip(pos, offs, GRID):
            if o < 0:
                inside = inside * (p > 0).astype(I32)
            if o > 0:
                inside = inside * (p < s - 1).astype(I32)
        if c % 3 == 1:
            x = mid_ref[c // 9, c // 3 % 3].astype(F32)
        else:
            x = (low_ref if c % 3 == 0 else high_ref)[c // 9, c // 3 % 3].astype(F32)
        alive = x < MARK * 0.5
        count = jnp.sum(jnp.where(alive, 1.0, 0.0), axis=0, keepdims=True).astype(I32)
        cnt_ref[c : c + 1, :] = count * inside
        present = iota((W, W), 0) < count * inside
        full[c * W : (c + 1) * W, :] = jnp.where(present, x, MARK)
        state_ref[c * W : (c + 1) * W, :] = jnp.where(present, x, 0.0).astype(BF16)
    pick_slabs(gidx_ref, full, picked, down_ref, up_ref)


def pick_slabs(gidx_ref, full, picked, down_ref, up_ref):
    def some(b, carry):
        for r in range(16):
            picked[pl.ds(b * 16 + r, 1), :] = full[pl.ds(gidx_ref[b * 16 + r], 1), :]
        return carry

    lax.fori_loop(0, 16, some, 0)
    for s in range(8):
        out_ref = up_ref if s // 4 else down_ref
        out_ref[s // 2 % 2, s % 2] = picked[s * SLAB : (s + 1) * SLAB, :].astype(BF16)


def receive(gidx, mid, low, high):
    return pl.pallas_call(
        receive_kernel,
        out_shape=[
            jax.ShapeDtypeStruct((ROWS, W), BF16),
            jax.ShapeDtypeStruct((32, W), I32),
            jax.ShapeDtypeStruct((2, 2, SLAB, W), BF16),
            jax.ShapeDtypeStruct((2, 2, SLAB, W), BF16),
        ],
        in_specs=[smem()] + [vmem()] * 3,
        out_specs=[vmem()] * 4,
        scratch_shapes=[pltpu.VMEM((ROWS, W), F32), pltpu.VMEM((8 * SLAB, W), F32)],
        compiler_params=pltpu.CompilerParams(vmem_limit_bytes=VMEM_LIMIT),
        name="receive",
    )(gidx, mid, low, high)


def sort_pairs(count):
    pairs = []
    size = 1
    while size < count:
        size *= 2
    p = 1
    while p < size:
        k = p
        while k >= 1:
            for j in range(k % p, size - k, 2 * k):
                for i in range(min(k, size - j - k)):
                    if (i + j) // (2 * p) == (i + j + k) // (2 * p) and i + j + k < count:
                        pairs.append((i + j, i + j + k))
            k //= 2
        p *= 2
    return pairs


def fill_ghosts(pos_ref, around, ghosts):
    first = [pos_ref[i] == 0 for i in range(3)]
    final = [pos_ref[i] == n - 1 for i, n in enumerate(GRID)]
    for s, p in enumerate(OUTER):
        a, b, c = p // 16, p // 4 % 4, p % 4
        absent = None
        for i, at in enumerate((a, b, c)):
            if at in (0, 3):
                edge = first[i] if at == 0 else final[i]
                absent = edge if absent is None else absent | edge
        x_low, x_high, y_low, y_high, z_low, z_high = around
        if c in (0, 3):
            slab = (z_high if c else z_low)[a, b]
        elif b in (0, 3):
            slab = (y_high if b else y_low)[a, c - 1]
        else:
            slab = (x_high if a else x_low)[b - 1, c - 1]
        slab = jnp.where(absent, MARK, slab.astype(F32)).astype(BF16)
        ghosts[s * SLAB : (s + 1) * SLAB, :] = slab


EMPTY = -2
NONE = -1


def near_kernel(nbr_ref, valid_ref, cnt_ref, held_ref):
    counts = cnt_ref[...]
    diag = iota((32, W), 0) == iota((32, W), 1)
    by_code = jnp.sum(jnp.where(diag, counts.astype(F32), 0.0), axis=0, keepdims=True)
    by_code = jnp.broadcast_to(by_code.astype(I32), (DEG, W))
    held_ref[CODES * DEG :, :] = jnp.full(((32 - CODES) * DEG, W), NONE, I32)
    for c in range(CODES):
        cols = slice(c * W, (c + 1) * W)
        node = nbr_ref[:, cols]
        near = jnp.minimum(jnp.maximum(node, 0), ROWS - 1)
        limit = jnp.take_along_axis(by_code, lax.shift_right_logical(near, 7), axis=1)
        node = jnp.where((node < ROWS) & ((near & (W - 1)) >= limit), EMPTY, node)
        here = iota((DEG, W), 1) < counts[c : c + 1, :]
        held_ref[c * DEG : (c + 1) * DEG, :] = jnp.where(
            here & (valid_ref[:, cols] > 0), node, NONE
        )


def near_nodes(nbr, valid, cnt):
    return pl.pallas_call(
        near_kernel,
        out_shape=jax.ShapeDtypeStruct((32 * DEG, W), I32),
        in_specs=[vmem()] * 3,
        out_specs=vmem(),
        compiler_params=pltpu.CompilerParams(vmem_limit_bytes=VMEM_LIMIT),
        name="near_nodes",
    )(nbr, valid, cnt)


def index_kernel(pos_ref, held, *refs):
    around, (idx_ref, steps_ref, times_ref, ghosts) = refs[:AROUND], refs[AROUND:]
    fill_ghosts(pos_ref, around, ghosts)
    alive = jnp.where(ghosts[...].astype(F32) < MARK * 0.5, 1.0, 0.0).astype(BF16)
    at = iota((W, GHOSTS), 1)
    bit = jnp.left_shift(1, at & 15).astype(F32)
    spread = jnp.where(lax.shift_right_logical(at, 4) == iota((W, GHOSTS), 0), bit, 0.0)
    words = dot(spread.astype(BF16), alive)
    eye = iota((W, W), 0) == iota((W, W), 1)
    words = jnp.sum(jnp.where(eye, words, 0.0), axis=0, keepdims=True).astype(I32)
    words = jnp.broadcast_to(words, (8, W))
    for b in range(4):
        keys = []
        dead = jnp.zeros((8, W), F32)
        for k in range(DEG):
            node = held[pl.ds(b * 8 * DEG + k, 8, stride=DEG), :]
            far = jnp.maximum(node - ROWS, 0)
            word = jnp.take_along_axis(words, lax.shift_right_logical(far, 4), axis=1)
            flag = lax.shift_right_logical(word, far & 15) & 1
            lives = (node >= 0) & ((node < ROWS) | (flag > 0))
            key = jnp.where(lives, node, DUMMY)
            dead = dead + jnp.where((node == EMPTY) | ((node >= ROWS) & (flag == 0)), 1.0, 0.0)
            keys.append(key.astype(F32))
        for i, j in sort_pairs(DEG):
            keys[i], keys[j] = jnp.minimum(keys[i], keys[j]), jnp.maximum(keys[i], keys[j])
        used = jnp.zeros((8, W), F32)
        for k in range(DEG):
            used = used + jnp.where(keys[k] < DUMMY, 1.0, 0.0)
            idx_ref[pl.ds(b * 8 * DEG + k, 8, stride=DEG), :] = keys[k].astype(I32)
        for shift in (1, 2, 4):
            used = jnp.maximum(used, pltpu.roll(used, W - shift, 1))
        steps_ref[b * 8 : (b + 1) * 8, :] = used.astype(I32)
        for c in range(b * 8, min(b * 8 + 8, CODES)):
            row = jnp.broadcast_to(dead[c - b * 8 : c - b * 8 + 1, :], (W, W))
            lone = jnp.where(eye, row, 0.0).astype(BF16)
            times_ref[c * W : (c + 1) * W, :] = dot(lone, jnp.ones((W, W), BF16)).astype(BF16)


def indices(pos, held, around):
    return pl.pallas_call(
        index_kernel,
        out_shape=[
            jax.ShapeDtypeStruct((DEG * 32, W), I32),
            jax.ShapeDtypeStruct((32, W), I32),
            jax.ShapeDtypeStruct((ROWS, W), BF16),
        ],
        in_specs=[smem()] + [vmem()] * (1 + AROUND),
        out_specs=[vmem()] * 3,
        scratch_shapes=[pltpu.VMEM((GHOSTS, W), BF16)],
        compiler_params=pltpu.CompilerParams(vmem_limit_bytes=VMEM_LIMIT),
        name="indices",
    )(pos, held, *around)


GROUP = 16
SPAN = 27
FIRST = 12
TAILS = (0, 1, 2, 3, 4, 6, 8, 12)
DUMP = ROWS
PARTS = ((0, 1), (1, 8), (8, CODES))


def project_kernel(state_ref, efirst_ref, table_ref, recv_ref):
    w_both = jnp.concatenate([efirst_ref[0:W, :], efirst_ref[W : 2 * W, :]], axis=1)

    def own(i, carry):
        rows = pl.ds(pl.multiple_of(i * 1152, 1152), 1152)
        both = dot(state_ref[rows, :], w_both)
        recv_ref[rows, :] = both[:, :W]
        table_ref[rows, :] = both[:, W:]
        return carry

    lax.fori_loop(0, ROWS // 1152, own, 0)
    table_ref[NODES : NODES + 8, :] = jnp.full((8, W), -MARK, F32)


def project(state, efirst):
    return pl.pallas_call(
        project_kernel,
        out_shape=[
            jax.ShapeDtypeStruct((NODES + 8, W), F32),
            jax.ShapeDtypeStruct((ROWS, W), F32),
        ],
        in_specs=[vmem()] * 2,
        out_specs=[vmem()] * 2,
        compiler_params=pltpu.CompilerParams(vmem_limit_bytes=VMEM_LIMIT),
        name="project",
    )(state, efirst)


def lone_kernel(state_ref, recv_ref, esecond_ref, nfirst_ref, alone_ref, first_ref):
    w_second = esecond_ref[...]
    n_state = nfirst_ref[0:W, :]

    def some(i, carry):
        rows = pl.ds(pl.multiple_of(i * 1152, 1152), 1152)
        alone = jnp.maximum(recv_ref[rows, :], 0.0).astype(BF16)
        alone_ref[rows, :] = jnp.maximum(dot(alone, w_second), 0.0).astype(BF16)
        first_ref[rows, :] = dot(state_ref[rows, :], n_state)
        return carry

    lax.fori_loop(0, ROWS // 1152, some, 0)


def lone(state, recv, esecond, nfirst):
    return pl.pallas_call(
        lone_kernel,
        out_shape=[
            jax.ShapeDtypeStruct((ROWS, W), BF16),
            jax.ShapeDtypeStruct((ROWS, W), F32),
        ],
        in_specs=[vmem()] * 4,
        out_specs=[vmem()] * 2,
        compiler_params=pltpu.CompilerParams(vmem_limit_bytes=VMEM_LIMIT),
        name="lone",
    )(state, recv, esecond, nfirst)


def layer_kernel(
    final,
    idx_hbm,
    pos_ref,
    steps_ref,
    cnt_ref,
    gidx_ref,
    table_in,
    recv,
    alone_ref,
    first_ref,
    times_ref,
    state_ref,
    *refs,
):
    around, refs = refs[:AROUND], refs[AROUND:]
    efirst_ref, esecond_ref, ethird_ref, nfirst_ref, nsecond_ref, nthird_ref = refs[:6]
    table, out_ref = refs[6:8]
    slabs, refs = ((), refs[8:]) if final else (refs[8:10], refs[10:])
    ghosts, hidden, agg, full, picked, idx_ref, homes, sems = refs
    del table_in
    copies = []
    for i, (lo, hi) in enumerate(PARTS):
        words = pl.ds(lo * DEG * W, (hi - lo) * DEG * W)
        copies.append(pltpu.make_async_copy(idx_hbm.at[words], idx_ref.at[words], sems.at[i]))
        copies[-1].start()
    w_send = efirst_ref[W : 2 * W, :]
    fill_ghosts(pos_ref, around, ghosts)

    def far(i, carry):
        x = ghosts[pl.ds(pl.multiple_of(i * 896, 128), 896), :].astype(F32)
        x = jnp.where(x < MARK * 0.5, x, 0.0).astype(BF16)
        table[pl.ds(pl.multiple_of(ROWS + i * 896, 128), 896), :] = dot(x, w_send)
        return carry

    lax.fori_loop(0, GHOSTS // 896, far, 0)

    w_second = esecond_ref[...]
    sub = iota((8, W), 0)

    def listed(c, n):
        for g in range(W // 8):
            homes[n + g] = c * W + g * 8
        return n + lax.shift_right_logical(cnt_ref[c, 0] + 7, 3)

    starts = [jnp.int32(0)]
    for lo, hi in PARTS:
        starts.append(lax.fori_loop(lo, hi, listed, starts[-1]))
    total = starts[-1]
    for extra in range(3):
        homes[total + extra] = homes[jnp.maximum(total - 1, 0)]
    rounds = lax.shift_right_logical(total + 3, 2)
    turns = [jnp.minimum(lax.shift_right_logical(n, 2), rounds) for n in starts[:-1]]

    def finish(h, rows):
        d = jnp.maximum(dot(h, w_second), 0.0).astype(BF16).astype(F32)
        d = jnp.sum(d.reshape(2, DEG, GROUP, W), axis=1)
        for u, row in enumerate(rows):
            piece = d[u // 2, (u % 2) * 8 : (u % 2) * 8 + 8, :]
            agg[pl.ds(pl.multiple_of(row, 8), 8), :] = piece

    def step(slot, bases, mines, k):
        both = []
        for half in range(2):
            base, mine = bases[2 * slot + half], mines[2 * slot + half]
            got = None
            for r in range(8):
                at = idx_ref[base + (k * W + r)]
                row = jnp.broadcast_to(table[pl.ds(at, 1), :], (8, W))
                got = row if got is None else jnp.where(sub == r, row, got)
            both.append(jnp.maximum(got + mine, 0.0))
        at = (slot * DEG + k) * GROUP
        hidden[at : at + GROUP, :] = jnp.concatenate(both, axis=0).astype(BF16)

    def gather(i, last):
        for turn, copy in zip(turns, copies):
            pl.when(i == turn)(copy.wait)
        rows = [pl.multiple_of(homes[4 * i + u], 8) for u in range(4)]
        codes = [lax.shift_right_logical(row, 7) for row in rows]
        bases = [row + code * ((DEG - 1) * W) for row, code in zip(rows, codes)]
        mines = [recv[pl.ds(row, 8), :] for row in rows]
        needs = [steps_ref[code, row & (W - 1)] for row, code in zip(rows, codes)]
        finish(hidden[...], last)
        for slot in range(2):
            for k in range(FIRST):
                step(slot, bases, mines, k)
        for slot in range(2):
            more = jnp.maximum(needs[2 * slot], needs[2 * slot + 1]) - FIRST
            which = sum((more > t).astype(I32) for t in TAILS[:-1])

            def tail(size, slot=slot):
                def run():
                    for k in range(FIRST, FIRST + size):
                        step(slot, bases, mines, k)
                    if FIRST + size < DEG:
                        rest = (DEG - FIRST - size) * GROUP
                        end = (slot + 1) * DEG * GROUP
                        hidden[end - rest : end, :] = jnp.zeros((rest, W), BF16)

                return run

            lax.switch(which, [tail(t) for t in TAILS])
        return tuple(rows)

    last = lax.fori_loop(0, rounds, gather, (jnp.int32(DUMP),) * 4)
    for turn, copy in zip(turns, copies):
        pl.when(turn == rounds)(copy.wait)
    finish(hidden[...], last)

    w_twice = jnp.concatenate([ethird_ref[...], ethird_ref[...]], axis=0)
    n_agg = nfirst_ref[W : 2 * W, :]
    n_second = nsecond_ref[...]
    n_third = nthird_ref[...]

    def node(i, carry):
        rows = pl.ds(pl.multiple_of(i * (SPAN * W), SPAN * W), SPAN * W)
        live = jnp.concatenate(
            [iota((W, W), 0) < cnt_ref[i * SPAN + j, 0] for j in range(SPAN)], axis=0
        )
        lone_part = times_ref[rows, :].astype(F32) * alone_ref[rows, :].astype(F32)
        summed = jnp.where(live, agg[rows, :] + lone_part, 0.0)
        top = summed.astype(BF16)
        rest = (summed - top.astype(F32)).astype(BF16)
        both = jnp.concatenate([top, rest], axis=1)
        total = dot(both, w_twice).astype(BF16)
        state = state_ref[rows, :]
        h = jnp.maximum(first_ref[rows, :] + dot(total, n_agg), 0.0).astype(BF16)
        h = jnp.maximum(dot(h, n_second), 0.0).astype(BF16)
        update = dot(h, n_third)
        mean = jnp.mean(update, axis=1, keepdims=True)
        centred = update - mean
        var = jnp.mean(centred * centred, axis=1, keepdims=True)
        new = state.astype(F32) + centred * lax.rsqrt(var + 1e-05)
        if not final:
            full[rows, :] = jnp.where(live, new, MARK)
        out_ref[rows, :] = jnp.where(live, new, 0.0).astype(BF16)
        return carry

    lax.fori_loop(0, ROWS // (SPAN * W), node, 0)
    if not final:
        pick_slabs(gidx_ref, full, picked, *slabs)


def one_layer(final, idx, pos, steps, cnt, gidx, own, times, state, around, weights):
    return pl.pallas_call(
        functools.partial(layer_kernel, final),
        out_shape=[
            jax.ShapeDtypeStruct((NODES + 8, W), F32),
            jax.ShapeDtypeStruct((ROWS, W), BF16),
        ]
        + [jax.ShapeDtypeStruct((2, 2, SLAB, W), BF16)] * (0 if final else 2),
        in_specs=[pl.BlockSpec(memory_space=pl.ANY)] + [smem()] * 4 + [vmem()] * (12 + AROUND),
        out_specs=[vmem()] * (2 if final else 4),
        input_output_aliases={5: 0},
        scratch_shapes=[
            pltpu.VMEM((GHOSTS, W), BF16),
            pltpu.VMEM((2 * DEG * GROUP, W), BF16),
            pltpu.VMEM((ROWS + GROUP, W), F32),
            pltpu.VMEM((ROWS, W), F32),
            pltpu.VMEM((8 * SLAB, W), F32),
            pltpu.SMEM((ROWS * DEG,), I32),
            pltpu.SMEM((512,), I32),
            pltpu.SemaphoreType.DMA((len(PARTS),)),
        ],
        compiler_params=pltpu.CompilerParams(vmem_limit_bytes=VMEM_LIMIT),
        name="layer",
    )(idx, pos, steps, cnt, gidx, *own, times, state, *around, *weights)[1:]


def both_ways(up, down, axis):
    n = lax.axis_size(axis)
    forward = [(i, (i + 1) % n) for i in range(n)]
    backward = [(b, a) for a, b in forward]
    return lax.ppermute(up, axis, forward), lax.ppermute(down, axis, backward)


def migrate(down, mid, up):
    low, high = both_ways(up, down, "gx")
    buffer = jnp.stack([low, mid, high])
    low, high = both_ways(buffer[:, 2], buffer[:, 0], "gy")
    buffer = jnp.stack([low, buffer[:, 1], high], axis=1)
    low, high = both_ways(buffer[:, :, 2], buffer[:, :, 0], "gz")
    return buffer[:, :, 1], low, high


def surround(down, up):
    x_low, x_high = both_ways(up, down, "gx")
    rows = (x_low, down, up, x_high)
    y_low, y_high = both_ways(
        jnp.stack([r[1] for r in rows]), jnp.stack([r[0] for r in rows]), "gy"
    )

    def face(c):
        return jnp.stack(
            [jnp.stack([y_low[a, c], r[0, c], r[1, c], y_high[a, c]]) for a, r in enumerate(rows)]
        )

    z_low, z_high = both_ways(face(1), face(0), "gz")
    return x_low, x_high, y_low, y_high, z_low, z_high


def body(
    latent,
    destination,
    neighbours,
    valid,
    ghost_index,
    edge_first,
    edge_second,
    edge_third,
    node_first,
    node_second,
    node_third,
):
    dest = destination.reshape(1, 1024)
    nbr = neighbours[0, 0, 0].T
    mask = valid[0, 0, 0].T
    gidx = ghost_index.reshape(-1)
    pos = jnp.stack([lax.axis_index(a) for a in HALO_AXES]).astype(I32)
    state, cnt, *sent = receive(gidx, *migrate(*pack(dest, latent[0, 0, 0])))
    for layer in range(edge_first.shape[0]):
        weights = [
            w[layer]
            for w in (edge_first, edge_second, edge_third, node_first, node_second, node_third)
        ]
        table, recv = project(state, weights[0])
        own = (table, recv, *lone(state, recv, weights[1], weights[3]))
        around = surround(*sent)
        if layer == 0:
            idx, steps, times = indices(pos, near_nodes(nbr, mask, cnt), around)
            idx = idx.reshape(-1)
        final = layer == edge_first.shape[0] - 1
        state, *sent = one_layer(
            final, idx, pos, steps, cnt, gidx, own, times, state, around, weights
        )
    return state.reshape(1, 1, 1, ROWS, W)


def solution(mesh):
    spread = P("gx", "gy", "gz", None, None)
    return jax.shard_map(
        body,
        mesh=mesh,
        in_specs=(spread,) * 5 + (P(),) * 6,
        out_specs=spread,
        check_vma=False,
    )
```
